32 devices in a mesh: cuts: 8 (over y, x, core), frame: 4 (over z).
Axes of the slice: x: 2, y: 2, z: 4, core: 2. Of those that a mesh axis runs over, the one named last changes fastest.
Arguments:
- basis: bfloat16 [2, 32, 128, 4, 256], P(None, None, 'cuts', 'frame'), may hold values from -6 to 6
- coil_maps: bfloat16 [2, 12, 128, 4, 256], P(None, None, 'cuts', 'frame'), may hold values from -3 to 3
- factors: bfloat16 [2, 32, 64], P(None, None, 'frame'), may hold values from -0.75 to 0.75
- lines: int32 [64, 16], P(None, 'cuts'), may hold values from 0 to 4095
- kdata: bfloat16 [2, 64, 16, 12, 4], P(None, None, 'cuts', None, 'frame'), may hold values from -6 to 6
Outputs:
- basis_grad: float32 [2, 32, 128, 4, 256], P(None, None, 'cuts', 'frame')
- factor_grad: float32 [2, 32, 64], P(None, None, 'frame')
The draws below stay inside these ranges and needn't reach their ends.
Inputs may be any that keep to these rules, and one draw needn't show every extreme that they name: lines[t, j] = (ky - (j // 2) * 32) * 128 + kz for a position (ky, kz) sampled in frame t whose ky lies in the rows (j // 2) * 32 to (j // 2 + 1) * 32 - 1; positions may repeat over frames.
All inputs are finite; a program needn't handle non-finite values.
Results may differ from the reference program's by a relative error of at most 0.011.
Values may be sent and summed in bfloat16 or wider, within the bound.
No kernel may reach another device: no remote copies, remote signals or barrier semaphores. Data moves between devices by JAX's collectives and lax.ppermute only.
A program may use at most 64 MiB of HBM per device.

```python
import math
import jax
import jax.numpy as jnp
from jax import lax

RANK = 32
COILS = 12
NY = 256
NZ = 128
LPD = 2
NXW = 4
FRAMES = 64
LINES = 16
RY = 32


def plant(entries, own_key, smallest, top_value):
    extent = entries.shape
    place = [jax.random.randint(jax.random.fold_in(own_key, axis), (), 0, extent[axis]) for axis in range(len(extent))]
    entries = entries.at[tuple(place)].set(smallest)
    longest = extent.index(max(extent))
    place[longest] = (place[longest] + 1) % extent[longest]
    return entries.at[tuple(place)].set(top_value)


def level_of(own_key, extent, shards, low, largest):
    gain = 1.0
    for position, shards_of in shards:
        draws = jax.random.uniform(jax.random.fold_in(jax.random.fold_in(own_key, 6), position), (shards_of,), jnp.float32, low / len(shards), largest / len(shards))
        gain = gain * jnp.repeat(jnp.exp(draws), extent[position] // shards_of).reshape((-1,) + (1,) * (len(extent) - 1 - position))
    return gain


def bell_draw(key, shape, deviation, most, shards=(), kind=jnp.bfloat16):
    gain = level_of(key, shape, shards, -0.22, 0.18) if shards else 1.0
    result = jax.random.normal(key, shape, jnp.float32) * deviation * gain
    return jnp.minimum(jnp.maximum(result, -most), most).astype(kind)


def setup_inputs(seed: int = 0) -> dict:
    splits = jax.random.split(jax.random.key(seed), 6)
    basis = bell_draw(splits[0], (2, RANK, NZ, NXW, NY), 1.0, 6.0, ((2, 8), (3, 4)))
    coil_maps = bell_draw(splits[1], (2, COILS, NZ, NXW, NY), 0.5, 3.0, ((2, 8), (3, 4)))
    factors = bell_draw(splits[2], (2, RANK, FRAMES), (2 * RANK) ** -0.5, 0.75, ((2, 4),))
    lines = plant(jax.random.randint(splits[3], (FRAMES, LINES), 0, RY * NZ), jax.random.fold_in(splits[3], 1), 0, (RY * NZ) - 1).astype(jnp.int32)
    kdata = bell_draw(splits[4], (2, FRAMES, LINES, COILS, NXW), 1.0, 6.0, ((2, 8), (4, 4)))
    return {"basis": basis, "coil_maps": coil_maps, "factors": factors, "lines": lines, "kdata": kdata}


HIGH = lax.Precision.HIGHEST

def twiddle(product, size):
    angle = product.astype(jnp.float32) * (2.0 * math.pi / size)
    factor = 1.0 / math.sqrt(size)
    return ((jnp.cos(angle) * factor).astype(jnp.bfloat16), (jnp.sin(angle) * factor).astype(jnp.bfloat16))

def dft_table(size, inverse):
    index = jnp.arange(size, dtype=jnp.int32)
    product = index[:, None] * index[None, :] % size
    cosine, sine = twiddle(product, size)
    imag = sine if inverse else -sine
    return jnp.stack([jnp.stack([cosine, imag]), jnp.stack([-imag, cosine])])

def rounded(value):
    return lax.optimization_barrier(value.astype(jnp.bfloat16)).astype(jnp.float32)

def reference(basis, coil_maps, factors, lines, kdata):
    fwd_y = dft_table(NY, False).astype(jnp.float32)
    inv_y = dft_table(NY, True).astype(jnp.float32)
    fwd_z = dft_table(NZ, False).astype(jnp.float32)
    inv_z = dft_table(NZ, True).astype(jnp.float32)
    column = jnp.arange(LINES, dtype=jnp.int32) // LPD
    ky_pos = column[None, :] * RY + lines // NZ
    kz_pos = lines % NZ
    v_re = factors[0].astype(jnp.float32)
    v_im = factors[1].astype(jnp.float32)
    b_re = basis[0].astype(jnp.float32)
    b_im = basis[1].astype(jnp.float32)
    scale = 1.0 / math.sqrt(COILS * LINES * NXW)

    def per_coil(carry, inputs):
        grad_acc, factor_acc = carry
        maps, data = inputs
        m_re = maps[0].astype(jnp.float32)[None]
        m_im = maps[1].astype(jnp.float32)[None]
        image = rounded(jnp.stack([m_re * b_re - m_im * b_im, m_re * b_im + m_im * b_re]))
        hybrid = rounded(jnp.einsum('plzxy,pqwy->qlzxw', image, fwd_y, precision=HIGH))
        kspace = jnp.einsum('plzxy,pqkz->qlkxy', hybrid, fwd_z, precision=HIGH)
        turned = kspace.transpose(2, 4, 0, 1, 3)
        picked = turned[kz_pos, ky_pos]
        p_re = picked[:, :, 0]
        p_im = picked[:, :, 1]
        pred_re = jnp.einsum('tjlx,lt->tjx', p_re, v_re, precision=HIGH) - jnp.einsum('tjlx,lt->tjx', p_im, v_im, precision=HIGH)
        pred_im = jnp.einsum('tjlx,lt->tjx', p_re, v_im, precision=HIGH) + jnp.einsum('tjlx,lt->tjx', p_im, v_re, precision=HIGH)
        resid = rounded(jnp.stack([pred_re, pred_im]) - data.astype(jnp.float32))
        r_re = resid[0]
        r_im = resid[1]
        gv_re = jnp.einsum('tjlx,tjx->lt', p_re, r_re, precision=HIGH) + jnp.einsum('tjlx,tjx->lt', p_im, r_im, precision=HIGH)
        gv_im = jnp.einsum('tjlx,tjx->lt', p_re, r_im, precision=HIGH) - jnp.einsum('tjlx,tjx->lt', p_im, r_re, precision=HIGH)
        vt_re = v_re.T[:, None, :, None]
        vt_im = v_im.T[:, None, :, None]
        val_re = r_re[:, :, None, :] * vt_re + r_im[:, :, None, :] * vt_im
        val_im = r_im[:, :, None, :] * vt_re - r_re[:, :, None, :] * vt_im
        values = jnp.stack([val_re, val_im], axis=2)
        kgrad = jnp.zeros((NZ, NY, 2, RANK, NXW), jnp.float32).at[kz_pos, ky_pos].add(values)
        zgrad = rounded(jnp.einsum('kwplx,pqzk->qlzxw', kgrad, inv_z, precision=HIGH))
        imgrad = jnp.einsum('plzxw,pqyw->qlzxy', zgrad, inv_y, precision=HIGH)
        g_re = imgrad[0]
        g_im = imgrad[1]
        update = jnp.stack([m_re * g_re + m_im * g_im, m_re * g_im - m_im * g_re])
        return ((grad_acc + update, factor_acc + jnp.stack([gv_re, gv_im])), None)
    start = (jnp.zeros((2, RANK, NZ, NXW, NY), jnp.float32), jnp.zeros((2, RANK, FRAMES), jnp.float32))
    inputs = (coil_maps.transpose(1, 0, 2, 3, 4), kdata.transpose(3, 0, 1, 2, 4))
    (grad_acc, factor_acc), unused = lax.scan(per_coil, start, inputs)
    return (grad_acc, factor_acc * scale)
```

```python
import functools
import math

import jax
import jax.numpy as jnp
import numpy as np
from jax import lax
from jax.experimental import pallas as pl
from jax.experimental.pallas import tpu as pltpu
from jax.sharding import PartitionSpec as P

F32 = jnp.float32
BF16 = jnp.bfloat16
LANES = 128
TILE = 16


def dft_parts(size):
    index = np.arange(size, dtype=np.int64)
    angle = ((index[:, None] * index[None, :]) % size).astype(np.float64) * (2.0 * math.pi / size)
    factor = 1.0 / math.sqrt(size)
    return (np.cos(angle) * factor).astype(BF16), (np.sin(angle) * factor).astype(BF16)


def nn(a, b):
    return lax.dot_general(a, b, (((1,), (0,)), ((), ())), preferred_element_type=F32)


def nt(a, b):
    return lax.dot_general(a, b, (((1,), (1,)), ((), ())), preferred_element_type=F32)


def tn(a, b):
    return lax.dot_general(a, b, (((0,), (0,)), ((), ())), preferred_element_type=F32)


def total(refs):
    value = refs[0][...].astype(F32)
    for ref in refs[1:]:
        value = value + ref[...].astype(F32)
    return value


def factor_matrix(refs):
    v = total(refs)
    rank = v.shape[1] // 2
    v_re, v_im = v[:, :rank], v[:, rank:]
    top = jnp.concatenate([v_re, -v_im], axis=1)
    bottom = jnp.concatenate([v_im, v_re], axis=1)
    return jnp.concatenate([top, bottom], axis=0).astype(BF16)


def predict_kernel(n_v, n_line, frames, slab, *refs):
    v_refs, refs = refs[:n_v], refs[n_v:]
    line_refs, refs = refs[:n_line], refs[n_line:]
    (b_ref, m_ref, taby_ref, tabz_ref, coil_ref, kd_ref, pred_ref, w_ref, fz_ref, i_ref, x_ref) = refs
    width = b_ref.shape[2]
    rows = m_ref.shape[1]
    pad = x_ref.shape[1]
    depth = tabz_ref.shape[0]
    samples = w_ref.shape[0]
    per = samples // frames
    coils = rows // slab

    pos = total(line_refs)
    groups = pos.shape[0] // 2
    ky = pos[:groups].T
    kz = pos[groups:].T
    at_y = lax.broadcasted_iota(jnp.int32, (LANES, width), 1).astype(F32)
    at_z = lax.broadcasted_iota(jnp.int32, (LANES, depth), 1).astype(F32)
    for g in range(groups):
        hot_y = jnp.where(at_y == ky[:, g : g + 1], 1.0, 0.0).astype(BF16)
        w_ref[g * LANES : (g + 1) * LANES, :] = nn(hot_y, taby_ref[...]).astype(BF16)
        hot_z = jnp.where(at_z == kz[:, g : g + 1], 1.0, 0.0).astype(BF16)
        fz_ref[g * LANES : (g + 1) * LANES, :] = nn(hot_z, tabz_ref[...]).astype(BF16)

    v = factor_matrix(v_refs)
    halves = width // LANES
    for z in range(slab):
        image = nn(v, b_ref[z])
        for h in range(halves):
            i_ref[h, z * 2 * frames : (z + 1) * 2 * frames, :] = image[
                :, h * LANES : (h + 1) * LANES
            ]

    m_re = m_ref[0].reshape(coils, slab, width)
    m_im = m_ref[1].reshape(coils, slab, width)

    def frame(t, carry):
        i_re, i_im = (
            jnp.concatenate(
                [i_ref[h, pl.ds(at, slab, stride=2 * frames), :] for h in range(halves)], axis=1
            ).astype(BF16)[None]
            for at in (t, frames + t)
        )
        p_re = (m_re * i_re - m_im * i_im).reshape(rows, width)
        p_im = (m_re * i_im + m_im * i_re).reshape(rows, width)
        at = pl.ds(pl.multiple_of(t * per, TILE), per)
        w = w_ref[at, :]
        lhs = jnp.concatenate([w[:, : 2 * width], w[:, 2 * width :]], axis=0)
        y = nt(lhs[:, :width], p_re) + nt(lhs[:, width:], p_im)
        y_re, y_im = y[:per], y[per:]
        f = fz_ref[at, :].astype(F32)
        f_cos, f_sin = f[:, :rows], f[:, pad : pad + rows]
        x_re = y_re * f_cos + y_im * f_sin
        x_im = y_im * f_cos - y_re * f_sin
        base = pl.multiple_of(t * 2 * per, TILE)
        x_ref[pl.ds(base, 2 * per), :rows] = jnp.concatenate([x_re, x_im], axis=0).astype(BF16)
        return carry

    lax.fori_loop(0, frames, frame, 0, unroll=2)
    chunk = min(512, 2 * samples)
    for s in range(0, 2 * samples, chunk):
        part = nt(coil_ref[:, :rows], x_ref[s : s + chunk, :rows])
        pred_ref[:, s : s + chunk] = (part - kd_ref[:, s : s + chunk].astype(F32)).astype(BF16)


def gradient_kernel(n_v, n_r, frames, slab, scale, *refs):
    v_refs, refs = refs[:n_v], refs[n_v:]
    r_refs, refs = refs[:n_r], refs[n_r:]
    (b_ref, m_ref, coil_ref, w_ref, fz_ref, grad_ref, fg_ref, g_ref, r_ref, mf_ref) = refs
    width = b_ref.shape[2]
    rows = m_ref.shape[1]
    pad = coil_ref.shape[1]
    samples = w_ref.shape[0]
    per = samples // frames
    coils = rows // slab

    resid = total(r_refs).astype(BF16)
    chunk = min(512, 2 * samples)
    for s in range(0, 2 * samples, chunk):
        r_ref[s : s + chunk, :] = tn(resid[:, s : s + chunk], coil_ref[...])
    mf_ref[...] = m_ref[...].astype(F32)
    halves = width // LANES

    def frame(t, carry):
        at = pl.ds(pl.multiple_of(t * per, TILE), per)
        w = w_ref[at, :]
        rhs = jnp.concatenate([w[:, : 2 * width], w[:, 2 * width :]], axis=0)
        f = fz_ref[at, :].astype(F32)
        f_cos, f_sin = f[:, :pad], f[:, pad:]
        base = pl.multiple_of(t * 2 * per, TILE)
        r = r_ref[pl.ds(base, 2 * per), :]
        r_re, r_im = r[:per], r[per:]
        q = jnp.concatenate([r_re * f_cos - r_im * f_sin, r_im * f_cos + r_re * f_sin], axis=0)
        u = tn(q[:, :rows].astype(BF16), rhs)
        u_re = u[:, :width].reshape(coils, slab, width)
        u_im = u[:, width:].reshape(coils, slab, width)
        m_re = mf_ref[0].reshape(coils, slab, width)
        m_im = mf_ref[1].reshape(coils, slab, width)
        g_re = jnp.sum(m_re * u_re + m_im * u_im, axis=0)
        g_im = jnp.sum(m_re * u_im - m_im * u_re, axis=0)
        for h in range(halves):
            lanes = slice(h * LANES, (h + 1) * LANES)
            g_ref[h, pl.ds(t, slab, stride=2 * frames), :] = g_re[:, lanes]
            g_ref[h, pl.ds(frames + t, slab, stride=2 * frames), :] = g_im[:, lanes]
        return carry

    lax.fori_loop(0, frames, frame, 0, unroll=2)
    v = factor_matrix(v_refs)
    rank = v.shape[1] // 2
    acc = jnp.zeros((2 * frames, 2 * rank), F32)
    for z in range(slab):
        at = pl.ds(z * 2 * frames, 2 * frames)
        g = jnp.concatenate([g_ref[h, at, :] for h in range(halves)], axis=1).astype(BF16)
        acc = acc + nt(g, b_ref[z])
        grad = tn(v, g)
        for h in range(halves):
            grad_ref[pl.ds(z * halves + h, 2 * rank, stride=slab * halves), :] = grad[
                :, h * LANES : (h + 1) * LANES
            ]
    top, bottom = acc[:frames], acc[frames:]
    g_re = top[:, :rank] + bottom[:, rank:]
    g_im = bottom[:, :rank] - top[:, rank:]
    fg_ref[...] = jnp.concatenate([g_re, g_im], axis=1) * scale


def stages(size):
    steps, stride = [], 1
    if (size.bit_length() - 1) % 2:
        steps.append((1, 2))
        stride = 2
    while stride < size:
        steps.append((stride, 4))
        stride *= 4
    return steps


def swap(value, axis, distance):
    size = lax.axis_size(axis)
    return lax.ppermute(value, axis, [(i, i ^ distance) for i in range(size)])


def shares(value, axis):
    steps = stages(lax.axis_size(axis))
    for number, (stride, radix) in enumerate(steps):
        terms = [value] + [swap(value, axis, stride * d) for d in range(1, radix)]
        if number + 1 < len(steps):
            value = functools.reduce(
                lambda a, b: a + b, [term.astype(F32) for term in terms]
            ).astype(value.dtype)
    return terms


def call(kernel, outs, scratch, flops, *operands):
    nbytes = sum(math.prod(x.shape) * x.dtype.itemsize for x in operands)
    return pl.pallas_call(
        kernel,
        out_shape=outs,
        scratch_shapes=scratch,
        compiler_params=pltpu.CompilerParams(vmem_limit_bytes=56 * 1024 * 1024),
        cost_estimate=pl.CostEstimate(flops=flops, bytes_accessed=nbytes, transcendentals=0),
    )(*operands)


def one_position(basis, coil_maps, factors, lines, kdata, scale):
    n_cuts, n_frame = lax.axis_size("cuts"), lax.axis_size("frame")
    cut, part = lax.axis_index("cuts"), lax.axis_index("frame")
    rank, slab, width = basis.shape[1:]
    coils = coil_maps.shape[1]
    own = lines.shape[1]
    frames = lines.shape[0]
    per = own * n_cuts
    samples = frames * per
    depth = slab * n_cuts
    ky_rows = width // n_cuts

    spread = max(1, TILE // slab)
    tall = spread * slab
    coil_groups = -(-coils // spread)
    rows = coil_groups * tall
    pad = -(-rows // LANES) * LANES
    coil_rows = -(-coils // TILE) * TILE

    kind = BF16 if max(width, depth) <= 256 else F32
    mine = jnp.stack([cut * ky_rows + lines // depth, lines % depth])
    column_owner = jnp.arange(per, dtype=jnp.int32) // own == cut
    placed = jnp.where(column_owner, jnp.tile(mine, (1, 1, n_cuts)), 0)
    line_terms = shares(placed.astype(kind).reshape(2 * samples // LANES, LANES), "cuts")
    turned = factors.transpose(2, 0, 1).reshape(factors.shape[2], 2 * rank)
    row_owner = jnp.arange(frames, dtype=jnp.int32)[:, None] // factors.shape[2] == part
    v_terms = shares(
        jnp.where(row_owner, jnp.tile(turned, (n_frame, 1)), jnp.zeros((), BF16)), "frame"
    )

    tab_cos, tab_sin = dft_parts(width)
    taby = jnp.asarray(np.concatenate([tab_cos, tab_sin, -tab_sin, tab_cos], axis=1))
    z_cos, z_sin = dft_parts(depth)
    tabz = lax.dynamic_slice_in_dim(jnp.asarray(np.stack([z_cos, z_sin])), cut * slab, slab, axis=2)
    tabz = jnp.pad(jnp.tile(tabz, (1, 1, rows // slab)), ((0, 0), (0, 0), (0, pad - rows)))
    tabz = jnp.concatenate([tabz[0], tabz[1]], axis=1)
    row_coil = np.arange(pad) // slab
    coil_of = jnp.asarray(
        ((row_coil[None] == np.arange(coil_rows)[:, None]) & (row_coil[None] < coils)).astype(BF16)
    )

    b_rows = jnp.tile(basis.reshape(2 * rank, slab, width).transpose(1, 0, 2), (spread, 1, 1))
    m_rows = jnp.pad(coil_maps, ((0, 0), (0, coil_groups * spread - coils), (0, 0), (0, 0)))
    m_rows = m_rows.reshape(2, rows, width)
    kd = jnp.tile(kdata.transpose(3, 1, 0, 2), (1, 1, 1, n_cuts))
    kd = jnp.where(column_owner, kd, jnp.zeros((), BF16)).reshape(coils, 2 * samples)
    kd = jnp.pad(kd, ((0, coil_rows - coils), (0, 0)))

    flops = 2 * frames * 2 * per * rows * 2 * width
    predicted, w, fz = call(
        functools.partial(predict_kernel, len(v_terms), len(line_terms), frames, tall),
        (
            jax.ShapeDtypeStruct((coil_rows, 2 * samples), BF16),
            jax.ShapeDtypeStruct((samples, 4 * width), BF16),
            jax.ShapeDtypeStruct((samples, 2 * pad), BF16),
        ),
        [pltpu.VMEM((width // LANES, tall * 2 * frames, LANES), F32), pltpu.VMEM((2 * samples, pad), BF16)],
        flops,
        *v_terms, *line_terms, b_rows, m_rows, taby, tabz, coil_of, kd,
    )
    resid_terms = shares(predicted, "cuts")
    grad, fg = call(
        functools.partial(
            gradient_kernel, len(v_terms), len(resid_terms), frames, tall, scale
        ),
        (
            jax.ShapeDtypeStruct((2 * rank * tall * width // LANES, LANES), F32),
            jax.ShapeDtypeStruct((frames, 2 * rank), F32),
        ),
        [
            pltpu.VMEM((width // LANES, tall * 2 * frames, LANES), F32),
            pltpu.VMEM((2 * samples, pad), F32),
            pltpu.VMEM((2, rows, width), F32),
        ],
        flops,
        *v_terms, *resid_terms, b_rows, m_rows, coil_of, w, fz,
    )
    if spread > 1:
        grad = jnp.sum(grad.reshape(2, rank, spread, slab, width), axis=2)
    return grad.reshape(2, rank, slab, width), fg


def body(basis, coil_maps, factors, lines, kdata):
    n_cuts, n_frame = lax.axis_size("cuts"), lax.axis_size("frame")
    readout = basis.shape[3]
    rank = basis.shape[1]
    own = factors.shape[2]
    scale = 1.0 / math.sqrt(coil_maps.shape[1] * lines.shape[1] * n_cuts * readout * n_frame)
    grads, fg = [], 0.0
    for x in range(readout):
        grad, term = one_position(
            basis[:, :, :, x], coil_maps[:, :, :, x], factors, lines, kdata[..., x], scale
        )
        grads.append(grad)
        fg = fg + term
    basis_grad = grads[0][:, :, :, None] if readout == 1 else jnp.stack(grads, axis=3)
    pieces = jnp.broadcast_to(
        fg.reshape(1, n_frame, own, 2 * rank), (n_cuts, n_frame, own, 2 * rank)
    ).reshape(n_cuts * n_frame, own, 2 * rank)
    gathered = lax.all_to_all(pieces, ("cuts", "frame"), 0, 0, tiled=True)
    factor_grad = jnp.sum(gathered, axis=0).reshape(own, 2, rank).transpose(1, 2, 0)
    return basis_grad, factor_grad


def solution(mesh):
    placed = (
        P(None, None, "cuts", "frame", None),
        P(None, None, "cuts", "frame", None),
        P(None, None, "frame"),
        P(None, "cuts"),
        P(None, None, "cuts", None, "frame"),
    )
    return jax.shard_map(
        body,
        mesh=mesh,
        in_specs=placed,
        out_specs=(P(None, None, "cuts", "frame", None), P(None, None, "frame")),
        check_vma=False,
    )
```

```python
import functools
import math

import jax
import jax.numpy as jnp
import numpy as np
from jax import lax
from jax.experimental import pallas as pl
from jax.experimental.pallas import tpu as pltpu
from jax.sharding import PartitionSpec as P

F32 = jnp.float32
BF16 = jnp.bfloat16
LANES = 128
TILE = 16
PITCH = 8


def dft_parts(size):
    index = np.arange(size, dtype=np.int64)
    angle = ((index[:, None] * index[None, :]) % size).astype(np.float64) * (2.0 * math.pi / size)
    factor = 1.0 / math.sqrt(size)
    return (np.cos(angle) * factor).astype(BF16), (np.sin(angle) * factor).astype(BF16)


def nn(a, b):
    return lax.dot_general(a, b, (((1,), (0,)), ((), ())), preferred_element_type=F32)


def nt(a, b):
    return lax.dot_general(a, b, (((1,), (1,)), ((), ())), preferred_element_type=F32)


def tn(a, b):
    return lax.dot_general(a, b, (((0,), (0,)), ((), ())), preferred_element_type=F32)


def total(refs):
    value = refs[0][...].astype(F32)
    for ref in refs[1:]:
        value = value + ref[...].astype(F32)
    return value


def factor_matrix(refs):
    v = total(refs)
    rank = v.shape[1] // 2
    v_re, v_im = v[:, :rank], v[:, rank:]
    top = jnp.concatenate([v_re, -v_im], axis=1)
    bottom = jnp.concatenate([v_im, v_re], axis=1)
    return jnp.concatenate([top, bottom], axis=0).astype(BF16)


def adjoint_pair(w):
    half = w.shape[1] // 2
    return jnp.concatenate([w, jnp.concatenate([-w[:, half:], w[:, :half]], axis=1)], axis=0)


def tree(value):
    terms = [value[i] for i in range(value.shape[0])]
    while len(terms) > 1:
        odd = [terms[-1]] if len(terms) % 2 else []
        terms = [a + b for a, b in zip(terms[::2], terms[1::2])] + odd
    return terms[0].astype(F32)


def predict_kernel(n_v, n_line, frames, slab, real, *refs):
    cut = lax.axis_index("cuts")
    v_refs, refs = refs[:n_v], refs[n_v:]
    line_refs, refs = refs[:n_line], refs[n_line:]
    (b_ref, m_ref, taby_ref, tabz_ref, coil_ref, kd_ref, pred_ref, w_ref, fz_ref, i_ref, x_ref) = refs
    width = b_ref.shape[2]
    rows = m_ref.shape[1]
    pad = x_ref.shape[1]
    depth = tabz_ref.shape[0]
    samples = w_ref.shape[0]
    per = samples // frames
    coils = rows // slab
    halves = width // LANES
    pitch = 2 * frames + PITCH

    pos = total(line_refs)
    groups = pos.shape[0] // 2
    ky = pos[:groups].T
    kz = pos[groups:].T
    at_y = lax.broadcasted_iota(jnp.int32, (LANES, width), 1).astype(F32)
    at_z = lax.broadcasted_iota(jnp.int32, (LANES, depth), 1).astype(F32)
    slice_of = lax.broadcasted_iota(jnp.int32, (depth, pad), 1) % real + cut * real
    own = (lax.broadcasted_iota(jnp.int32, (depth, pad), 0) == slice_of).astype(F32).astype(BF16)
    tabz = jnp.concatenate(
        [nn(tabz_ref[:, :depth], own), nn(tabz_ref[:, depth:], own)], axis=1
    ).astype(BF16)
    for g in range(groups):
        hot_y = jnp.where(at_y == ky[:, g : g + 1], 1.0, 0.0).astype(BF16)
        w_ref[g * LANES : (g + 1) * LANES, :] = nn(hot_y, taby_ref[...]).astype(BF16)
        hot_z = jnp.where(at_z == kz[:, g : g + 1], 1.0, 0.0).astype(BF16)
        fz_ref[g * LANES : (g + 1) * LANES, :] = nn(hot_z, tabz).astype(BF16)

    v = factor_matrix(v_refs)
    for z in range(slab):
        image = nn(v, b_ref[z])
        for h in range(halves):
            i_ref[h, z * pitch : z * pitch + 2 * frames, :] = image[
                :, h * LANES : (h + 1) * LANES
            ]

    m_re = m_ref[0].reshape(coils, slab, width)
    m_im = m_ref[1].reshape(coils, slab, width)

    def frame(t, carry):
        i_re, i_im = (
            jnp.concatenate(
                [i_ref[h, pl.ds(at, slab, stride=pitch), :] for h in range(halves)], axis=1
            ).astype(BF16)[None]
            for at in (t, frames + t)
        )
        p_re = (m_re * i_re - m_im * i_im).reshape(rows, width)
        p_im = (m_re * i_im + m_im * i_re).reshape(rows, width)
        at = pl.ds(pl.multiple_of(t * per, TILE), per)
        w = w_ref[at, :]
        lhs = adjoint_pair(w)
        y = nt(lhs[:, :width], p_re) + nt(lhs[:, width:], p_im)
        y_re, y_im = y[:per], y[per:]
        f = fz_ref[at, :].astype(F32)
        f_cos, f_sin = f[:, :rows], f[:, pad : pad + rows]
        x_re = y_re * f_cos + y_im * f_sin
        x_im = y_im * f_cos - y_re * f_sin
        base = pl.multiple_of(t * 2 * per, TILE)
        x_ref[pl.ds(base, 2 * per), :rows] = jnp.concatenate([x_re, x_im], axis=0).astype(BF16)
        return carry

    lax.fori_loop(0, frames, frame, 0, unroll=math.gcd(frames, 16))
    chunk = min(512, 2 * samples)
    for s in range(0, 2 * samples, chunk):
        part = nt(coil_ref[:, :rows], x_ref[s : s + chunk, :rows])
        pred_ref[:, s : s + chunk] = (part - kd_ref[:, s : s + chunk].astype(F32)).astype(BF16)


def gradient_kernel(n_v, n_r, frames, slab, scale, *refs):
    v_refs, refs = refs[:n_v], refs[n_v:]
    r_refs, refs = refs[:n_r], refs[n_r:]
    (b_ref, m_ref, coil_ref, w_ref, fz_ref, grad_ref, fg_ref, g_ref, r_ref) = refs
    width = b_ref.shape[2]
    rows = m_ref.shape[1]
    pad = coil_ref.shape[1]
    samples = w_ref.shape[0]
    per = samples // frames
    coils = rows // slab

    resid = total(r_refs).astype(BF16)
    chunk = min(512, 2 * samples)
    for s in range(0, 2 * samples, chunk):
        r_ref[s : s + chunk, :] = tn(resid[:, s : s + chunk], coil_ref[...])
    halves = width // LANES
    pitch = 2 * frames + PITCH

    def frame(t, carry):
        at = pl.ds(pl.multiple_of(t * per, TILE), per)
        w = w_ref[at, :]
        rhs = adjoint_pair(w)
        f = fz_ref[at, :].astype(F32)
        f_cos, f_sin = f[:, :pad], f[:, pad:]
        base = pl.multiple_of(t * 2 * per, TILE)
        r = r_ref[pl.ds(base, 2 * per), :]
        r_re, r_im = r[:per], r[per:]
        q = jnp.concatenate([r_re * f_cos - r_im * f_sin, r_im * f_cos + r_re * f_sin], axis=0)
        u = tn(q[:, :rows].astype(BF16), rhs).astype(BF16)
        u_re = u[:, :width].reshape(coils, slab, width)
        u_im = u[:, width:].reshape(coils, slab, width)
        m_re = m_ref[0].reshape(coils, slab, width)
        m_im = m_ref[1].reshape(coils, slab, width)
        g_re = tree(m_re * u_re + m_im * u_im)
        g_im = tree(m_re * u_im - m_im * u_re)
        for h in range(halves):
            lanes = slice(h * LANES, (h + 1) * LANES)
            g_ref[h, pl.ds(t, slab, stride=pitch), :] = g_re[:, lanes]
            g_ref[h, pl.ds(frames + t, slab, stride=pitch), :] = g_im[:, lanes]
        return carry

    lax.fori_loop(0, frames, frame, 0, unroll=math.gcd(frames, 16))
    v = factor_matrix(v_refs)
    rank = v.shape[1] // 2
    acc = jnp.zeros((2 * frames, 2 * rank), F32)
    for z in range(slab):
        at = pl.ds(z * pitch, 2 * frames)
        g = jnp.concatenate([g_ref[h, at, :] for h in range(halves)], axis=1).astype(BF16)
        acc = acc + nt(g, b_ref[z])
        grad = tn(v, g)
        for h in range(halves):
            grad_ref[pl.ds(z * halves + h, 2 * rank, stride=slab * halves), :] = grad[
                :, h * LANES : (h + 1) * LANES
            ]
    top, bottom = acc[:frames], acc[frames:]
    g_re = top[:, :rank] + bottom[:, rank:]
    g_im = bottom[:, :rank] - top[:, rank:]
    fg = jnp.concatenate([g_re, g_im], axis=1) * scale
    n_frame, n_rows, n_lanes = fg_ref.shape[1:]
    own, fold = frames // n_frame, n_lanes // (2 * rank)
    for f in range(n_frame):
        piece = [fg[f * own + k * n_rows : f * own + (k + 1) * n_rows] for k in range(fold)]
        fg_ref[:, f] = jnp.broadcast_to(
            jnp.concatenate(piece, axis=1)[None], (fg_ref.shape[0], n_rows, n_lanes)
        )


def stages(size):
    steps, stride = [], 1
    if (size.bit_length() - 1) % 2:
        steps.append((1, 2))
        stride = 2
    while stride < size:
        steps.append((stride, 4))
        stride *= 4
    return steps


def swap(value, axis, distance):
    size = lax.axis_size(axis)
    return lax.ppermute(value, axis, [(i, i ^ distance) for i in range(size)])


def shares(value, axis):
    steps = stages(lax.axis_size(axis))
    for number, (stride, radix) in enumerate(steps):
        terms = [value] + [swap(value, axis, stride * d) for d in range(1, radix)]
        if number + 1 < len(steps):
            value = functools.reduce(
                lambda a, b: a + b, [term.astype(F32) for term in terms]
            ).astype(value.dtype)
    return terms


def call(kernel, outs, scratch, flops, *operands):
    def size(x):
        rows = [-(-x.shape[-2] // TILE) * TILE, -(-x.shape[-1] // LANES) * LANES]
        return math.prod(x.shape[:-2]) * math.prod(rows) * jnp.dtype(x.dtype).itemsize

    nbytes = sum(size(x) for x in operands)
    held = nbytes + sum(size(x) for x in (*outs, *scratch))
    limit = min(56, 10 + held * 5 // (4 * 1024 * 1024)) * 1024 * 1024
    return pl.pallas_call(
        kernel,
        out_shape=outs,
        scratch_shapes=scratch,
        compiler_params=pltpu.CompilerParams(vmem_limit_bytes=limit),
        cost_estimate=pl.CostEstimate(flops=flops, bytes_accessed=nbytes, transcendentals=0),
    )(*operands)


def one_position(basis, coil_maps, factors, lines, kdata, scale):
    n_cuts, n_frame = lax.axis_size("cuts"), lax.axis_size("frame")
    cut, part = lax.axis_index("cuts"), lax.axis_index("frame")
    rank, slab, width = basis.shape[1:]
    coils = coil_maps.shape[1]
    own = lines.shape[1]
    frames = lines.shape[0]
    per = own * n_cuts
    samples = frames * per
    depth = slab * n_cuts
    ky_rows = width // n_cuts

    spread = max(1, TILE // slab)
    tall = spread * slab
    coil_groups = -(-coils // spread)
    rows = coil_groups * tall
    pad = -(-rows // LANES) * LANES
    coil_rows = -(-coils // TILE) * TILE

    kind = BF16 if max(width, depth) <= 256 else F32
    mine = jnp.stack([cut * ky_rows + lines // depth, lines % depth])
    column_owner = jnp.arange(per, dtype=jnp.int32) // own == cut
    placed = jnp.where(column_owner, jnp.tile(mine, (1, 1, n_cuts)), 0)
    line_terms = shares(placed.astype(kind).reshape(2 * samples // LANES, LANES), "cuts")
    turned = factors.transpose(2, 0, 1).reshape(factors.shape[2], 2 * rank)
    row_owner = jnp.arange(frames, dtype=jnp.int32)[:, None] // factors.shape[2] == part
    v_terms = shares(
        jnp.where(row_owner, jnp.tile(turned, (n_frame, 1)), jnp.zeros((), BF16)), "frame"
    )

    taby = jnp.asarray(np.concatenate(dft_parts(width), axis=1))
    tabz = jnp.asarray(np.concatenate(dft_parts(depth), axis=1))
    row_coil = np.arange(pad) // slab
    coil_of = jnp.asarray(
        ((row_coil[None] == np.arange(coil_rows)[:, None]) & (row_coil[None] < coils)).astype(BF16)
    )

    b_rows = jnp.tile(basis.reshape(2 * rank, slab, width).transpose(1, 0, 2), (spread, 1, 1))
    m_rows = jnp.pad(coil_maps, ((0, 0), (0, coil_groups * spread - coils), (0, 0), (0, 0)))
    m_rows = m_rows.reshape(2, rows, width)
    kd = jnp.tile(kdata.transpose(3, 1, 0, 2), (1, 1, 1, n_cuts))
    kd = jnp.where(column_owner, kd, jnp.zeros((), BF16)).reshape(coils, 2 * samples)
    kd = jnp.pad(kd, ((0, coil_rows - coils), (0, 0)))

    fold = max(1, LANES // (2 * rank))
    flops = 2 * frames * 2 * per * rows * 2 * width
    predicted, w, fz = call(
        functools.partial(predict_kernel, len(v_terms), len(line_terms), frames, tall, slab),
        (
            jax.ShapeDtypeStruct((coil_rows, 2 * samples), BF16),
            jax.ShapeDtypeStruct((samples, 2 * width), BF16),
            jax.ShapeDtypeStruct((samples, 2 * pad), BF16),
        ),
        [pltpu.VMEM((width // LANES, tall * (2 * frames + PITCH), LANES), F32), pltpu.VMEM((2 * samples, pad), BF16)],
        flops,
        *v_terms, *line_terms, b_rows, m_rows, taby, tabz, coil_of, kd,
    )
    resid_terms = shares(predicted, "cuts")
    grad, fg = call(
        functools.partial(
            gradient_kernel, len(v_terms), len(resid_terms), frames, tall, scale
        ),
        (
            jax.ShapeDtypeStruct((2 * rank * tall * width // LANES, LANES), F32),
            jax.ShapeDtypeStruct((n_cuts, n_frame, frames // n_frame // fold, 2 * rank * fold), F32),
        ),
        [
            pltpu.VMEM((width // LANES, tall * (2 * frames + PITCH), LANES), F32),
            pltpu.VMEM((2 * samples, pad), F32),
        ],
        flops,
        *v_terms, *resid_terms, b_rows, m_rows, coil_of, w, fz,
    )
    if spread > 1:
        grad = jnp.sum(grad.reshape(2, rank, spread, slab, width), axis=2)
    return grad.reshape(2, rank, slab, width), fg


def body(basis, coil_maps, factors, lines, kdata):
    n_cuts, n_frame = lax.axis_size("cuts"), lax.axis_size("frame")
    readout = basis.shape[3]
    rank = basis.shape[1]
    own = factors.shape[2]
    scale = 1.0 / math.sqrt(coil_maps.shape[1] * lines.shape[1] * n_cuts * readout * n_frame)
    grads, fg = [], 0.0
    for x in range(readout):
        grad, term = one_position(
            basis[:, :, :, x], coil_maps[:, :, :, x], factors, lines, kdata[..., x], scale
        )
        grads.append(grad)
        fg = fg + term
    basis_grad = grads[0][:, :, :, None] if readout == 1 else jnp.stack(grads, axis=3)
    pieces = fg.reshape((n_cuts * n_frame,) + fg.shape[2:])
    gathered = jnp.sum(lax.all_to_all(pieces, ("cuts", "frame"), 0, 0, tiled=True), axis=0)
    folded = gathered.reshape(gathered.shape[0], -1, 2, rank)
    factor_grad = folded.transpose(2, 3, 1, 0).reshape(2, rank, own)
    return basis_grad, factor_grad


def solution(mesh):
    placed = (
        P(None, None, "cuts", "frame", None),
        P(None, None, "cuts", "frame", None),
        P(None, None, "frame"),
        P(None, "cuts"),
        P(None, None, "cuts", None, "frame"),
    )
    return jax.shard_map(
        body,
        mesh=mesh,
        in_specs=placed,
        out_specs=(P(None, None, "cuts", "frame", None), P(None, None, "frame")),
        check_vma=False,
    )
```

```python
import functools
import math

import jax
import jax.numpy as jnp
import numpy as np
from jax import lax
from jax.experimental import pallas as pl
from jax.experimental.pallas import tpu as pltpu
from jax.sharding import PartitionSpec as P

F32 = jnp.float32
BF16 = jnp.bfloat16
LANES = 128
TILE = 16
PITCH = 8


def dft_parts(size):
    index = np.arange(size, dtype=np.int64)
    angle = ((index[:, None] * index[None, :]) % size).astype(np.float64) * (2.0 * math.pi / size)
    factor = 1.0 / math.sqrt(size)
    return (np.cos(angle) * factor).astype(BF16), (np.sin(angle) * factor).astype(BF16)


def nn(a, b):
    return lax.dot_general(a, b, (((1,), (0,)), ((), ())), preferred_element_type=F32)


def nt(a, b):
    return lax.dot_general(a, b, (((1,), (1,)), ((), ())), preferred_element_type=F32)


def tn(a, b):
    return lax.dot_general(a, b, (((0,), (0,)), ((), ())), preferred_element_type=F32)


def total(refs):
    terms = [ref[...].astype(F32) for ref in refs]
    while len(terms) > 1:
        odd = [terms[-1]] if len(terms) % 2 else []
        terms = [a + b for a, b in zip(terms[::2], terms[1::2])] + odd
    return terms[0]


def arrived(sent_ref, got_ref):
    sent, got = sent_ref[...].astype(F32), got_ref[...].astype(F32)
    even = lax.axis_index("cuts") % 2 == 0
    return jnp.where(even, sent, got), jnp.where(even, got, sent)


def factor_matrix(v_re, v_im):
    top = jnp.concatenate([v_re, -v_im], axis=1)
    bottom = jnp.concatenate([v_im, v_re], axis=1)
    return jnp.concatenate([top, bottom], axis=0).astype(BF16)


def own_and_rest(v_ref, others):
    _, own, rank = v_ref.shape
    v = v_ref[...].astype(F32)
    starts = range(0, rank * (lax.axis_size("frame") - 1), rank)
    rest = [
        jnp.concatenate([others[p * own : (p + 1) * own, a : a + rank] for a in starts], axis=0)
        for p in range(2)
    ]
    return (v[0], v[1]), rest


def adjoint_pair(w):
    half = w.shape[1] // 2
    return jnp.concatenate([w, jnp.concatenate([-w[:, half:], w[:, :half]], axis=1)], axis=0)


def tree(value):
    terms = [value[i] for i in range(value.shape[0])]
    while len(terms) > 1:
        odd = [terms[-1]] if len(terms) % 2 else []
        terms = [a + b for a, b in zip(terms[::2], terms[1::2])] + odd
    return terms[0].astype(F32)


def frame_of(step, own):
    return ((step // own) ^ lax.axis_index("frame")) * own + step % own


def stage_kernel(real, coils, after_ref, table_ref, b_ref, *refs):
    del after_ref
    taby_out, tabz_out, coil_out, b_out, turn_ref = refs
    width, depth, pad = taby_out.shape[0], tabz_out.shape[0], coil_out.shape[1]
    taby_out[...] = table_ref[:width, : 2 * width].astype(BF16)
    table = table_ref[width : width + depth, : 2 * depth].astype(BF16)
    column = lax.broadcasted_iota(jnp.int32, coil_out.shape, 1) // real
    row = lax.broadcasted_iota(jnp.int32, coil_out.shape, 0)
    coil_out[...] = ((row == column) & (row < coils)).astype(F32).astype(BF16)
    slice_of = lax.broadcasted_iota(jnp.int32, (depth, pad), 1) % real
    slice_of = slice_of + lax.axis_index("cuts") * real
    own = (lax.broadcasted_iota(jnp.int32, (depth, pad), 0) == slice_of).astype(F32).astype(BF16)
    tabz_out[...] = jnp.concatenate(
        [nn(table[:, :depth], own), nn(table[:, depth:], own)], axis=1
    ).astype(BF16)
    images, slab, width = b_ref.shape
    pitch = turn_ref.shape[1] // images
    for h in range(width // LANES):
        lanes = slice(h * LANES, (h + 1) * LANES)
        for n in range(images):
            turn_ref[h, n * pitch : n * pitch + slab, :] = b_ref[n, :, lanes].astype(F32)
        for z in range(slab):
            rows = turn_ref[h, pl.ds(z, images, stride=pitch), :].astype(BF16)
            for k in range(z, b_out.shape[0], slab):
                b_out[k, :, lanes] = rows


def write_tables(pos, taby_ref, tabz_ref, w_ref, fz_ref):
    per, frames = pos.shape[0] // 2, pos.shape[1]
    at_y = lax.broadcasted_iota(jnp.int32, (per, taby_ref.shape[0]), 1).astype(F32)
    at_z = lax.broadcasted_iota(jnp.int32, (per, tabz_ref.shape[0]), 1).astype(F32)
    group = max(1, 128 // per)
    for g in range(0, frames, group):
        hot_y, hot_z = (
            jnp.concatenate(
                [
                    jnp.where(iota == pos[first : first + per, t : t + 1], 1.0, 0.0)
                    for t in range(g, g + group)
                ],
                axis=0,
            ).astype(BF16)
            for iota, first in ((at_y, 0), (at_z, per))
        )
        rows = slice(g * per, (g + group) * per)
        w_ref[rows, :] = nn(hot_y, taby_ref[...]).astype(BF16)
        fz_ref[rows, :] = nn(hot_z, tabz_ref[...]).astype(BF16)


def samples_step(x_ref, frames, per):
    return x_ref.shape[1] // (2 * per)


def predict_kernel(own, frames, slab, *refs):
    sent_ref, got_ref, v_ref, taby_ref, tabz_ref, coil_ref, b_ref, m_ref, kd_ref = refs[:9]
    pred_ref, w_ref, fz_ref, x_ref, i_ref = refs[9:]
    steps = frames
    width = b_ref.shape[2]
    rows = m_ref.shape[1]
    pad = fz_ref.shape[1] // 2
    per = w_ref.shape[0] // frames
    coils = rows // slab
    halves = width // LANES
    pitch = 2 * steps + PITCH
    stride = samples_step(x_ref, frames, per)

    pos, others = arrived(sent_ref, got_ref)
    write_tables(pos[: 2 * per, :frames], taby_ref, tabz_ref, w_ref, fz_ref)
    mine, rest = own_and_rest(v_ref, others)
    v = factor_matrix(*(jnp.concatenate(both, axis=0) for both in zip(mine, rest)))
    for z in range(slab):
        image = nn(v, b_ref[z])
        for h in range(halves):
            i_ref[h, z * pitch : z * pitch + 2 * steps, :] = image[:, h * LANES : (h + 1) * LANES]

    m_re = m_ref[0].reshape(coils, slab, width)
    m_im = m_ref[1].reshape(coils, slab, width)

    def frame(step, carry):
        t = frame_of(step, own)
        i_re, i_im = (
            jnp.concatenate(
                [i_ref[h, pl.ds(at, slab, stride=pitch), :] for h in range(halves)], axis=1
            ).astype(BF16)[None]
            for at in (step, steps + step)
        )
        p_re = (m_re * i_re - m_im * i_im).reshape(rows, width)
        p_im = (m_re * i_im + m_im * i_re).reshape(rows, width)
        at = pl.ds(pl.multiple_of(t * per, TILE), per)
        lhs = adjoint_pair(w_ref[at, :])
        y = nt(lhs[:, :width], p_re) + nt(lhs[:, width:], p_im)
        y_re, y_im = y[:per], y[per:]
        f = fz_ref[at, :].astype(F32)
        f_cos, f_sin = f[:, :rows], f[:, pad : pad + rows]
        x = jnp.concatenate([y_re * f_cos + y_im * f_sin, y_im * f_cos - y_re * f_sin], axis=0)
        for h in range(x_ref.shape[0]):
            lanes = min(LANES, rows - h * LANES)
            x_ref[h, pl.ds(t, 2 * per, stride=stride), :lanes] = x[:, h * LANES : h * LANES + lanes]
        return carry

    lax.fori_loop(0, steps, frame, 0, unroll=math.gcd(steps, 16))
    blocks = max(1, min(8, 512 // frames))
    for s in range(0, 2 * per, blocks):
        x = jnp.concatenate(
            [
                jnp.concatenate(
                    [x_ref[h, k * stride : k * stride + frames, :] for h in range(x_ref.shape[0])],
                    axis=1,
                )[:, :rows]
                for k in range(s, s + blocks)
            ],
            axis=0,
        )
        pred_ref[:, s * frames : (s + blocks) * frames] = nt(
            coil_ref[:, :rows], x.astype(BF16)
        ).astype(BF16)
    size = kd_ref.shape[2]
    for part in range(2):
        at = part * per * frames + lax.axis_index("cuts") * size
        at = pl.ds(pl.multiple_of(at, LANES), size)
        pred_ref[:, at] = (pred_ref[:, at].astype(F32) - kd_ref[part].astype(F32)).astype(BF16)


def gradient_kernel(first, steps, own, frames, slab, scale, n_r, *refs):
    r_refs, refs = refs[:n_r], refs[n_r:]
    if n_r:
        b_ref, m_ref, w_ref, fz_ref, coil_ref, fg_ref, gz_ref, r_ref, g_ref = refs
    else:
        b_ref, m_ref, w_ref, fz_ref, r_ref, fg_ref, gz_ref, g_ref = refs
    width = b_ref.shape[2]
    rank = b_ref.shape[1] // 2
    rows = m_ref.shape[1]
    pad = fz_ref.shape[1] // 2
    per = w_ref.shape[0] // frames
    coils = rows // slab
    halves = width // LANES
    pitch = 2 * steps + PITCH
    stride = samples_step(r_ref, frames, per)

    if n_r:
        resid = total(r_refs).astype(BF16)
        blocks = max(1, min(8, 512 // frames))
        for s in range(0, 2 * per, blocks):
            r = tn(resid[:, s * frames : (s + blocks) * frames], coil_ref[...])
            for k in range(blocks):
                at = slice((s + k) * stride, (s + k) * stride + frames)
                for h in range(r_ref.shape[0]):
                    r_ref[h, at, :] = r[
                        k * frames : (k + 1) * frames, h * LANES : (h + 1) * LANES
                    ]

    m_re = m_ref[0].reshape(coils, slab, width)
    m_im = m_ref[1].reshape(coils, slab, width)

    def frame(step, carry):
        t = frame_of(first + step, own)
        at = pl.ds(pl.multiple_of(t * per, TILE), per)
        rhs = adjoint_pair(w_ref[at, :])
        f = fz_ref[at, :].astype(F32)
        f_cos, f_sin = f[:, :pad], f[:, pad:]
        r = jnp.concatenate(
            [r_ref[h, pl.ds(t, 2 * per, stride=stride), :] for h in range(r_ref.shape[0])], axis=1
        )
        r_re, r_im = r[:per], r[per:]
        q = jnp.concatenate([r_re * f_cos - r_im * f_sin, r_im * f_cos + r_re * f_sin], axis=0)
        u = tn(q[:, :rows].astype(BF16), rhs).astype(BF16)
        u_re = u[:, :width].reshape(coils, slab, width)
        u_im = u[:, width:].reshape(coils, slab, width)
        g_re = tree(m_re * u_re + m_im * u_im)
        g_im = tree(m_re * u_im - m_im * u_re)
        for h in range(halves):
            lanes = slice(h * LANES, (h + 1) * LANES)
            g_ref[h, pl.ds(step, slab, stride=pitch), :] = g_re[:, lanes]
            g_ref[h, pl.ds(steps + step, slab, stride=pitch), :] = g_im[:, lanes]
        return carry

    lax.fori_loop(0, steps, frame, 0, unroll=math.gcd(steps, 16))
    acc = jnp.zeros((2 * steps, 2 * rank), F32)
    for z in range(slab):
        at = pl.ds(z * pitch, 2 * steps)
        g = jnp.concatenate([g_ref[h, at, :] for h in range(halves)], axis=1).astype(BF16)
        gz_ref[z] = g
        acc = acc + nt(g, b_ref[z])
    top, bottom = acc[:steps], acc[steps:]
    fg = jnp.concatenate(
        [top[:, :rank] + bottom[:, rank:], bottom[:, :rank] - top[:, rank:]], axis=1
    )
    fg_ref[...] = (fg * scale).reshape(fg_ref.shape)


def basis_kernel(sent_ref, got_ref, v_ref, rest_ref, own_ref, grad_ref):
    slab, _, width = own_ref.shape
    mine, rest = own_and_rest(v_ref, arrived(sent_ref, got_ref)[1])
    v_own, v_rest = factor_matrix(*mine), factor_matrix(*rest)
    halves = width // LANES
    for z in range(slab):
        grad = tn(v_own, own_ref[z]) + tn(v_rest, rest_ref[z])
        for h in range(halves):
            grad_ref[pl.ds(z * halves + h, grad.shape[0], stride=slab * halves), :] = grad[
                :, h * LANES : (h + 1) * LANES
            ]


def stages(size):
    steps, stride = [(1, 2)], 2
    if (size // stride).bit_length() % 2 == 0:
        steps.append((stride, 2))
        stride *= 2
    while stride < size:
        steps.append((stride, 4))
        stride *= 4
    return steps


def swap(value, axis, distance):
    size = lax.axis_size(axis)
    return lax.ppermute(value, axis, [(i, i ^ distance) for i in range(size)])


def shares(value, axis, last=1):
    steps = stages(lax.axis_size(axis))
    for number, (stride, radix) in enumerate(steps):
        if number + last == len(steps) + 1:
            return value
        terms = [value] + [swap(value, axis, stride * d) for d in range(1, radix)]
        if number + 1 < len(steps):
            value = pairs([term.astype(F32) for term in terms]).astype(value.dtype)
    return terms


def grown(value, rows, lanes):
    return jnp.pad(value, ((0, rows - value.shape[0]), (0, lanes - value.shape[1])))


def collect(positions, v_own, meanwhile):
    n_cuts, n_frame = lax.axis_size("cuts"), lax.axis_size("frame")
    even = lax.axis_index("cuts") % 2 == 0
    stride, radix = stages(n_cuts)[-1]
    near = shares(positions, "cuts", last=2)
    rank = v_own.shape[2]
    rows = max(near.shape[0], math.prod(v_own.shape[:2]))
    lanes = max(near.shape[1], rank)
    v_packet = grown(v_own.reshape(-1, rank).astype(near.dtype), rows, lanes)
    near, v_packet = lax.optimization_barrier((near, v_packet))
    packet = jnp.where(even, grown(near, rows, lanes), v_packet)
    got = []
    for d in range(1, max(radix, n_frame)):
        route = []
        for c in range(n_cuts):
            for f in range(n_frame):
                if c % 2 == 0 and d < radix:
                    route.append((c * n_frame + f, (c ^ stride * d) * n_frame + f))
                if c % 2 == 1 and d < n_frame:
                    route.append((c * n_frame + f, c * n_frame + (f ^ d)))
        got.append(lax.ppermute(packet, ("cuts", "frame"), route))
    staged = meanwhile(packet)
    got, staged = lax.optimization_barrier((got, staged))
    joined = pairs([x.astype(F32) for x in (packet, *got[: radix - 1])]).astype(near.dtype)
    others = jnp.concatenate([x[:, :rank] for x in got[: n_frame - 1]], axis=1)
    lanes = max(lanes, others.shape[1])
    sent = jnp.where(even, grown(joined, rows, lanes), grown(others, rows, lanes))
    return sent, swap(sent, "cuts", 1), staged


def call(kernel, outs, scratch, flops, *operands, limit=0):
    def size(x):
        rows = [-(-x.shape[-2] // TILE) * TILE, -(-x.shape[-1] // LANES) * LANES]
        return math.prod(x.shape[:-2]) * math.prod(rows) * jnp.dtype(x.dtype).itemsize

    nbytes = sum(size(x) for x in operands)
    held = nbytes + sum(size(x) for x in (*outs, *scratch))
    limit = limit or min(56, 10 + held * 5 // (4 * 1024 * 1024))
    return pl.pallas_call(
        kernel,
        out_shape=outs,
        scratch_shapes=scratch,
        compiler_params=pltpu.CompilerParams(vmem_limit_bytes=limit * 1024 * 1024),
        cost_estimate=pl.CostEstimate(flops=flops, bytes_accessed=nbytes, transcendentals=0),
    )(*operands)


def one_position(basis, coil_maps, factors, lines, kdata, scale):
    n_cuts, n_frame = lax.axis_size("cuts"), lax.axis_size("frame")
    cut = lax.axis_index("cuts")
    rank, slab, width = basis.shape[1:]
    coils = coil_maps.shape[1]
    columns = lines.shape[1]
    frames = lines.shape[0]
    own = factors.shape[2]
    rest = frames - own
    per = columns * n_cuts
    samples = frames * per
    depth = slab * n_cuts
    ky_rows = width // n_cuts

    spread = max(1, TILE // slab)
    tall = spread * slab
    coil_groups = -(-coils // spread)
    rows = coil_groups * tall
    pad = -(-rows // LANES) * LANES
    coil_rows = -(-coils // TILE) * TILE

    kind = BF16 if max(width, depth) <= 256 else F32
    turned = lines.T
    mine = jnp.stack([cut * ky_rows + turned // depth, turned % depth])
    owner = jnp.arange(n_cuts, dtype=jnp.int32)[None, :, None, None] == cut
    placed = jnp.where(owner, mine[:, None], 0).astype(kind).reshape(2 * per, frames)
    v_own = factors.transpose(0, 2, 1)
    table_y = np.concatenate(dft_parts(width), axis=1).astype(np.float32)
    table_z = np.concatenate(dft_parts(depth), axis=1).astype(np.float32)
    lanes = max(table_y.shape[1], table_z.shape[1])
    tables = jnp.asarray(
        np.concatenate([np.pad(x, ((0, 0), (0, lanes - x.shape[1]))) for x in (table_y, table_z)])
    )
    m_rows = jnp.pad(coil_maps, ((0, 0), (0, coil_groups * spread - coils), (0, 0), (0, 0)))
    m_rows = m_rows.reshape(2, rows, width)
    kd = kdata.transpose(0, 3, 2, 1).reshape(2, coils, columns * frames)
    kd = jnp.pad(kd, ((0, 0), (0, coil_rows - coils), (0, 0)))

    flops = 2 * 2 * per * rows * 2 * width * 8
    halves = width // LANES
    x_shape = jax.ShapeDtypeStruct((pad // LANES, 2 * per * (frames + PITCH), LANES), F32)

    def images(steps):
        return pltpu.VMEM((halves, tall * (2 * steps + PITCH), LANES), F32)

    def stage(packet):
        return call(
            functools.partial(stage_kernel, slab, coils),
            (
                jax.ShapeDtypeStruct((width, 2 * width), BF16),
                jax.ShapeDtypeStruct((depth, 2 * pad), BF16),
                jax.ShapeDtypeStruct((coil_rows, pad), BF16),
                jax.ShapeDtypeStruct((tall, 2 * rank, width), BF16),
            ),
            [pltpu.VMEM((halves, 2 * rank * (-(-slab // 8) * 8 + PITCH), LANES), F32)],
            2 * 1024 * 1024 * 1024,
            packet, tables, basis.reshape(2 * rank, slab, width),
        )

    sent, got, (taby, tabz, coil_of, b_rows) = collect(placed, v_own, stage)
    predicted, w, fz = call(
        functools.partial(predict_kernel, own, frames, tall),
        (
            jax.ShapeDtypeStruct((coil_rows, 2 * samples), BF16),
            jax.ShapeDtypeStruct((samples, 2 * width), BF16),
            jax.ShapeDtypeStruct((samples, 2 * pad), BF16),
        ),
        [pltpu.VMEM(x_shape.shape, F32), images(frames)],
        flops * frames,
        sent, got, v_own, taby, tabz, coil_of, b_rows, m_rows, kd,
    )
    resid_terms = shares(predicted, "cuts")

    def gradient(first, steps, n_r, *operands):
        outs = [
            jax.ShapeDtypeStruct((steps // own, own, 2 * rank), F32),
            jax.ShapeDtypeStruct((tall, 2 * steps, width), BF16),
        ] + ([x_shape] if n_r else [])
        return call(
            functools.partial(gradient_kernel, first, steps, own, frames, tall, scale, n_r),
            tuple(outs),
            [images(steps)],
            flops * steps,
            *operands,
        )

    fg_rest, g_rest, r = gradient(
        own, rest, len(resid_terms), *resid_terms, b_rows, m_rows, w, fz, coil_of
    )
    others = [swap(fg_rest[d - 1], "frame", d) for d in range(1, n_frame)]
    fg_own, g_own = gradient(0, own, 0, b_rows, m_rows, w, fz, r)
    (grad,) = call(
        basis_kernel,
        (jax.ShapeDtypeStruct((2 * rank * tall * halves, LANES), F32),),
        [],
        2 * 2 * rank * 2 * frames * tall * width * 8,
        sent, got, v_own, g_rest, g_own,
    )
    if spread > 1:
        grad = jnp.sum(grad.reshape(2, rank, spread, slab, width), axis=2)
    return grad.reshape(2, rank, slab, width), pairs([fg_own[0], *others])


def pairs(terms):
    while len(terms) > 1:
        odd = [terms[-1]] if len(terms) % 2 else []
        terms = [a + b for a, b in zip(terms[::2], terms[1::2])] + odd
    return terms[0]


def body(basis, coil_maps, factors, lines, kdata):
    n_cuts, n_frame = lax.axis_size("cuts"), lax.axis_size("frame")
    readout = basis.shape[3]
    rank = basis.shape[1]
    own = factors.shape[2]
    scale = 1.0 / math.sqrt(coil_maps.shape[1] * lines.shape[1] * n_cuts * readout * n_frame)
    grads, fg = [], 0.0
    for x in range(readout):
        grad, term = one_position(
            basis[:, :, :, x], coil_maps[:, :, :, x], factors, lines, kdata[..., x], scale
        )
        grads.append(grad)
        fg = fg + term
    basis_grad = grads[0][:, :, :, None] if readout == 1 else jnp.stack(grads, axis=3)
    summed = pairs(shares(fg, "cuts"))
    return basis_grad, summed.reshape(own, 2, rank).transpose(1, 2, 0)


def solution(mesh):
    placed = (
        P(None, None, "cuts", "frame", None),
        P(None, None, "cuts", "frame", None),
        P(None, None, "frame"),
        P(None, "cuts"),
        P(None, None, "cuts", None, "frame"),
    )
    return jax.shard_map(
        body,
        mesh=mesh,
        in_specs=placed,
        out_specs=(P(None, None, "cuts", "frame", None), P(None, None, "frame")),
        check_vma=False,
    )
```

```python
import functools
import math

import jax
import jax.numpy as jnp
import numpy as np
from jax import lax
from jax.experimental import pallas as pl
from jax.experimental.pallas import tpu as pltpu
from jax.sharding import PartitionSpec as P

F32 = jnp.float32
BF16 = jnp.bfloat16
LANES = 128
TILE = 16
PITCH = 8


def trig(product, size):
    angle = (product % size).astype(F32) * (2.0 * math.pi / size)
    return jnp.cos(angle), jnp.sin(angle)


def write_dft(out_ref, size, index):
    lanes = index.shape[1]
    fine = lax.broadcasted_iota(jnp.int32, (TILE, lanes), 0)
    b_cos, b_sin = trig(fine * index[:TILE], size)
    coarse = lax.broadcasted_iota(jnp.int32, (size // TILE, lanes), 0) * TILE
    a_cos, a_sin = trig(coarse * index[: size // TILE], size)
    factor = 1.0 / math.sqrt(size)
    a_cos, a_sin = a_cos * factor, a_sin * factor
    for a in range(size // TILE):
        rows = slice(a * TILE, (a + 1) * TILE)
        p_cos, p_sin = a_cos[a : a + 1], a_sin[a : a + 1]
        out_ref[rows, :lanes] = (p_cos * b_cos - p_sin * b_sin).astype(BF16)
        out_ref[rows, lanes:] = (p_sin * b_cos + p_cos * b_sin).astype(BF16)


def nn(a, b):
    return lax.dot_general(a, b, (((1,), (0,)), ((), ())), preferred_element_type=F32)


def nt(a, b):
    return lax.dot_general(a, b, (((1,), (1,)), ((), ())), preferred_element_type=F32)


def tn(a, b):
    return lax.dot_general(a, b, (((0,), (0,)), ((), ())), preferred_element_type=F32)


def total(refs):
    terms = [ref[...].astype(F32) for ref in refs]
    while len(terms) > 1:
        odd = [terms[-1]] if len(terms) % 2 else []
        terms = [a + b for a, b in zip(terms[::2], terms[1::2])] + odd
    return terms[0]


def arrived(sent_ref, got_ref):
    sent, got = sent_ref[...].astype(F32), got_ref[...].astype(F32)
    even = lax.axis_index("cuts") % 2 == 0
    return jnp.where(even, sent, got), jnp.where(even, got, sent)


def factor_matrix(v_re, v_im):
    top = jnp.concatenate([v_re, -v_im], axis=1)
    bottom = jnp.concatenate([v_im, v_re], axis=1)
    return jnp.concatenate([top, bottom], axis=0).astype(BF16)


def own_and_rest(v_ref, others):
    _, own, rank = v_ref.shape
    v = v_ref[...].astype(F32)
    starts = range(0, rank * (lax.axis_size("frame") - 1), rank)
    rest = [
        jnp.concatenate([others[p * own : (p + 1) * own, a : a + rank] for a in starts], axis=0)
        for p in range(2)
    ]
    return (v[0], v[1]), rest


def adjoint_pair(w):
    half = w.shape[1] // 2
    return jnp.concatenate([w, jnp.concatenate([-w[:, half:], w[:, :half]], axis=1)], axis=0)


def tree(value):
    terms = [value[i] for i in range(value.shape[0])]
    while len(terms) > 1:
        odd = [terms[-1]] if len(terms) % 2 else []
        terms = [a + b for a, b in zip(terms[::2], terms[1::2])] + odd
    return terms[0].astype(F32)


def frame_of(step, own):
    return ((step // own) ^ lax.axis_index("frame")) * own + step % own


def tables_kernel(real, coils, after_ref, taby_ref, tabz_ref, coil_ref):
    del after_ref
    width, depth, pad = taby_ref.shape[0], tabz_ref.shape[0], coil_ref.shape[2]
    write_dft(taby_ref, width, lax.broadcasted_iota(jnp.int32, (max(TILE, width // TILE), width), 1))
    slice_of = lax.broadcasted_iota(jnp.int32, (max(TILE, depth // TILE), pad), 1) % real
    write_dft(tabz_ref, depth, slice_of + lax.axis_index("cuts") * real)
    column = lax.broadcasted_iota(jnp.int32, coil_ref.shape[1:], 1) // real
    row = lax.broadcasted_iota(jnp.int32, coil_ref.shape[1:], 0)
    for part in range(2):
        place = (row == column + part * coils) & (column < coils)
        coil_ref[part] = place.astype(F32).astype(BF16)


def turn_kernel(after_ref, b_ref, b_out, turn_ref):
    del after_ref
    images, slab, width = b_ref.shape
    pitch = turn_ref.shape[1] // images
    for h in range(width // LANES):
        lanes = slice(h * LANES, (h + 1) * LANES)
        for n in range(images):
            turn_ref[h, n * pitch : n * pitch + slab, :] = b_ref[n, :, lanes].astype(F32)
        for z in range(slab):
            rows = turn_ref[h, pl.ds(z, images, stride=pitch), :].astype(BF16)
            for k in range(z, b_out.shape[0], slab):
                b_out[k, :, lanes] = rows


def write_tables(pos, taby_ref, tabz_ref, w_ref, fz_ref):
    per, frames = pos.shape[0] // 2, pos.shape[1]
    at_y = lax.broadcasted_iota(jnp.int32, (per, taby_ref.shape[0]), 1).astype(F32)
    at_z = lax.broadcasted_iota(jnp.int32, (per, tabz_ref.shape[0]), 1).astype(F32)
    group = max(1, 128 // per)
    for g in range(0, frames, group):
        hot_y, hot_z = (
            jnp.concatenate(
                [
                    jnp.where(iota == pos[first : first + per, t : t + 1], 1.0, 0.0)
                    for t in range(g, g + group)
                ],
                axis=0,
            ).astype(BF16)
            for iota, first in ((at_y, 0), (at_z, per))
        )
        rows = slice(g * per, (g + group) * per)
        w_ref[rows, :] = nn(hot_y, taby_ref[...]).astype(BF16)
        fz_ref[rows, :] = nn(hot_z, tabz_ref[...]).astype(BF16)


def samples_step(x_ref, frames, per):
    return x_ref.shape[1] // (2 * per)


def predict_kernel(own, frames, slab, *refs):
    sent_ref, got_ref, v_ref, taby_ref, tabz_ref, coil_ref, b_ref, m_ref, kd_ref = refs[:9]
    pred_ref, w_ref, fz_ref, x_ref, i_ref = refs[9:]
    steps = frames
    width = b_ref.shape[2]
    rows = m_ref.shape[1]
    pad = fz_ref.shape[1] // 2
    per = w_ref.shape[0] // frames
    coils = rows // slab
    halves = width // LANES
    pitch = 2 * steps + PITCH
    stride = samples_step(x_ref, frames, per)

    pos, others = arrived(sent_ref, got_ref)
    write_tables(pos[: 2 * per, :frames], taby_ref, tabz_ref, w_ref, fz_ref)
    mine, rest = own_and_rest(v_ref, others)
    v = factor_matrix(*(jnp.concatenate(both, axis=0) for both in zip(mine, rest)))
    for z in range(slab):
        image = nn(v, b_ref[z])
        for h in range(halves):
            i_ref[h, z * pitch : z * pitch + 2 * steps, :] = image[:, h * LANES : (h + 1) * LANES]

    m_re = m_ref[0].reshape(coils, slab, width)
    m_im = m_ref[1].reshape(coils, slab, width)

    def frame(step, carry):
        t = frame_of(step, own)
        i_re, i_im = (
            jnp.concatenate(
                [i_ref[h, pl.ds(at, slab, stride=pitch), :] for h in range(halves)], axis=1
            ).astype(BF16)[None]
            for at in (step, steps + step)
        )
        p_re = (m_re * i_re - m_im * i_im).reshape(rows, width)
        p_im = (m_re * i_im + m_im * i_re).reshape(rows, width)
        at = pl.ds(pl.multiple_of(t * per, TILE), per)
        lhs = adjoint_pair(w_ref[at, :])
        y = nt(lhs[:, :width], p_re) + nt(lhs[:, width:], p_im)
        y_re, y_im = y[:per], y[per:]
        f = fz_ref[at, :].astype(F32)
        f_cos, f_sin = f[:, :rows], f[:, pad : pad + rows]
        x = jnp.concatenate([y_re * f_cos + y_im * f_sin, y_im * f_cos - y_re * f_sin], axis=0)
        for h in range(x_ref.shape[0]):
            lanes = min(LANES, rows - h * LANES)
            x_ref[h, pl.ds(t, 2 * per, stride=stride), :lanes] = x[:, h * LANES : h * LANES + lanes]
        return carry

    lax.fori_loop(0, steps, frame, 0, unroll=math.gcd(steps, 32))
    blocks = max(1, min(per, 512 // frames))

    def summed(part, first):
        at = [(part * per + first + k) * stride for k in range(blocks)]
        halves_of = [
            jnp.concatenate([x_ref[h, a : a + frames, :] for a in at], axis=0)
            for h in range(x_ref.shape[0])
        ]
        x = jnp.concatenate(halves_of, axis=1)[:, :rows].astype(BF16)
        return nt(coil_ref[part, :, :rows], x)

    for first in range(0, per, blocks):
        pred_ref[:, first * frames : (first + blocks) * frames] = (
            summed(0, first) + summed(1, first)
        ).astype(BF16)
    size = kd_ref.shape[1]
    at = pl.ds(pl.multiple_of(lax.axis_index("cuts") * size, LANES), size)
    pred_ref[:, at] = (pred_ref[:, at].astype(F32) - kd_ref[...].astype(F32)).astype(BF16)


def gradient_kernel(own, frames, slab, scale, n_r, *refs):
    r_refs, refs = refs[:n_r], refs[n_r:]
    b_ref, m_ref, w_ref, fz_ref, coil_ref, fg_ref, gz_ref, r_ref, g_ref = refs
    steps = frames
    width = b_ref.shape[2]
    rank = b_ref.shape[1] // 2
    rows = m_ref.shape[1]
    pad = fz_ref.shape[1] // 2
    per = w_ref.shape[0] // frames
    coils = rows // slab
    halves = width // LANES
    pitch = 2 * steps + PITCH
    stride = samples_step(r_ref, frames, per)

    resid = total(r_refs).astype(BF16)
    blocks = max(1, min(per, 512 // frames))
    for part in range(2):
        for first in range(0, per, blocks):
            r = tn(resid[:, first * frames : (first + blocks) * frames], coil_ref[part])
            for k in range(blocks):
                at = (part * per + first + k) * stride
                for h in range(r_ref.shape[0]):
                    r_ref[h, at : at + frames, :] = r[
                        k * frames : (k + 1) * frames, h * LANES : (h + 1) * LANES
                    ]

    m_re = m_ref[0].reshape(coils, slab, width)
    m_im = m_ref[1].reshape(coils, slab, width)

    def frame(step, carry):
        t = frame_of(step, own)
        at = pl.ds(pl.multiple_of(t * per, TILE), per)
        rhs = adjoint_pair(w_ref[at, :])
        f = fz_ref[at, :].astype(F32)
        f_cos, f_sin = f[:, :pad], f[:, pad:]
        r = jnp.concatenate(
            [r_ref[h, pl.ds(t, 2 * per, stride=stride), :] for h in range(r_ref.shape[0])], axis=1
        )
        r_re, r_im = r[:per], r[per:]
        q = jnp.concatenate([r_re * f_cos - r_im * f_sin, r_im * f_cos + r_re * f_sin], axis=0)
        u = tn(q[:, :rows].astype(BF16), rhs).astype(BF16)
        u_re = u[:, :width].reshape(coils, slab, width)
        u_im = u[:, width:].reshape(coils, slab, width)
        g_re = tree(m_re * u_re + m_im * u_im)
        g_im = tree(m_re * u_im - m_im * u_re)
        for h in range(halves):
            lanes = slice(h * LANES, (h + 1) * LANES)
            g_ref[h, pl.ds(step, slab, stride=pitch), :] = g_re[:, lanes]
            g_ref[h, pl.ds(steps + step, slab, stride=pitch), :] = g_im[:, lanes]
        return carry

    lax.fori_loop(0, steps, frame, 0, unroll=math.gcd(steps, 32))
    acc = jnp.zeros((2 * steps, 2 * rank), F32)
    for z in range(slab):
        at = pl.ds(z * pitch, 2 * steps)
        g = jnp.concatenate([g_ref[h, at, :] for h in range(halves)], axis=1).astype(BF16)
        gz_ref[z] = g
        acc = acc + nt(g, b_ref[z])
    top, bottom = acc[:steps], acc[steps:]
    fg = jnp.concatenate(
        [top[:, :rank] + bottom[:, rank:], bottom[:, :rank] - top[:, rank:]], axis=1
    )
    fg = (fg * scale).astype(fg_ref.dtype)
    n_cuts, n_frame, n_rows, n_lanes = fg_ref.shape
    for d in range(n_frame):
        piece = jnp.concatenate(
            [
                fg[d * own + k : d * own + k + n_rows].astype(F32)
                for k in range(0, own, n_rows)
            ],
            axis=1,
        ).astype(fg_ref.dtype)
        target = lax.axis_index("frame") ^ d
        for c in range(n_cuts):
            fg_ref[c, pl.ds(target, 1)] = piece[None]


def basis_kernel(sent_ref, got_ref, v_ref, g_ref, grad_ref):
    slab, _, width = g_ref.shape
    mine, rest = own_and_rest(v_ref, arrived(sent_ref, got_ref)[1])
    v = factor_matrix(*(jnp.concatenate(both, axis=0) for both in zip(mine, rest)))
    halves = width // LANES
    for z in range(slab):
        grad = tn(v, g_ref[z])
        for h in range(halves):
            grad_ref[pl.ds(z * halves + h, grad.shape[0], stride=slab * halves), :] = grad[
                :, h * LANES : (h + 1) * LANES
            ]


def stages(size):
    steps, stride = [(1, 2)], 2
    if (size // stride).bit_length() % 2 == 0:
        steps.append((stride, 2))
        stride *= 2
    while stride < size:
        steps.append((stride, 4))
        stride *= 4
    return steps


def swap(value, axis, distance):
    size = lax.axis_size(axis)
    return lax.ppermute(value, axis, [(i, i ^ distance) for i in range(size)])


def shares(value, axis, last=1):
    steps = stages(lax.axis_size(axis))
    for number, (stride, radix) in enumerate(steps):
        if number + last == len(steps) + 1:
            return value
        terms = [value] + [swap(value, axis, stride * d) for d in range(1, radix)]
        if number + 1 < len(steps):
            value = pairs([term.astype(F32) for term in terms]).astype(value.dtype)
    return terms


def grown(value, rows, lanes):
    return jnp.pad(value, ((0, rows - value.shape[0]), (0, lanes - value.shape[1])))


def collect(positions, v_own, meanwhile):
    n_cuts, n_frame = lax.axis_size("cuts"), lax.axis_size("frame")
    even = lax.axis_index("cuts") % 2 == 0
    stride, radix = stages(n_cuts)[-1]
    near = shares(positions, "cuts", last=2)
    rank = v_own.shape[2]
    rows = max(near.shape[0], math.prod(v_own.shape[:2]))
    lanes = max(near.shape[1], rank)
    v_packet = grown(v_own.reshape(-1, rank).astype(near.dtype), rows, lanes)
    near, v_packet = lax.optimization_barrier((near, v_packet))
    packet = jnp.where(even, grown(near, rows, lanes), v_packet)
    got = []
    for d in range(1, max(radix, n_frame)):
        route = []
        for c in range(n_cuts):
            for f in range(n_frame):
                if c % 2 == 0 and d < radix:
                    route.append((c * n_frame + f, (c ^ stride * d) * n_frame + f))
                if c % 2 == 1 and d < n_frame:
                    route.append((c * n_frame + f, c * n_frame + (f ^ d)))
        got.append(lax.ppermute(packet, ("cuts", "frame"), route))
    staged = meanwhile(packet)
    got, staged = lax.optimization_barrier((got, staged))
    joined = pairs([x.astype(F32) for x in (packet, *got[: radix - 1])]).astype(near.dtype)
    others = jnp.concatenate([x[:, :rank] for x in got[: n_frame - 1]], axis=1)
    lanes = max(lanes, others.shape[1])
    sent = jnp.where(even, grown(joined, rows, lanes), grown(others, rows, lanes))
    return sent, swap(sent, "cuts", 1), staged


def call(kernel, outs, scratch, flops, *operands, limit=0):
    def size(x):
        rows = [-(-x.shape[-2] // TILE) * TILE, -(-x.shape[-1] // LANES) * LANES]
        return math.prod(x.shape[:-2]) * math.prod(rows) * jnp.dtype(x.dtype).itemsize

    nbytes = sum(size(x) for x in operands)
    held = nbytes + sum(size(x) for x in (*outs, *scratch))
    limit = limit or min(56, 10 + held * 5 // (4 * 1024 * 1024))
    return pl.pallas_call(
        kernel,
        out_shape=outs,
        scratch_shapes=scratch,
        compiler_params=pltpu.CompilerParams(vmem_limit_bytes=limit * 1024 * 1024),
        cost_estimate=pl.CostEstimate(flops=flops, bytes_accessed=nbytes, transcendentals=0),
    )(*operands)


def one_position(basis, coil_maps, factors, lines, kdata, scale):
    n_cuts, n_frame = lax.axis_size("cuts"), lax.axis_size("frame")
    cut = lax.axis_index("cuts")
    rank, slab, width = basis.shape[1:]
    coils = coil_maps.shape[1]
    columns = lines.shape[1]
    frames = lines.shape[0]
    own = factors.shape[2]
    per = columns * n_cuts
    samples = frames * per
    depth = slab * n_cuts
    ky_rows = width // n_cuts

    spread = max(1, TILE // slab)
    tall = spread * slab
    coil_groups = -(-coils // spread)
    rows = coil_groups * tall
    pad = -(-rows // LANES) * LANES
    coil_rows = -(-2 * coils // 8) * 8

    kind = BF16 if max(width, depth) <= 256 else F32
    turned = lines.T
    mine = jnp.stack([cut * ky_rows + turned // depth, turned % depth])
    owner = jnp.arange(n_cuts, dtype=jnp.int32)[None, :, None, None] == cut
    placed = jnp.where(owner, mine[:, None], 0).astype(kind).reshape(2 * per, frames)
    v_own = factors.transpose(0, 2, 1)
    m_rows = jnp.pad(coil_maps, ((0, 0), (0, coil_groups * spread - coils), (0, 0), (0, 0)))
    m_rows = m_rows.reshape(2, rows, width)
    flops = 2 * 2 * per * rows * 2 * width * 8
    halves = width // LANES
    x_shape = jax.ShapeDtypeStruct((pad // LANES, 2 * per * (frames + PITCH), LANES), F32)

    def images(steps):
        return pltpu.VMEM((halves, tall * (2 * steps + PITCH), LANES), F32)

    def stage(packet):
        return call(
            functools.partial(tables_kernel, slab, coils),
            (
                jax.ShapeDtypeStruct((width, 2 * width), BF16),
                jax.ShapeDtypeStruct((depth, 2 * pad), BF16),
                jax.ShapeDtypeStruct((2, coil_rows, pad), BF16),
            ),
            [],
            1024 * 1024 * 1024,
            packet,
        )

    sent, got, (taby, tabz, coil_of) = collect(placed, v_own, stage)
    (b_rows,) = call(
        turn_kernel,
        (jax.ShapeDtypeStruct((tall, 2 * rank, width), BF16),),
        [pltpu.VMEM((halves, 2 * rank * (-(-slab // 8) * 8 + PITCH), LANES), F32)],
        1024 * 1024 * 1024,
        sent, basis.reshape(2 * rank, slab, width),
    )
    _, kdata = lax.optimization_barrier((sent, kdata))
    kd = kdata.transpose(0, 3, 2, 1).reshape(2 * coils, columns * frames)
    kd = jnp.pad(kd, ((0, coil_rows - 2 * coils), (0, 0)))

    predicted, w, fz = call(
        functools.partial(predict_kernel, own, frames, tall),
        (
            jax.ShapeDtypeStruct((coil_rows, samples), BF16),
            jax.ShapeDtypeStruct((samples, 2 * width), BF16),
            jax.ShapeDtypeStruct((samples, 2 * pad), BF16),
        ),
        [pltpu.VMEM(x_shape.shape, F32), images(frames)],
        flops * frames,
        sent, got, v_own, taby, tabz, coil_of, b_rows, m_rows, kd,
    )
    resid_terms = shares(predicted, "cuts")

    fold = max(1, LANES // (2 * rank))
    pieces, g = call(
        functools.partial(gradient_kernel, own, frames, tall, scale, len(resid_terms)),
        (
            jax.ShapeDtypeStruct((n_cuts, n_frame, own // fold, 2 * rank * fold), BF16),
            jax.ShapeDtypeStruct((tall, 2 * frames, width), BF16),
        ),
        [pltpu.VMEM(x_shape.shape, F32), images(frames)],
        flops * frames,
        *resid_terms, b_rows, m_rows, w, fz, coil_of,
    )
    (grad,) = call(
        basis_kernel,
        (jax.ShapeDtypeStruct((2 * rank * tall * halves, LANES), F32),),
        [],
        2 * 2 * rank * 2 * frames * tall * width * 8,
        sent, got, v_own, g,
    )
    if spread > 1:
        grad = jnp.sum(grad.reshape(2, rank, spread, slab, width), axis=2)
    return grad.reshape(2, rank, slab, width), pieces


def pairs(terms):
    while len(terms) > 1:
        odd = [terms[-1]] if len(terms) % 2 else []
        terms = [a + b for a, b in zip(terms[::2], terms[1::2])] + odd
    return terms[0]


def body(basis, coil_maps, factors, lines, kdata):
    n_cuts, n_frame = lax.axis_size("cuts"), lax.axis_size("frame")
    readout = basis.shape[3]
    rank = basis.shape[1]
    own = factors.shape[2]
    scale = 1.0 / math.sqrt(coil_maps.shape[1] * lines.shape[1] * n_cuts * readout * n_frame)
    grads, fg = [], 0.0
    for x in range(readout):
        grad, term = one_position(
            basis[:, :, :, x], coil_maps[:, :, :, x], factors, lines, kdata[..., x], scale
        )
        grads.append(grad)
        fg = fg + term
    basis_grad = grads[0][:, :, :, None] if readout == 1 else jnp.stack(grads, axis=3)
    pieces = fg.reshape((n_cuts * n_frame,) + fg.shape[2:])
    arriving = lax.all_to_all(pieces, ("cuts", "frame"), 0, 0, tiled=True)
    summed = jnp.sum(arriving.astype(F32), axis=0)
    folded = summed.reshape(summed.shape[0], -1, 2, rank)
    return basis_grad, folded.transpose(2, 3, 1, 0).reshape(2, rank, own)


def solution(mesh):
    placed = (
        P(None, None, "cuts", "frame", None),
        P(None, None, "cuts", "frame", None),
        P(None, None, "frame"),
        P(None, "cuts"),
        P(None, None, "cuts", None, "frame"),
    )
    return jax.shard_map(
        body,
        mesh=mesh,
        in_specs=placed,
        out_specs=(P(None, None, "cuts", "frame", None), P(None, None, "frame")),
        check_vma=False,
    )
```

```python
import functools
import math

import jax
import jax.numpy as jnp
import numpy as np
from jax import lax
from jax.experimental import pallas as pl
from jax.experimental.pallas import tpu as pltpu
from jax.sharding import PartitionSpec as P

F32 = jnp.float32
BF16 = jnp.bfloat16
LANES = 128
TILE = 16
PITCH = 8


def trig(product, size):
    angle = (product % size).astype(F32) * (2.0 * math.pi / size)
    return jnp.cos(angle), jnp.sin(angle)


def write_dft(out_ref, size, index):
    lanes = index.shape[1]
    fine = lax.broadcasted_iota(jnp.int32, (TILE, lanes), 0)
    b_cos, b_sin = trig(fine * index[:TILE], size)
    coarse = lax.broadcasted_iota(jnp.int32, (size // TILE, lanes), 0) * TILE
    a_cos, a_sin = trig(coarse * index[: size // TILE], size)
    factor = 1.0 / math.sqrt(size)
    a_cos, a_sin = a_cos * factor, a_sin * factor
    for a in range(size // TILE):
        rows = slice(a * TILE, (a + 1) * TILE)
        p_cos, p_sin = a_cos[a : a + 1], a_sin[a : a + 1]
        out_ref[rows, :lanes] = (p_cos * b_cos - p_sin * b_sin).astype(BF16)
        out_ref[rows, lanes:] = (p_sin * b_cos + p_cos * b_sin).astype(BF16)


def nn(a, b):
    return lax.dot_general(a, b, (((1,), (0,)), ((), ())), preferred_element_type=F32)


def nt(a, b):
    return lax.dot_general(a, b, (((1,), (1,)), ((), ())), preferred_element_type=F32)


def tn(a, b):
    return lax.dot_general(a, b, (((0,), (0,)), ((), ())), preferred_element_type=F32)


def total(refs):
    terms = [ref[...].astype(F32) for ref in refs]
    while len(terms) > 1:
        odd = [terms[-1]] if len(terms) % 2 else []
        terms = [a + b for a, b in zip(terms[::2], terms[1::2])] + odd
    return terms[0]


def arrived(sent_ref, got_ref):
    sent, got = sent_ref[...].astype(F32), got_ref[...].astype(F32)
    even = in_pair()[1] == 0
    return jnp.where(even, sent, got), jnp.where(even, got, sent)


def factor_matrix(v_re, v_im):
    top = jnp.concatenate([v_re, -v_im], axis=1)
    bottom = jnp.concatenate([v_im, v_re], axis=1)
    return jnp.concatenate([top, bottom], axis=0).astype(BF16)


def half_factors(v_ref, others, place):
    _, own, rank = v_ref.shape
    half = own // 2
    v = v_ref[...].astype(F32)
    blocks = [(v[0], v[1])]
    for a in range(0, rank * (lax.axis_size("frame") - 1), rank):
        blocks.append((others[:own, a : a + rank], others[own : 2 * own, a : a + rank]))
    return [
        jnp.concatenate(
            [jnp.where(place == 0, b[p][:half], b[p][half:]) for b in blocks], axis=0
        )
        for p in range(2)
    ]


def adjoint_pair(w):
    half = w.shape[1] // 2
    return jnp.concatenate([w, jnp.concatenate([-w[:, half:], w[:, :half]], axis=1)], axis=0)


def tree(value):
    terms = [value[i] for i in range(value.shape[0])]
    while len(terms) > 1:
        odd = [terms[-1]] if len(terms) % 2 else []
        terms = [a + b for a, b in zip(terms[::2], terms[1::2])] + odd
    return terms[0].astype(F32)


def in_pair():
    return lax.axis_index("cuts") // 2, lax.axis_index("cuts") % 2


def frame_of(step, own):
    return ((step // own) ^ lax.axis_index("frame")) * own + step % own


def tables_kernel(real, coils, after_ref, taby_ref, tabz_ref, coil_ref):
    del after_ref
    width, depth, pad = taby_ref.shape[0], tabz_ref.shape[0], coil_ref.shape[2]
    write_dft(taby_ref, width, lax.broadcasted_iota(jnp.int32, (max(TILE, width // TILE), width), 1))
    slice_of = lax.broadcasted_iota(jnp.int32, (max(TILE, depth // TILE), pad), 1) % real
    write_dft(tabz_ref, depth, slice_of + in_pair()[0] * real)
    column = lax.broadcasted_iota(jnp.int32, coil_ref.shape[1:], 1) // real
    row = lax.broadcasted_iota(jnp.int32, coil_ref.shape[1:], 0)
    for part in range(2):
        place = (row == column + part * coils) & (column < coils)
        coil_ref[part] = place.astype(F32).astype(BF16)


def turn_kernel(after_ref, b_ref, b_got_ref, m_ref, m_got_ref, b_out, m_out, turn_ref):
    del after_ref
    images, slab, width = b_ref.shape
    pitch = turn_ref.shape[1] // images
    first = in_pair()[1] == 0
    for n, ref in enumerate((b_ref, b_got_ref)):
        start = jnp.where(first, n, 1 - n) * slab
        for h in range(width // LANES):
            lanes = slice(h * LANES, (h + 1) * LANES)
            for k in range(images):
                turn_ref[h, k * pitch : k * pitch + slab, :] = ref[k, :, lanes].astype(F32)
            for z in range(slab):
                rows = turn_ref[h, pl.ds(z, images, stride=pitch), :].astype(BF16)
                for k in range(0, b_out.shape[0], 2 * slab):
                    b_out[pl.ds(start + z + k, 1), :, lanes] = rows[None]
    mine, got = m_ref[...].astype(F32), m_got_ref[...].astype(F32)
    both = [jnp.where(first, mine, got), jnp.where(first, got, mine)]
    m_out[...] = jnp.concatenate(both, axis=2).astype(BF16)


def write_tables(pos, taby_ref, tabz_ref, w_ref, fz_ref):
    per, own = pos.shape[0] // 2, pos.shape[1] // lax.axis_size("frame")
    half = own // 2
    first_half = in_pair()[1] == 0
    frames = pos.shape[1] // 2

    def column(row, u):
        t = u // half * own + u % half
        rows = slice(row, row + per)
        return jnp.where(first_half, pos[rows, t : t + 1], pos[rows, t + half : t + half + 1])

    at_y = lax.broadcasted_iota(jnp.int32, (per, taby_ref.shape[0]), 1).astype(F32)
    at_z = lax.broadcasted_iota(jnp.int32, (per, tabz_ref.shape[0]), 1).astype(F32)
    group = max(1, 128 // per)
    for g in range(0, frames, group):
        hot_y, hot_z = (
            jnp.concatenate(
                [
                    jnp.where(iota == column(first, t), 1.0, 0.0)
                    for t in range(g, g + group)
                ],
                axis=0,
            ).astype(BF16)
            for iota, first in ((at_y, 0), (at_z, per))
        )
        rows = slice(g * per, (g + group) * per)
        w_ref[rows, :] = nn(hot_y, taby_ref[...]).astype(BF16)
        fz_ref[rows, :] = nn(hot_z, tabz_ref[...]).astype(BF16)


def samples_step(x_ref, frames, per):
    return x_ref.shape[1] // (2 * per)


def predict_kernel(own, frames, slab, *refs):
    sent_ref, got_ref, v_ref, taby_ref, tabz_ref, coil_ref, b_ref, m_ref, kd_ref = refs[:9]
    pred_ref, w_ref, fz_ref, x_ref, i_ref = refs[9:]
    steps = frames
    width = b_ref.shape[2]
    rows = m_ref.shape[1]
    pad = fz_ref.shape[1] // 2
    per = w_ref.shape[0] // frames
    coils = rows // slab
    halves = width // LANES
    pitch = 2 * steps + PITCH
    stride = samples_step(x_ref, frames, per)

    pos, others = arrived(sent_ref, got_ref)
    write_tables(pos[: 2 * per, : 2 * frames], taby_ref, tabz_ref, w_ref, fz_ref)
    v = factor_matrix(*half_factors(v_ref, others, in_pair()[1]))
    for z in range(slab):
        image = nn(v, b_ref[z])
        for h in range(halves):
            i_ref[h, z * pitch : z * pitch + 2 * steps, :] = image[:, h * LANES : (h + 1) * LANES]

    m_re = m_ref[0].reshape(coils, slab, width)
    m_im = m_ref[1].reshape(coils, slab, width)

    def frame(step, carry):
        t = frame_of(step, own)
        i_re, i_im = (
            jnp.concatenate(
                [i_ref[h, pl.ds(at, slab, stride=pitch), :] for h in range(halves)], axis=1
            ).astype(BF16)[None]
            for at in (step, steps + step)
        )
        p_re = (m_re * i_re - m_im * i_im).reshape(rows, width)
        p_im = (m_re * i_im + m_im * i_re).reshape(rows, width)
        at = pl.ds(pl.multiple_of(t * per, TILE), per)
        lhs = adjoint_pair(w_ref[at, :])
        y = nt(lhs[:, :width], p_re) + nt(lhs[:, width:], p_im)
        y_re, y_im = y[:per], y[per:]
        f = fz_ref[at, :].astype(F32)
        f_cos, f_sin = f[:, :rows], f[:, pad : pad + rows]
        x = jnp.concatenate([y_re * f_cos + y_im * f_sin, y_im * f_cos - y_re * f_sin], axis=0)
        for h in range(x_ref.shape[0]):
            lanes = min(LANES, rows - h * LANES)
            x_ref[h, pl.ds(t, 2 * per, stride=stride), :lanes] = x[:, h * LANES : h * LANES + lanes]
        return carry

    lax.fori_loop(0, steps, frame, 0, unroll=math.gcd(steps, 16))
    blocks = max(1, min(per, 512 // frames))

    def summed(part, first):
        at = [(part * per + first + k) * stride for k in range(blocks)]
        halves_of = [
            jnp.concatenate([x_ref[h, a : a + frames, :] for a in at], axis=0)
            for h in range(x_ref.shape[0])
        ]
        x = jnp.concatenate(halves_of, axis=1)[:, :rows].astype(BF16)
        return nt(coil_ref[part, :, :rows], x)

    for first in range(0, per, blocks):
        pred_ref[:, first * frames : (first + blocks) * frames] = (
            summed(0, first) + summed(1, first)
        ).astype(BF16)
    size = kd_ref.shape[1]
    at = pl.ds(pl.multiple_of(in_pair()[0] * size, LANES), size)
    pred_ref[:, at] = (pred_ref[:, at].astype(F32) - kd_ref[...].astype(F32)).astype(BF16)


def gradient_kernel(own, frames, slab, real, scale, n_r, *refs):
    r_refs, refs = refs[:n_r], refs[n_r:]
    b_ref, m_ref, w_ref, fz_ref, coil_ref, fg_ref, mine_ref, theirs_ref, r_ref, g_ref = refs
    steps = frames
    width = b_ref.shape[2]
    rank = b_ref.shape[1] // 2
    rows = m_ref.shape[1]
    pad = fz_ref.shape[1] // 2
    per = w_ref.shape[0] // frames
    coils = rows // slab
    halves = width // LANES
    pitch = 2 * steps + PITCH
    stride = samples_step(r_ref, frames, per)

    resid = total(r_refs).astype(BF16)
    blocks = max(1, min(per, 512 // frames))
    for part in range(2):
        for first in range(0, per, blocks):
            r = tn(resid[:, first * frames : (first + blocks) * frames], coil_ref[part])
            for k in range(blocks):
                at = (part * per + first + k) * stride
                for h in range(r_ref.shape[0]):
                    r_ref[h, at : at + frames, :] = r[
                        k * frames : (k + 1) * frames, h * LANES : (h + 1) * LANES
                    ]

    m_re = m_ref[0].reshape(coils, slab, width)
    m_im = m_ref[1].reshape(coils, slab, width)

    def frame(step, carry):
        t = frame_of(step, own)
        at = pl.ds(pl.multiple_of(t * per, TILE), per)
        rhs = adjoint_pair(w_ref[at, :])
        f = fz_ref[at, :].astype(F32)
        f_cos, f_sin = f[:, :pad], f[:, pad:]
        r = jnp.concatenate(
            [r_ref[h, pl.ds(t, 2 * per, stride=stride), :] for h in range(r_ref.shape[0])], axis=1
        )
        r_re, r_im = r[:per], r[per:]
        q = jnp.concatenate([r_re * f_cos - r_im * f_sin, r_im * f_cos + r_re * f_sin], axis=0)
        u = tn(q[:, :rows].astype(BF16), rhs).astype(BF16)
        u_re = u[:, :width].reshape(coils, slab, width)
        u_im = u[:, width:].reshape(coils, slab, width)
        g_re = tree(m_re * u_re + m_im * u_im)
        g_im = tree(m_re * u_im - m_im * u_re)
        for h in range(halves):
            lanes = slice(h * LANES, (h + 1) * LANES)
            g_ref[h, pl.ds(step, slab, stride=pitch), :] = g_re[:, lanes]
            g_ref[h, pl.ds(steps + step, slab, stride=pitch), :] = g_im[:, lanes]
        return carry

    lax.fori_loop(0, steps, frame, 0, unroll=math.gcd(steps, 16))
    acc = jnp.zeros((2 * steps, 2 * rank), F32)
    for ref, place in ((mine_ref, in_pair()[1]), (theirs_ref, 1 - in_pair()[1])):
        for n in range(ref.shape[0]):
            z = n // real * 2 * real + place * real + n % real
            at = pl.ds(pl.multiple_of(z * pitch, 8), 2 * steps)
            g = jnp.concatenate([g_ref[h, at, :] for h in range(halves)], axis=1).astype(BF16)
            ref[n] = g
            acc = acc + nt(g, b_ref[pl.ds(z, 1)][0])
    top, bottom = acc[:steps], acc[steps:]
    fg = jnp.concatenate(
        [top[:, :rank] + bottom[:, rank:], bottom[:, :rank] - top[:, rank:]], axis=1
    )
    fg = (fg * scale).astype(fg_ref.dtype)
    n_cuts, n_frame, n_rows, n_lanes = fg_ref.shape
    for d in range(n_frame):
        piece = jnp.concatenate(
            [
                fg[d * own + k : d * own + k + n_rows].astype(F32)
                for k in range(0, own, n_rows)
            ],
            axis=1,
        ).astype(fg_ref.dtype)
        target = lax.axis_index("frame") ^ d
        for c in range(n_cuts):
            fg_ref[c, pl.ds(target, 1)] = piece[None]


def basis_kernel(sent_ref, got_ref, v_ref, g_ref, g_got_ref, grad_ref):
    _, others = arrived(sent_ref, got_ref)
    place = in_pair()[1]
    pairs_of = [
        (factor_matrix(*half_factors(v_ref, others, place)), g_ref),
        (factor_matrix(*half_factors(v_ref, others, 1 - place)), g_got_ref),
    ]
    halves = g_ref.shape[2] // LANES
    slab = grad_ref.shape[0] // (2 * v_ref.shape[2] * halves)
    for z in range(slab):
        grad = functools.reduce(
            jnp.add,
            [tn(v, ref[k]) for v, ref in pairs_of for k in range(z, g_ref.shape[0], slab)],
        )
        for h in range(halves):
            grad_ref[pl.ds(z * halves + h, grad.shape[0], stride=slab * halves), :] = grad[
                :, h * LANES : (h + 1) * LANES
            ]


def stages(size):
    steps, stride = [(1, 2)], 2
    if (size // stride).bit_length() % 2 == 0:
        steps.append((stride, 2))
        stride *= 2
    while stride < size:
        steps.append((stride, 4))
        stride *= 4
    return steps


def swap(value, axis, distance):
    size = lax.axis_size(axis)
    return lax.ppermute(value, axis, [(i, i ^ distance) for i in range(size)])


def shares(value, axis, last=1, skip=0):
    steps = stages(lax.axis_size(axis))[skip:]
    for number, (stride, radix) in enumerate(steps):
        if number + last == len(steps) + 1:
            return value
        terms = [value] + [swap(value, axis, stride * d) for d in range(1, radix)]
        if number + 1 < len(steps):
            value = pairs([term.astype(F32) for term in terms]).astype(value.dtype)
    return terms


def grown(value, rows, lanes):
    return jnp.pad(value, ((0, rows - value.shape[0]), (0, lanes - value.shape[1])))


def collect(positions, v_own, meanwhile):
    n_cuts, n_frame = lax.axis_size("cuts"), lax.axis_size("frame")
    even = lax.axis_index("cuts") % 2 == 0
    stride, radix = stages(n_cuts)[-1]
    near = shares(positions, "cuts", last=2)
    rank = v_own.shape[2]
    rows = max(near.shape[0], math.prod(v_own.shape[:2]))
    lanes = max(near.shape[1], rank)
    v_packet = grown(v_own.reshape(-1, rank).astype(near.dtype), rows, lanes)
    near, v_packet = lax.optimization_barrier((near, v_packet))
    packet = jnp.where(even, grown(near, rows, lanes), v_packet)
    got = []
    for d in range(1, max(radix, n_frame)):
        route = []
        for c in range(n_cuts):
            for f in range(n_frame):
                if c % 2 == 0 and d < radix:
                    route.append((c * n_frame + f, (c ^ stride * d) * n_frame + f))
                if c % 2 == 1 and d < n_frame:
                    route.append((c * n_frame + f, c * n_frame + (f ^ d)))
        got.append(lax.ppermute(packet, ("cuts", "frame"), route))
    staged = meanwhile(packet)
    got, staged = lax.optimization_barrier((got, staged))
    joined = pairs([x.astype(F32) for x in (packet, *got[: radix - 1])]).astype(near.dtype)
    others = jnp.concatenate([x[:, :rank] for x in got[: n_frame - 1]], axis=1)
    lanes = max(lanes, others.shape[1])
    sent = jnp.where(even, grown(joined, rows, lanes), grown(others, rows, lanes))
    return sent, swap(sent, "cuts", 1), staged


def call(kernel, outs, scratch, flops, *operands, limit=0):
    def size(x):
        rows = [-(-x.shape[-2] // TILE) * TILE, -(-x.shape[-1] // LANES) * LANES]
        return math.prod(x.shape[:-2]) * math.prod(rows) * jnp.dtype(x.dtype).itemsize

    nbytes = sum(size(x) for x in operands)
    held = nbytes + sum(size(x) for x in (*outs, *scratch))
    limit = limit or min(56, 10 + held * 5 // (4 * 1024 * 1024))
    return pl.pallas_call(
        kernel,
        out_shape=outs,
        scratch_shapes=scratch,
        compiler_params=pltpu.CompilerParams(vmem_limit_bytes=limit * 1024 * 1024),
        cost_estimate=pl.CostEstimate(flops=flops, bytes_accessed=nbytes, transcendentals=0),
    )(*operands)


def one_position(basis, coil_maps, factors, lines, kdata, scale):
    n_cuts, n_frame = lax.axis_size("cuts"), lax.axis_size("frame")
    cut = lax.axis_index("cuts")
    rank, slab, width = basis.shape[1:]
    coils = coil_maps.shape[1]
    columns = lines.shape[1]
    half = factors.shape[2] // 2
    frames = lines.shape[0] // 2
    per = columns * n_cuts
    samples = frames * per
    depth = slab * n_cuts
    ky_rows = width // n_cuts

    spread = max(1, TILE // (2 * slab))
    tall = spread * 2 * slab
    coil_groups = -(-coils // spread)
    rows = coil_groups * tall
    pad = -(-rows // LANES) * LANES
    coil_rows = -(-2 * coils // 8) * 8

    kind = BF16 if max(width, depth) <= 256 else F32
    turned = lines.T
    mine = jnp.stack([cut * ky_rows + turned // depth, turned % depth])
    owner = lax.broadcasted_iota(jnp.int32, (2 * per, 2 * frames), 0) // columns % n_cuts == cut
    every = jnp.broadcast_to(mine[:, None], (2, n_cuts, columns, 2 * frames))
    placed = jnp.where(owner, every.reshape(2 * per, 2 * frames), 0).astype(kind)
    v_own = factors.transpose(0, 2, 1)
    maps = jnp.pad(coil_maps, ((0, 0), (0, coil_groups * spread - coils), (0, 0), (0, 0)))
    images_in = basis.reshape(2 * rank, slab, width)

    flops = 2 * 2 * per * rows * 2 * width * 8
    halves = width // LANES
    x_shape = jax.ShapeDtypeStruct((pad // LANES, 2 * per * (frames + PITCH), LANES), F32)

    def images(steps):
        return pltpu.VMEM((halves, tall * (2 * steps + PITCH), LANES), F32)

    _, b, m, k = lax.optimization_barrier((placed, images_in, maps, kdata))
    b_got, m_got, k_got = (swap(x, "cuts", 1) for x in (b, m, k))

    def stage(packet):
        tables = call(
            functools.partial(tables_kernel, 2 * slab, coils),
            (
                jax.ShapeDtypeStruct((width, 2 * width), BF16),
                jax.ShapeDtypeStruct((depth, 2 * pad), BF16),
                jax.ShapeDtypeStruct((2, coil_rows, pad), BF16),
            ),
            [],
            1024 * 1024 * 1024,
            b_got,
        )
        turned = call(
            turn_kernel,
            (
                jax.ShapeDtypeStruct((tall, 2 * rank, width), BF16),
                jax.ShapeDtypeStruct((2, maps.shape[1], 2 * slab, width), BF16),
            ),
            [pltpu.VMEM((halves, 2 * rank * (-(-slab // 8) * 8 + PITCH), LANES), F32)],
            1024 * 1024 * 1024,
            packet, images_in, b_got, maps, m_got,
        )
        return tables, turned

    sent, got, ((taby, tabz, coil_of), (b_rows, m_rows)) = collect(placed, v_own, stage)
    m_rows = m_rows.reshape(2, rows, width)
    even = lax.axis_index("cuts") % 2 == 0
    _, mine, k_got = lax.optimization_barrier((sent, kdata, k_got))
    both = jnp.stack([jnp.where(even, mine, k_got), jnp.where(even, k_got, mine)])
    both = both.transpose(1, 4, 0, 3, 2).reshape(2 * coils, 2 * columns, n_frame, 2, half)
    kd = jnp.where(even, both[..., 0, :], both[..., 1, :]).reshape(2 * coils, -1)
    kd = jnp.pad(kd, ((0, coil_rows - 2 * coils), (0, 0)))
    predicted, w, fz = call(
        functools.partial(predict_kernel, half, frames, tall),
        (
            jax.ShapeDtypeStruct((coil_rows, samples), BF16),
            jax.ShapeDtypeStruct((samples, 2 * width), BF16),
            jax.ShapeDtypeStruct((samples, 2 * pad), BF16),
        ),
        [pltpu.VMEM(x_shape.shape, F32), images(frames)],
        flops * frames,
        sent, got, v_own, taby, tabz, coil_of, b_rows, m_rows, kd,
    )
    resid_terms = shares(predicted, "cuts", skip=1)

    fold = max(1, LANES // (2 * rank))
    own_slab = jax.ShapeDtypeStruct((tall // 2, 2 * frames, width), BF16)
    pieces, g, theirs = call(
        functools.partial(gradient_kernel, half, frames, tall, slab, scale, len(resid_terms)),
        (
            jax.ShapeDtypeStruct((n_cuts, n_frame, half // fold, 2 * rank * fold), F32),
            own_slab,
            own_slab,
        ),
        [pltpu.VMEM(x_shape.shape, F32), images(frames)],
        flops * frames,
        *resid_terms, b_rows, m_rows, w, fz, coil_of,
    )
    (grad,) = call(
        basis_kernel,
        (jax.ShapeDtypeStruct((2 * rank * slab * halves, LANES), F32),),
        [],
        2 * 2 * rank * 4 * frames * slab * width * 8,
        sent, got, v_own, g, swap(theirs, "cuts", 1),
    )
    return grad, pieces


def pairs(terms):
    while len(terms) > 1:
        odd = [terms[-1]] if len(terms) % 2 else []
        terms = [a + b for a, b in zip(terms[::2], terms[1::2])] + odd
    return terms[0]


def body(basis, coil_maps, factors, lines, kdata):
    n_cuts, n_frame = lax.axis_size("cuts"), lax.axis_size("frame")
    readout = basis.shape[3]
    rank = basis.shape[1]
    own = factors.shape[2]
    scale = 1.0 / math.sqrt(coil_maps.shape[1] * lines.shape[1] * n_cuts * readout * n_frame)
    grads, fg = [], 0.0
    for x in range(readout):
        grad, term = one_position(
            basis[:, :, :, x], coil_maps[:, :, :, x], factors, lines, kdata[..., x], scale
        )
        grads.append(grad)
        fg = fg + term
    pieces = fg.reshape((n_cuts * n_frame,) + fg.shape[2:])
    arriving = lax.all_to_all(pieces, ("cuts", "frame"), 0, 0, tiled=True)
    arriving, grads = lax.optimization_barrier((arriving, grads))
    grads = [grad.reshape(2, rank, basis.shape[2], -1) for grad in grads]
    basis_grad = grads[0][:, :, :, None] if readout == 1 else jnp.stack(grads, axis=3)
    parts = arriving.astype(F32).reshape((n_cuts // 2, 2, n_frame) + fg.shape[2:])
    summed = jnp.sum(parts, axis=(0, 2))
    folded = summed.reshape(2, summed.shape[1], -1, 2, rank)
    return basis_grad, folded.transpose(3, 4, 0, 2, 1).reshape(2, rank, own)


def solution(mesh):
    placed = (
        P(None, None, "cuts", "frame", None),
        P(None, None, "cuts", "frame", None),
        P(None, None, "frame"),
        P(None, "cuts"),
        P(None, None, "cuts", None, "frame"),
    )
    return jax.shard_map(
        body,
        mesh=mesh,
        in_specs=placed,
        out_specs=(P(None, None, "cuts", "frame", None), P(None, None, "frame")),
        check_vma=False,
    )
```

```python
import functools
import math

import jax
import jax.numpy as jnp
import numpy as np
from jax import lax
from jax.experimental import pallas as pl
from jax.experimental.pallas import tpu as pltpu
from jax.sharding import PartitionSpec as P

F32 = jnp.float32
BF16 = jnp.bfloat16
LANES = 128
TILE = 16
PITCH = 8


def trig(product, size):
    angle = (product % size).astype(F32) * (2.0 * math.pi / size)
    return jnp.cos(angle), jnp.sin(angle)


def write_dft(out_ref, size, index):
    lanes = index.shape[1]
    fine = lax.broadcasted_iota(jnp.int32, (TILE, lanes), 0)
    b_cos, b_sin = trig(fine * index[:TILE], size)
    coarse = lax.broadcasted_iota(jnp.int32, (size // TILE, lanes), 0) * TILE
    a_cos, a_sin = trig(coarse * index[: size // TILE], size)
    factor = 1.0 / math.sqrt(size)
    a_cos, a_sin = a_cos * factor, a_sin * factor
    for a in range(size // TILE):
        rows = slice(a * TILE, (a + 1) * TILE)
        p_cos, p_sin = a_cos[a : a + 1], a_sin[a : a + 1]
        out_ref[rows, :lanes] = (p_cos * b_cos - p_sin * b_sin).astype(BF16)
        out_ref[rows, lanes:] = (p_sin * b_cos + p_cos * b_sin).astype(BF16)


def nn(a, b):
    return lax.dot_general(a, b, (((1,), (0,)), ((), ())), preferred_element_type=F32)


def nt(a, b):
    return lax.dot_general(a, b, (((1,), (1,)), ((), ())), preferred_element_type=F32)


def tn(a, b):
    return lax.dot_general(a, b, (((0,), (0,)), ((), ())), preferred_element_type=F32)


def total(refs):
    terms = [ref[...].astype(F32) for ref in refs]
    while len(terms) > 1:
        odd = [terms[-1]] if len(terms) % 2 else []
        terms = [a + b for a, b in zip(terms[::2], terms[1::2])] + odd
    return terms[0]


def arrived(sent_ref, got_ref):
    sent, got = sent_ref[...].astype(F32), got_ref[...].astype(F32)
    even = in_pair()[1] == 0
    return jnp.where(even, sent, got), jnp.where(even, got, sent)


def factor_matrix(v_re, v_im):
    top = jnp.concatenate([v_re, -v_im], axis=1)
    bottom = jnp.concatenate([v_im, v_re], axis=1)
    return jnp.concatenate([top, bottom], axis=0).astype(BF16)


def half_factors(v_ref, others, place):
    _, own, rank = v_ref.shape
    half = own // 2
    v = v_ref[...].astype(F32)
    blocks = [(v[0], v[1])]
    for a in range(0, rank * (lax.axis_size("frame") - 1), rank):
        blocks.append((others[:own, a : a + rank], others[own : 2 * own, a : a + rank]))
    return [
        jnp.concatenate(
            [jnp.where(place == 0, b[p][:half], b[p][half:]) for b in blocks], axis=0
        )
        for p in range(2)
    ]


def adjoint_pair(w):
    half = w.shape[1] // 2
    return jnp.concatenate([w, jnp.concatenate([-w[:, half:], w[:, :half]], axis=1)], axis=0)


def tree(value):
    terms = [value[i] for i in range(value.shape[0])]
    while len(terms) > 1:
        odd = [terms[-1]] if len(terms) % 2 else []
        terms = [a + b for a, b in zip(terms[::2], terms[1::2])] + odd
    return terms[0].astype(F32)


def in_pair():
    return lax.axis_index("cuts") // 2, lax.axis_index("cuts") % 2


def frame_of(step, own):
    return ((step // own) ^ lax.axis_index("frame")) * own + step % own


def tables_kernel(real, coils, after_ref, taby_ref, tabz_ref, coil_ref):
    del after_ref
    width, depth, pad = taby_ref.shape[0], tabz_ref.shape[0], coil_ref.shape[2]
    write_dft(taby_ref, width, lax.broadcasted_iota(jnp.int32, (max(TILE, width // TILE), width), 1))
    slice_of = lax.broadcasted_iota(jnp.int32, (max(TILE, depth // TILE), pad), 1) % real
    write_dft(tabz_ref, depth, slice_of + in_pair()[0] * real)
    column = lax.broadcasted_iota(jnp.int32, coil_ref.shape[1:], 1) // real
    row = lax.broadcasted_iota(jnp.int32, coil_ref.shape[1:], 0)
    for part in range(2):
        place = (row == column + part * coils) & (column < coils)
        coil_ref[part] = place.astype(F32).astype(BF16)


def turn_kernel(after_ref, b_ref, b_got_ref, m_ref, m_got_ref, b_out, m_out, turn_ref):
    del after_ref
    images, slab, width = b_ref.shape
    pitch = turn_ref.shape[1] // images
    first = in_pair()[1] == 0
    for n, ref in enumerate((b_ref, b_got_ref)):
        start = jnp.where(first, n, 1 - n) * slab
        for h in range(width // LANES):
            lanes = slice(h * LANES, (h + 1) * LANES)
            for k in range(images):
                turn_ref[h, k * pitch : k * pitch + slab, :] = ref[k, :, lanes].astype(F32)
            for z in range(slab):
                rows = turn_ref[h, pl.ds(z, images, stride=pitch), :].astype(BF16)
                for k in range(0, b_out.shape[0], 2 * slab):
                    b_out[pl.ds(start + z + k, 1), :, lanes] = rows[None]
    mine, got = m_ref[...].astype(F32), m_got_ref[...].astype(F32)
    both = [jnp.where(first, mine, got), jnp.where(first, got, mine)]
    m_out[...] = jnp.concatenate(both, axis=2).astype(BF16)


def write_tables(pos, taby_ref, tabz_ref, w_ref, fz_ref):
    per, own = pos.shape[0] // 2, pos.shape[1] // lax.axis_size("frame")
    half = own // 2
    first_half = in_pair()[1] == 0
    frames = pos.shape[1] // 2

    def column(row, u):
        t = u // half * own + u % half
        rows = slice(row, row + per)
        return jnp.where(first_half, pos[rows, t : t + 1], pos[rows, t + half : t + half + 1])

    at_y = lax.broadcasted_iota(jnp.int32, (per, taby_ref.shape[0]), 1).astype(F32)
    at_z = lax.broadcasted_iota(jnp.int32, (per, tabz_ref.shape[0]), 1).astype(F32)
    group = max(1, 128 // per)
    for g in range(0, frames, group):
        hot_y, hot_z = (
            jnp.concatenate(
                [
                    jnp.where(iota == column(first, t), 1.0, 0.0)
                    for t in range(g, g + group)
                ],
                axis=0,
            ).astype(BF16)
            for iota, first in ((at_y, 0), (at_z, per))
        )
        rows = slice(g * per, (g + group) * per)
        w_ref[rows, :] = nn(hot_y, taby_ref[...]).astype(BF16)
        fz_ref[rows, :] = nn(hot_z, tabz_ref[...]).astype(BF16)


def samples_step(x_ref, frames, per):
    return x_ref.shape[1] // (2 * per)


def predict_kernel(own, frames, slab, *refs):
    sent_ref, got_ref, v_ref, taby_ref, tabz_ref, coil_ref, b_ref, m_ref, kd_ref = refs[:9]
    pred_ref, w_ref, fz_ref, x_ref, i_ref = refs[9:]
    steps = frames
    width = b_ref.shape[2]
    rows = m_ref.shape[1]
    pad = fz_ref.shape[1] // 2
    per = w_ref.shape[0] // frames
    coils = rows // slab
    halves = width // LANES
    pitch = 2 * steps + PITCH
    stride = samples_step(x_ref, frames, per)

    pos, others = arrived(sent_ref, got_ref)
    write_tables(pos[: 2 * per, : 2 * frames], taby_ref, tabz_ref, w_ref, fz_ref)
    v = factor_matrix(*half_factors(v_ref, others, in_pair()[1]))
    for z in range(slab):
        image = nn(v, b_ref[z])
        for h in range(halves):
            i_ref[h, z * pitch : z * pitch + 2 * steps, :] = image[:, h * LANES : (h + 1) * LANES]

    m_re = m_ref[0].reshape(coils, slab, width)
    m_im = m_ref[1].reshape(coils, slab, width)

    def frame(step, carry):
        t = frame_of(step, own)
        i_re, i_im = (
            jnp.concatenate(
                [i_ref[h, pl.ds(at, slab, stride=pitch), :] for h in range(halves)], axis=1
            ).astype(BF16)[None]
            for at in (step, steps + step)
        )
        p_re = (m_re * i_re - m_im * i_im).reshape(rows, width)
        p_im = (m_re * i_im + m_im * i_re).reshape(rows, width)
        at = pl.ds(pl.multiple_of(t * per, TILE), per)
        lhs = adjoint_pair(w_ref[at, :])
        y = jnp.concatenate([(nt(p_re[k:k+128], lhs[:, :width]) + nt(p_im[k:k+128], lhs[:, width:])).T for k in range(0,rows,128)],axis=1)
        y_re, y_im = y[:per], y[per:]
        f = fz_ref[at, :].astype(F32)
        f_cos, f_sin = f[:, :rows], f[:, pad : pad + rows]
        x = jnp.concatenate([y_re * f_cos + y_im * f_sin, y_im * f_cos - y_re * f_sin], axis=0)
        for h in range(x_ref.shape[0]):
            lanes = min(LANES, rows - h * LANES)
            x_ref[h, pl.ds(t, 2 * per, stride=stride), :lanes] = x[:, h * LANES : h * LANES + lanes]
        return carry

    lax.fori_loop(0, steps, frame, 0, unroll=math.gcd(steps, 16))
    blocks = max(1, min(per, 512 // frames))

    def summed(part, first):
        at = [(part * per + first + k) * stride for k in range(blocks)]
        halves_of = [
            jnp.concatenate([x_ref[h, a : a + frames, :] for a in at], axis=0)
            for h in range(x_ref.shape[0])
        ]
        x = jnp.concatenate(halves_of, axis=1)[:, :rows].astype(BF16)
        return nt(coil_ref[part, :, :rows], x)

    for first in range(0, per, blocks):
        pred_ref[:, first * frames : (first + blocks) * frames] = (
            summed(0, first) + summed(1, first)
        ).astype(BF16)
    size = kd_ref.shape[1]
    at = pl.ds(pl.multiple_of(in_pair()[0] * size, LANES), size)
    pred_ref[:, at] = (pred_ref[:, at].astype(F32) - kd_ref[...].astype(F32)).astype(BF16)


def gradient_kernel(own, frames, slab, real, scale, n_r, *refs):
    r_refs, refs = refs[:n_r], refs[n_r:]
    b_ref, m_ref, w_ref, fz_ref, coil_ref, fg_ref, mine_ref, theirs_ref, r_ref, g_ref = refs
    steps = frames
    width = b_ref.shape[2]
    rank = b_ref.shape[1] // 2
    rows = m_ref.shape[1]
    pad = fz_ref.shape[1] // 2
    per = w_ref.shape[0] // frames
    coils = rows // slab
    halves = width // LANES
    pitch = 2 * steps + PITCH
    stride = samples_step(r_ref, frames, per)

    resid = total(r_refs).astype(BF16)
    blocks = max(1, min(per, 512 // frames))
    for part in range(2):
        for first in range(0, per, blocks):
            r = tn(resid[:, first * frames : (first + blocks) * frames], coil_ref[part])
            for k in range(blocks):
                at = (part * per + first + k) * stride
                for h in range(r_ref.shape[0]):
                    r_ref[h, at : at + frames, :] = r[
                        k * frames : (k + 1) * frames, h * LANES : (h + 1) * LANES
                    ]

    m_re = m_ref[0].reshape(coils, slab, width)
    m_im = m_ref[1].reshape(coils, slab, width)

    def frame(step, carry):
        t = frame_of(step, own)
        at = pl.ds(pl.multiple_of(t * per, TILE), per)
        rhs = adjoint_pair(w_ref[at, :])
        f = fz_ref[at, :].astype(F32)
        f_cos, f_sin = f[:, :pad], f[:, pad:]
        r = jnp.concatenate(
            [r_ref[h, pl.ds(t, 2 * per, stride=stride), :] for h in range(r_ref.shape[0])], axis=1
        )
        r_re, r_im = r[:per], r[per:]
        q = jnp.concatenate([r_re * f_cos - r_im * f_sin, r_im * f_cos + r_re * f_sin], axis=0)
        u = tn(q[:, :rows].astype(BF16), rhs).astype(BF16)
        u_re = u[:, :width].reshape(coils, slab, width)
        u_im = u[:, width:].reshape(coils, slab, width)
        g_re = tree(m_re * u_re + m_im * u_im)
        g_im = tree(m_re * u_im - m_im * u_re)
        for h in range(halves):
            lanes = slice(h * LANES, (h + 1) * LANES)
            g_ref[h, pl.ds(step, slab, stride=pitch), :] = g_re[:, lanes]
            g_ref[h, pl.ds(steps + step, slab, stride=pitch), :] = g_im[:, lanes]
        return carry

    lax.fori_loop(0, steps, frame, 0, unroll=math.gcd(steps, 16))
    acc = jnp.zeros((2 * steps, 2 * rank), F32)
    for ref, place in ((mine_ref, in_pair()[1]), (theirs_ref, 1 - in_pair()[1])):
        for n in range(ref.shape[0]):
            z = n // real * 2 * real + place * real + n % real
            at = pl.ds(pl.multiple_of(z * pitch, 8), 2 * steps)
            g = jnp.concatenate([g_ref[h, at, :] for h in range(halves)], axis=1).astype(BF16)
            ref[n] = g
            acc = acc + nt(g, b_ref[pl.ds(z, 1)][0])
    top, bottom = acc[:steps], acc[steps:]
    fg = jnp.concatenate(
        [top[:, :rank] + bottom[:, rank:], bottom[:, :rank] - top[:, rank:]], axis=1
    )
    fg = (fg * scale).astype(fg_ref.dtype)
    n_cuts, n_frame, n_rows, n_lanes = fg_ref.shape
    for d in range(n_frame):
        piece = jnp.concatenate(
            [
                fg[d * own + k : d * own + k + n_rows].astype(F32)
                for k in range(0, own, n_rows)
            ],
            axis=1,
        ).astype(fg_ref.dtype)
        target = lax.axis_index("frame") ^ d
        for c in range(n_cuts):
            fg_ref[c, pl.ds(target, 1)] = piece[None]


def basis_kernel(sent_ref, got_ref, v_ref, g_ref, g_got_ref, grad_ref):
    _, others = arrived(sent_ref, got_ref)
    place = in_pair()[1]
    pairs_of = [
        (factor_matrix(*half_factors(v_ref, others, place)), g_ref),
        (factor_matrix(*half_factors(v_ref, others, 1 - place)), g_got_ref),
    ]
    halves = g_ref.shape[2] // LANES
    slab = grad_ref.shape[0] // (2 * v_ref.shape[2] * halves)
    for z in range(slab):
        grad = functools.reduce(
            jnp.add,
            [tn(v, ref[k]) for v, ref in pairs_of for k in range(z, g_ref.shape[0], slab)],
        )
        for h in range(halves):
            grad_ref[pl.ds(z * halves + h, grad.shape[0], stride=slab * halves), :] = grad[
                :, h * LANES : (h + 1) * LANES
            ]


def stages(size):
    steps, stride = [(1, 2)], 2
    if (size // stride).bit_length() % 2 == 0:
        steps.append((stride, 2))
        stride *= 2
    while stride < size:
        steps.append((stride, 4))
        stride *= 4
    return steps


def swap(value, axis, distance):
    size = lax.axis_size(axis)
    return lax.ppermute(value, axis, [(i, i ^ distance) for i in range(size)])


def shares(value, axis, last=1, skip=0):
    steps = stages(lax.axis_size(axis))[skip:]
    for number, (stride, radix) in enumerate(steps):
        if number + last == len(steps) + 1:
            return value
        terms = [value] + [swap(value, axis, stride * d) for d in range(1, radix)]
        if number + 1 < len(steps):
            value = pairs([term.astype(F32) for term in terms]).astype(value.dtype)
    return terms


def grown(value, rows, lanes):
    return jnp.pad(value, ((0, rows - value.shape[0]), (0, lanes - value.shape[1])))


def collect(positions, v_own, meanwhile):
    n_cuts, n_frame = lax.axis_size("cuts"), lax.axis_size("frame")
    even = lax.axis_index("cuts") % 2 == 0
    stride, radix = stages(n_cuts)[-1]
    near = shares(positions, "cuts", last=2)
    rank = v_own.shape[2]
    rows = max(near.shape[0], math.prod(v_own.shape[:2]))
    lanes = max(near.shape[1], rank)
    v_packet = grown(v_own.reshape(-1, rank).astype(near.dtype), rows, lanes)
    near, v_packet = lax.optimization_barrier((near, v_packet))
    packet = jnp.where(even, grown(near, rows, lanes), v_packet)
    got = []
    for d in range(1, max(radix, n_frame)):
        route = []
        for c in range(n_cuts):
            for f in range(n_frame):
                if c % 2 == 0 and d < radix:
                    route.append((c * n_frame + f, (c ^ stride * d) * n_frame + f))
                if c % 2 == 1 and d < n_frame:
                    route.append((c * n_frame + f, c * n_frame + (f ^ d)))
        got.append(lax.ppermute(packet, ("cuts", "frame"), route))
    staged = meanwhile(packet)
    got, staged = lax.optimization_barrier((got, staged))
    joined = pairs([x.astype(F32) for x in (packet, *got[: radix - 1])]).astype(near.dtype)
    others = jnp.concatenate([x[:, :rank] for x in got[: n_frame - 1]], axis=1)
    lanes = max(lanes, others.shape[1])
    sent = jnp.where(even, grown(joined, rows, lanes), grown(others, rows, lanes))
    return sent, swap(sent, "cuts", 1), staged


def call(kernel, outs, scratch, flops, *operands, limit=0):
    def size(x):
        rows = [-(-x.shape[-2] // TILE) * TILE, -(-x.shape[-1] // LANES) * LANES]
        return math.prod(x.shape[:-2]) * math.prod(rows) * jnp.dtype(x.dtype).itemsize

    nbytes = sum(size(x) for x in operands)
    held = nbytes + sum(size(x) for x in (*outs, *scratch))
    limit = limit or min(56, 10 + held * 5 // (4 * 1024 * 1024))
    return pl.pallas_call(
        kernel,
        out_shape=outs,
        scratch_shapes=scratch,
        compiler_params=pltpu.CompilerParams(vmem_limit_bytes=limit * 1024 * 1024),
        cost_estimate=pl.CostEstimate(flops=flops, bytes_accessed=nbytes, transcendentals=0),
    )(*operands)


def one_position(basis, coil_maps, factors, lines, kdata, scale):
    n_cuts, n_frame = lax.axis_size("cuts"), lax.axis_size("frame")
    cut = lax.axis_index("cuts")
    rank, slab, width = basis.shape[1:]
    coils = coil_maps.shape[1]
    columns = lines.shape[1]
    half = factors.shape[2] // 2
    frames = lines.shape[0] // 2
    per = columns * n_cuts
    samples = frames * per
    depth = slab * n_cuts
    ky_rows = width // n_cuts

    spread = max(1, TILE // (2 * slab))
    tall = spread * 2 * slab
    coil_groups = -(-coils // spread)
    rows = coil_groups * tall
    pad = -(-rows // LANES) * LANES
    coil_rows = -(-2 * coils // 8) * 8

    kind = BF16 if max(width, depth) <= 256 else F32
    turned = lines.T
    mine = jnp.stack([cut * ky_rows + turned // depth, turned % depth])
    owner = lax.broadcasted_iota(jnp.int32, (2 * per, 2 * frames), 0) // columns % n_cuts == cut
    every = jnp.broadcast_to(mine[:, None], (2, n_cuts, columns, 2 * frames))
    placed = jnp.where(owner, every.reshape(2 * per, 2 * frames), 0).astype(kind)
    v_own = factors.transpose(0, 2, 1)
    maps = jnp.pad(coil_maps, ((0, 0), (0, coil_groups * spread - coils), (0, 0), (0, 0)))
    images_in = basis.reshape(2 * rank, slab, width)

    flops = 2 * 2 * per * rows * 2 * width * 8
    halves = width // LANES
    x_shape = jax.ShapeDtypeStruct((pad // LANES, 2 * per * (frames + PITCH), LANES), F32)

    def images(steps):
        return pltpu.VMEM((halves, tall * (2 * steps + PITCH), LANES), F32)

    _, b, m, k = lax.optimization_barrier((placed, images_in, maps, kdata))
    b_got, m_got, k_got = (swap(x, "cuts", 1) for x in (b, m, k))

    def stage(packet):
        tables = call(
            functools.partial(tables_kernel, 2 * slab, coils),
            (
                jax.ShapeDtypeStruct((width, 2 * width), BF16),
                jax.ShapeDtypeStruct((depth, 2 * pad), BF16),
                jax.ShapeDtypeStruct((2, coil_rows, pad), BF16),
            ),
            [],
            1024 * 1024 * 1024,
            b_got,
        )
        turned = call(
            turn_kernel,
            (
                jax.ShapeDtypeStruct((tall, 2 * rank, width), BF16),
                jax.ShapeDtypeStruct((2, maps.shape[1], 2 * slab, width), BF16),
            ),
            [pltpu.VMEM((halves, 2 * rank * (-(-slab // 8) * 8 + PITCH), LANES), F32)],
            1024 * 1024 * 1024,
            packet, images_in, b_got, maps, m_got,
        )
        return tables, turned

    sent, got, ((taby, tabz, coil_of), (b_rows, m_rows)) = collect(placed, v_own, stage)
    m_rows = m_rows.reshape(2, rows, width)
    even = lax.axis_index("cuts") % 2 == 0
    _, mine, k_got = lax.optimization_barrier((sent, kdata, k_got))
    both = jnp.stack([jnp.where(even, mine, k_got), jnp.where(even, k_got, mine)])
    both = both.transpose(1, 4, 0, 3, 2).reshape(2 * coils, 2 * columns, n_frame, 2, half)
    kd = jnp.where(even, both[..., 0, :], both[..., 1, :]).reshape(2 * coils, -1)
    kd = jnp.pad(kd, ((0, coil_rows - 2 * coils), (0, 0)))
    predicted, w, fz = call(
        functools.partial(predict_kernel, half, frames, tall),
        (
            jax.ShapeDtypeStruct((coil_rows, samples), BF16),
            jax.ShapeDtypeStruct((samples, 2 * width), BF16),
            jax.ShapeDtypeStruct((samples, 2 * pad), BF16),
        ),
        [pltpu.VMEM(x_shape.shape, F32), images(frames)],
        flops * frames,
        sent, got, v_own, taby, tabz, coil_of, b_rows, m_rows, kd,
    )
    resid_terms = shares(predicted, "cuts", skip=1)

    fold = max(1, LANES // (2 * rank))
    own_slab = jax.ShapeDtypeStruct((tall // 2, 2 * frames, width), BF16)
    pieces, g, theirs = call(
        functools.partial(gradient_kernel, half, frames, tall, slab, scale, len(resid_terms)),
        (
            jax.ShapeDtypeStruct((n_cuts, n_frame, half // fold, 2 * rank * fold), F32),
            own_slab,
            own_slab,
        ),
        [pltpu.VMEM(x_shape.shape, F32), images(frames)],
        flops * frames,
        *resid_terms, b_rows, m_rows, w, fz, coil_of,
    )
    (grad,) = call(
        basis_kernel,
        (jax.ShapeDtypeStruct((2 * rank * slab * halves, LANES), F32),),
        [],
        2 * 2 * rank * 4 * frames * slab * width * 8,
        sent, got, v_own, g, swap(theirs, "cuts", 1),
    )
    return grad, pieces


def pairs(terms):
    while len(terms) > 1:
        odd = [terms[-1]] if len(terms) % 2 else []
        terms = [a + b for a, b in zip(terms[::2], terms[1::2])] + odd
    return terms[0]


def body(basis, coil_maps, factors, lines, kdata):
    n_cuts, n_frame = lax.axis_size("cuts"), lax.axis_size("frame")
    readout = basis.shape[3]
    rank = basis.shape[1]
    own = factors.shape[2]
    scale = 1.0 / math.sqrt(coil_maps.shape[1] * lines.shape[1] * n_cuts * readout * n_frame)
    grads, fg = [], 0.0
    for x in range(readout):
        grad, term = one_position(
            basis[:, :, :, x], coil_maps[:, :, :, x], factors, lines, kdata[..., x], scale
        )
        grads.append(grad)
        fg = fg + term
    pieces = fg.reshape((n_cuts * n_frame,) + fg.shape[2:])
    arriving = lax.all_to_all(pieces, ("cuts", "frame"), 0, 0, tiled=True)
    arriving, grads = lax.optimization_barrier((arriving, grads))
    grads = [grad.reshape(2, rank, basis.shape[2], -1) for grad in grads]
    basis_grad = grads[0][:, :, :, None] if readout == 1 else jnp.stack(grads, axis=3)
    parts = arriving.astype(F32).reshape((n_cuts // 2, 2, n_frame) + fg.shape[2:])
    summed = jnp.sum(parts, axis=(0, 2))
    folded = summed.reshape(2, summed.shape[1], -1, 2, rank)
    return basis_grad, folded.transpose(3, 4, 0, 2, 1).reshape(2, rank, own)


def solution(mesh):
    placed = (
        P(None, None, "cuts", "frame", None),
        P(None, None, "cuts", "frame", None),
        P(None, None, "frame"),
        P(None, "cuts"),
        P(None, None, "cuts", None, "frame"),
    )
    return jax.shard_map(
        body,
        mesh=mesh,
        in_specs=placed,
        out_specs=(P(None, None, "cuts", "frame", None), P(None, None, "frame")),
        check_vma=False,
    )
```

```python
import functools
import math

import jax
import jax.numpy as jnp
import numpy as np
from jax import lax
from jax.experimental import pallas as pl
from jax.experimental.pallas import tpu as pltpu
from jax.sharding import PartitionSpec as P

F32 = jnp.float32
BF16 = jnp.bfloat16
LANES = 128
TILE = 16
PITCH = 8


def trig(product, size):
    angle = (product % size).astype(F32) * (2.0 * math.pi / size)
    return jnp.cos(angle), jnp.sin(angle)


def write_dft(out_ref, size, index):
    lanes = index.shape[1]
    fine = lax.broadcasted_iota(jnp.int32, (TILE, lanes), 0)
    b_cos, b_sin = trig(fine * index[:TILE], size)
    coarse = lax.broadcasted_iota(jnp.int32, (size // TILE, lanes), 0) * TILE
    a_cos, a_sin = trig(coarse * index[: size // TILE], size)
    factor = 1.0 / math.sqrt(size)
    a_cos, a_sin = a_cos * factor, a_sin * factor
    for a in range(size // TILE):
        rows = slice(a * TILE, (a + 1) * TILE)
        p_cos, p_sin = a_cos[a : a + 1], a_sin[a : a + 1]
        out_ref[rows, :lanes] = (p_cos * b_cos - p_sin * b_sin).astype(BF16)
        out_ref[rows, lanes:] = (p_sin * b_cos + p_cos * b_sin).astype(BF16)


def nn(a, b):
    return lax.dot_general(a, b, (((1,), (0,)), ((), ())), preferred_element_type=F32)


def nt(a, b):
    return lax.dot_general(a, b, (((1,), (1,)), ((), ())), preferred_element_type=F32)


def tn(a, b):
    return lax.dot_general(a, b, (((0,), (0,)), ((), ())), preferred_element_type=F32)


def total(refs):
    terms = [ref[...].astype(F32) for ref in refs]
    while len(terms) > 1:
        odd = [terms[-1]] if len(terms) % 2 else []
        terms = [a + b for a, b in zip(terms[::2], terms[1::2])] + odd
    return terms[0]


def arrived(sent_ref, got_ref):
    sent, got = sent_ref[...].astype(F32), got_ref[...].astype(F32)
    even = in_pair()[1] == 0
    return jnp.where(even, sent, got), jnp.where(even, got, sent)


def factor_matrix(v_re, v_im):
    top = jnp.concatenate([v_re, -v_im], axis=1)
    bottom = jnp.concatenate([v_im, v_re], axis=1)
    return jnp.concatenate([top, bottom], axis=0).astype(BF16)


def half_factors(v_ref, others, place):
    _, own, rank = v_ref.shape
    half = own // 2
    v = v_ref[...].astype(F32)
    blocks = [(v[0], v[1])]
    for a in range(0, rank * (lax.axis_size("frame") - 1), rank):
        blocks.append((others[:own, a : a + rank], others[own : 2 * own, a : a + rank]))
    return [
        jnp.concatenate(
            [jnp.where(place == 0, b[p][:half], b[p][half:]) for b in blocks], axis=0
        )
        for p in range(2)
    ]


def adjoint_pair(w):
    half = w.shape[1] // 2
    return jnp.concatenate([w, jnp.concatenate([-w[:, half:], w[:, :half]], axis=1)], axis=0)


def tree(value):
    terms = [value[i] for i in range(value.shape[0])]
    while len(terms) > 1:
        odd = [terms[-1]] if len(terms) % 2 else []
        terms = [a + b for a, b in zip(terms[::2], terms[1::2])] + odd
    return terms[0].astype(F32)


def in_pair():
    return lax.axis_index("cuts") // 2, lax.axis_index("cuts") % 2


def frame_of(step, own):
    return ((step // own) ^ lax.axis_index("frame")) * own + step % own


def tables_kernel(real, coils, after_ref, taby_ref, tabz_ref, coil_ref):
    del after_ref
    width, depth, pad = taby_ref.shape[0], tabz_ref.shape[0], coil_ref.shape[2]
    write_dft(taby_ref, width, lax.broadcasted_iota(jnp.int32, (max(TILE, width // TILE), width), 1))
    slice_of = lax.broadcasted_iota(jnp.int32, (max(TILE, depth // TILE), pad), 1) % real
    write_dft(tabz_ref, depth, slice_of + in_pair()[0] * real)
    column = lax.broadcasted_iota(jnp.int32, coil_ref.shape[1:], 1) // real
    row = lax.broadcasted_iota(jnp.int32, coil_ref.shape[1:], 0)
    for part in range(2):
        place = (row == column + part * coils) & (column < coils)
        coil_ref[part] = place.astype(F32).astype(BF16)


def turn_kernel(after_ref, b_ref, b_got_ref, m_ref, m_got_ref, b_out, m_out, turn_ref):
    del after_ref
    images, slab, width = b_ref.shape
    pitch = -(-slab // 8) * 8 + PITCH
    first = in_pair()[1] == 0
    for n, ref in enumerate((b_ref, b_got_ref)):
        start = jnp.where(first, n, 1 - n) * slab
        for h in range(width // LANES):
            lanes = slice(h * LANES, (h + 1) * LANES)
            for k in range(images):
                turn_ref[h, k * pitch : k * pitch + slab, :] = ref[k, :, lanes].astype(F32)
            for z in range(slab):
                rows = turn_ref[h, pl.ds(z, images, stride=pitch), :].astype(BF16)
                for k in range(0, b_out.shape[0], 2 * slab):
                    b_out[pl.ds(start + z + k, 1), :, lanes] = rows[None]
    mine, got = m_ref[...].astype(F32), m_got_ref[...].astype(F32)
    both = [jnp.where(first, mine, got), jnp.where(first, got, mine)]
    m_out[...] = jnp.concatenate(both, axis=2).astype(BF16)


def write_tables(pos, taby_ref, tabz_ref, w_ref, fz_ref):
    per, own = pos.shape[0] // 2, pos.shape[1] // lax.axis_size("frame")
    half = own // 2
    first_half = in_pair()[1] == 0
    frames = pos.shape[1] // 2

    def column(row, u):
        t = u // half * own + u % half
        rows = slice(row, row + per)
        return jnp.where(first_half, pos[rows, t : t + 1], pos[rows, t + half : t + half + 1])

    at_y = lax.broadcasted_iota(jnp.int32, (per, taby_ref.shape[0]), 1).astype(F32)
    at_z = lax.broadcasted_iota(jnp.int32, (per, tabz_ref.shape[0]), 1).astype(F32)
    group = max(1, 128 // per)
    for g in range(0, frames, group):
        hot_y, hot_z = (
            jnp.concatenate(
                [
                    jnp.where(iota == column(first, t), 1.0, 0.0)
                    for t in range(g, g + group)
                ],
                axis=0,
            ).astype(BF16)
            for iota, first in ((at_y, 0), (at_z, per))
        )
        rows = slice(g * per, (g + group) * per)
        w_ref[rows, :] = nn(hot_y, taby_ref[...]).astype(BF16)
        fz_ref[rows, :] = nn(hot_z, tabz_ref[...]).astype(BF16)


def predict_kernel(own, frames, slab, *refs):
    sent_ref, got_ref, v_ref, taby_ref, tabz_ref, coil_ref, b_ref, m_ref, kd_ref = refs[:9]
    pred_ref, w_ref, fz_ref, x_ref, i_ref = refs[9:]
    steps = frames
    width = b_ref.shape[2]
    rows = m_ref.shape[1]
    pad = fz_ref.shape[1] // 2
    per = w_ref.shape[0] // frames
    coils = rows // slab
    halves = width // LANES
    pitch = 2 * steps + PITCH
    stride = frames + PITCH

    pos, others = arrived(sent_ref, got_ref)
    write_tables(pos[: 2 * per, : 2 * frames], taby_ref, tabz_ref, w_ref, fz_ref)
    v = factor_matrix(*half_factors(v_ref, others, in_pair()[1]))
    for z in range(slab):
        image = nn(v, b_ref[z])
        for h in range(halves):
            i_ref[h, z * pitch : z * pitch + 2 * steps, :] = image[:, h * LANES : (h + 1) * LANES]

    m_re = m_ref[0].reshape(coils, slab, width)
    m_im = m_ref[1].reshape(coils, slab, width)

    def frame(step, carry):
        t = frame_of(step, own)
        i_re, i_im = (
            jnp.concatenate(
                [i_ref[h, pl.ds(at, slab, stride=pitch), :] for h in range(halves)], axis=1
            ).astype(BF16)[None]
            for at in (step, steps + step)
        )
        p_re = (m_re * i_re - m_im * i_im).reshape(rows, width)
        p_im = (m_re * i_im + m_im * i_re).reshape(rows, width)
        at = pl.ds(pl.multiple_of(t * per, TILE), per)
        lhs = adjoint_pair(w_ref[at, :])
        y = jnp.concatenate([(nt(p_re[k:k+128], lhs[:, :width]) + nt(p_im[k:k+128], lhs[:, width:])).T for k in range(0,rows,128)],axis=1)
        y_re, y_im = y[:per], y[per:]
        f = fz_ref[at, :].astype(F32)
        f_cos, f_sin = f[:, :rows], f[:, pad : pad + rows]
        x = jnp.concatenate([y_re * f_cos + y_im * f_sin, y_im * f_cos - y_re * f_sin], axis=0)
        for h in range(x_ref.shape[0]):
            lanes = min(LANES, rows - h * LANES)
            x_ref[h, pl.ds(t, 2 * per, stride=stride), :lanes] = x[:, h * LANES : h * LANES + lanes]
        return carry

    lax.fori_loop(0, steps, frame, 0, unroll=math.gcd(steps, 16))
    blocks = max(1, min(per, 512 // frames))

    def summed(part, first):
        at = [(part * per + first + k) * stride for k in range(blocks)]
        halves_of = [
            jnp.concatenate([x_ref[h, a : a + frames, :] for a in at], axis=0)
            for h in range(x_ref.shape[0])
        ]
        x = jnp.concatenate(halves_of, axis=1)[:, :rows].astype(BF16)
        return nt(coil_ref[part, :, :rows], x)

    for first in range(0, per, blocks):
        pred_ref[:, first * frames : (first + blocks) * frames] = (
            summed(0, first) + summed(1, first)
        ).astype(BF16)
    size = kd_ref.shape[1]
    at = pl.ds(pl.multiple_of(in_pair()[0] * size, LANES), size)
    pred_ref[:, at] = (pred_ref[:, at].astype(F32) - kd_ref[...].astype(F32)).astype(BF16)


def gradient_kernel(own, frames, slab, real, scale, n_r, *refs):
    r_refs, refs = refs[:n_r], refs[n_r:]
    b_ref, m_ref, w_ref, fz_ref, coil_ref, fg_ref, mine_ref, theirs_ref, r_ref, g_ref = refs
    steps = frames
    width = b_ref.shape[2]
    rank = b_ref.shape[1] // 2
    rows = m_ref.shape[1]
    pad = fz_ref.shape[1] // 2
    per = w_ref.shape[0] // frames
    coils = rows // slab
    halves = width // LANES
    pitch = 2 * steps + PITCH
    stride = frames + PITCH

    resid = total(r_refs).astype(BF16)
    blocks = max(1, min(per, 512 // frames))
    for part in range(2):
        for first in range(0, per, blocks):
            r = tn(resid[:, first * frames : (first + blocks) * frames], coil_ref[part])
            for k in range(blocks):
                at = (part * per + first + k) * stride
                for h in range(r_ref.shape[0]):
                    r_ref[h, at : at + frames, :] = r[
                        k * frames : (k + 1) * frames, h * LANES : (h + 1) * LANES
                    ]

    m_re = m_ref[0].reshape(coils, slab, width)
    m_im = m_ref[1].reshape(coils, slab, width)

    def frame(step, carry):
        t = frame_of(step, own)
        at = pl.ds(pl.multiple_of(t * per, TILE), per)
        rhs = adjoint_pair(w_ref[at, :])
        f = fz_ref[at, :].astype(F32)
        f_cos, f_sin = f[:, :pad], f[:, pad:]
        r = jnp.concatenate(
            [r_ref[h, pl.ds(t, 2 * per, stride=stride), :] for h in range(r_ref.shape[0])], axis=1
        )
        r_re, r_im = r[:per], r[per:]
        q = jnp.concatenate([r_re * f_cos - r_im * f_sin, r_im * f_cos + r_re * f_sin], axis=0)
        u = tn(q[:, :rows].astype(BF16), rhs).astype(BF16)
        u_re = u[:, :width].reshape(coils, slab, width)
        u_im = u[:, width:].reshape(coils, slab, width)
        g_re = tree(m_re * u_re + m_im * u_im)
        g_im = tree(m_re * u_im - m_im * u_re)
        for h in range(halves):
            lanes = slice(h * LANES, (h + 1) * LANES)
            g_ref[h, pl.ds(step, slab, stride=pitch), :] = g_re[:, lanes]
            g_ref[h, pl.ds(steps + step, slab, stride=pitch), :] = g_im[:, lanes]
        return carry

    lax.fori_loop(0, steps, frame, 0, unroll=math.gcd(steps, 16))
    acc = jnp.zeros((2 * steps, 2 * rank), F32)
    for ref, place in ((mine_ref, in_pair()[1]), (theirs_ref, 1 - in_pair()[1])):
        for n in range(ref.shape[0]):
            z = n // real * 2 * real + place * real + n % real
            at = pl.ds(pl.multiple_of(z * pitch, 8), 2 * steps)
            g = jnp.concatenate([g_ref[h, at, :] for h in range(halves)], axis=1).astype(BF16)
            ref[n] = g
            acc = acc + nt(g, b_ref[pl.ds(z, 1)][0])
    top, bottom = acc[:steps], acc[steps:]
    fg = jnp.concatenate(
        [top[:, :rank] + bottom[:, rank:], bottom[:, :rank] - top[:, rank:]], axis=1
    )
    fg = (fg * scale).astype(fg_ref.dtype)
    n_cuts, n_frame, n_rows, n_lanes = fg_ref.shape
    for d in range(n_frame):
        piece = jnp.concatenate(
            [
                fg[d * own + k : d * own + k + n_rows].astype(F32)
                for k in range(0, own, n_rows)
            ],
            axis=1,
        ).astype(fg_ref.dtype)
        target = lax.axis_index("frame") ^ d
        for c in range(n_cuts):
            fg_ref[c, pl.ds(target, 1)] = piece[None]


def basis_kernel(sent_ref, got_ref, v_ref, g_ref, g_got_ref, grad_ref, rows_ref):
    _, others = arrived(sent_ref, got_ref)
    place = in_pair()[1]
    pairs_of = [
        (factor_matrix(*half_factors(v_ref, others, place)), g_ref),
        (factor_matrix(*half_factors(v_ref, others, 1 - place)), g_got_ref),
    ]
    halves = g_ref.shape[2] // LANES
    images = 2 * v_ref.shape[2]
    slab = grad_ref.shape[0] // (images * halves)
    pitch = slab * halves + PITCH
    for z in range(slab):
        grad = functools.reduce(
            jnp.add,
            [tn(v, ref[k]) for v, ref in pairs_of for k in range(z, g_ref.shape[0], slab)],
        )
        for h in range(halves):
            rows_ref[pl.ds(z * halves + h, images, stride=pitch), :] = grad[
                :, h * LANES : (h + 1) * LANES
            ]
    for n in range(images):
        grad_ref[n * slab * halves : (n + 1) * slab * halves, :] = rows_ref[
            n * pitch : n * pitch + slab * halves, :
        ]


def stages(size):
    steps, stride = [(1, 2)], 2
    if (size // stride).bit_length() % 2 == 0:
        steps.append((stride, 2))
        stride *= 2
    while stride < size:
        steps.append((stride, 4))
        stride *= 4
    return steps


def swap(value, axis, distance):
    size = lax.axis_size(axis)
    return lax.ppermute(value, axis, [(i, i ^ distance) for i in range(size)])


def shares(value, axis, last=1, skip=0):
    steps = stages(lax.axis_size(axis))[skip:]
    for number, (stride, radix) in enumerate(steps):
        if number + last == len(steps) + 1:
            return value
        terms = [value] + [swap(value, axis, stride * d) for d in range(1, radix)]
        if number + 1 < len(steps):
            value = pairs([term.astype(F32) for term in terms]).astype(value.dtype)
    return terms


def grown(value, rows, lanes):
    return jnp.pad(value, ((0, rows - value.shape[0]), (0, lanes - value.shape[1])))


def collect(positions, v_own, meanwhile):
    n_cuts, n_frame = lax.axis_size("cuts"), lax.axis_size("frame")
    even = lax.axis_index("cuts") % 2 == 0
    stride, radix = stages(n_cuts)[-1]
    near = shares(positions, "cuts", last=2)
    rank = v_own.shape[2]
    rows = max(near.shape[0], math.prod(v_own.shape[:2]))
    lanes = max(near.shape[1], rank)
    v_packet = grown(v_own.reshape(-1, rank).astype(near.dtype), rows, lanes)
    near, v_packet = lax.optimization_barrier((near, v_packet))
    packet = jnp.where(even, grown(near, rows, lanes), v_packet)
    got = []
    for d in range(1, max(radix, n_frame)):
        route = []
        for c in range(n_cuts):
            for f in range(n_frame):
                if c % 2 == 0 and d < radix:
                    route.append((c * n_frame + f, (c ^ stride * d) * n_frame + f))
                if c % 2 == 1 and d < n_frame:
                    route.append((c * n_frame + f, c * n_frame + (f ^ d)))
        got.append(lax.ppermute(packet, ("cuts", "frame"), route))
    staged = meanwhile(packet)
    got, staged = lax.optimization_barrier((got, staged))
    joined = pairs([x.astype(F32) for x in (packet, *got[: radix - 1])]).astype(near.dtype)
    others = jnp.concatenate([x[:, :rank] for x in got[: n_frame - 1]], axis=1)
    lanes = max(lanes, others.shape[1])
    sent = jnp.where(even, grown(joined, rows, lanes), grown(others, rows, lanes))
    return sent, swap(sent, "cuts", 1), staged


def call(kernel, outs, scratch, flops, *operands, limit=0):
    def size(x):
        rows = [-(-x.shape[-2] // TILE) * TILE, -(-x.shape[-1] // LANES) * LANES]
        return math.prod(x.shape[:-2]) * math.prod(rows) * jnp.dtype(x.dtype).itemsize

    nbytes = sum(size(x) for x in operands)
    held = nbytes + sum(size(x) for x in (*outs, *scratch))
    limit = limit or min(56, 10 + held * 5 // (4 * 1024 * 1024))
    return pl.pallas_call(
        kernel,
        out_shape=outs,
        scratch_shapes=scratch,
        compiler_params=pltpu.CompilerParams(vmem_limit_bytes=limit * 1024 * 1024),
        cost_estimate=pl.CostEstimate(flops=flops, bytes_accessed=nbytes, transcendentals=0),
    )(*operands)


def one_position(basis, coil_maps, factors, lines, kdata, scale):
    n_cuts, n_frame = lax.axis_size("cuts"), lax.axis_size("frame")
    cut = lax.axis_index("cuts")
    rank, slab, width = basis.shape[1:]
    coils = coil_maps.shape[1]
    columns = lines.shape[1]
    half = factors.shape[2] // 2
    frames = lines.shape[0] // 2
    per = columns * n_cuts
    samples = frames * per
    depth = slab * n_cuts
    ky_rows = width // n_cuts

    spread = max(1, TILE // (2 * slab))
    tall = spread * 2 * slab
    coil_groups = -(-coils // spread)
    rows = coil_groups * tall
    pad = -(-rows // LANES) * LANES
    coil_rows = -(-2 * coils // 8) * 8

    kind = BF16 if max(width, depth) <= 256 else F32
    turned = lines.T
    mine = jnp.stack([cut * ky_rows + turned // depth, turned % depth])
    owner = lax.broadcasted_iota(jnp.int32, (2 * per, 2 * frames), 0) // columns % n_cuts == cut
    every = jnp.broadcast_to(mine[:, None], (2, n_cuts, columns, 2 * frames))
    placed = jnp.where(owner, every.reshape(2 * per, 2 * frames), 0).astype(kind)
    v_own = factors.transpose(0, 2, 1)
    maps = jnp.pad(coil_maps, ((0, 0), (0, coil_groups * spread - coils), (0, 0), (0, 0)))
    images_in = basis.reshape(2 * rank, slab, width)

    flops = 2 * 2 * per * rows * 2 * width * 8
    halves = width // LANES
    x_shape = jax.ShapeDtypeStruct((pad // LANES, (2 * per + 1) * (frames + PITCH), LANES), F32)

    def images(steps):
        return pltpu.VMEM((halves, (tall + 1) * (2 * steps + PITCH), LANES), F32)

    _, b, m, k = lax.optimization_barrier((placed, images_in, maps, kdata))
    b_got, m_got, k_got = (swap(x, "cuts", 1) for x in (b, m, k))

    def stage(packet):
        tables = call(
            functools.partial(tables_kernel, 2 * slab, coils),
            (
                jax.ShapeDtypeStruct((width, 2 * width), BF16),
                jax.ShapeDtypeStruct((depth, 2 * pad), BF16),
                jax.ShapeDtypeStruct((2, coil_rows, pad), BF16),
            ),
            [],
            1024 * 1024 * 1024,
            b_got,
        )
        turned = call(
            turn_kernel,
            (
                jax.ShapeDtypeStruct((tall, 2 * rank, width), BF16),
                jax.ShapeDtypeStruct((2, maps.shape[1], 2 * slab, width), BF16),
            ),
            [pltpu.VMEM((halves, (2 * rank + 1) * (-(-slab // 8) * 8 + PITCH), LANES), F32)],
            1024 * 1024 * 1024,
            packet, images_in, b_got, maps, m_got,
        )
        return tables, turned

    sent, got, ((taby, tabz, coil_of), (b_rows, m_rows)) = collect(placed, v_own, stage)
    m_rows = m_rows.reshape(2, rows, width)
    even = lax.axis_index("cuts") % 2 == 0
    _, mine, k_got = lax.optimization_barrier((sent, kdata, k_got))
    both = jnp.stack([jnp.where(even, mine, k_got), jnp.where(even, k_got, mine)])
    both = both.transpose(1, 4, 0, 3, 2).reshape(2 * coils, 2 * columns, n_frame, 2, half)
    kd = jnp.where(even, both[..., 0, :], both[..., 1, :]).reshape(2 * coils, -1)
    kd = jnp.pad(kd, ((0, coil_rows - 2 * coils), (0, 0)))
    predicted, w, fz = call(
        functools.partial(predict_kernel, half, frames, tall),
        (
            jax.ShapeDtypeStruct((coil_rows, samples), BF16),
            jax.ShapeDtypeStruct((samples, 2 * width), BF16),
            jax.ShapeDtypeStruct((samples, 2 * pad), BF16),
        ),
        [pltpu.VMEM(x_shape.shape, F32), images(frames)],
        flops * frames,
        sent, got, v_own, taby, tabz, coil_of, b_rows, m_rows, kd,
    )
    resid_terms = shares(predicted, "cuts", skip=1)

    fold = max(1, LANES // (2 * rank))
    own_slab = jax.ShapeDtypeStruct((tall // 2, 2 * frames, width), BF16)
    pieces, g, theirs = call(
        functools.partial(gradient_kernel, half, frames, tall, slab, scale, len(resid_terms)),
        (
            jax.ShapeDtypeStruct((n_cuts, n_frame, half // fold, 2 * rank * fold), F32),
            own_slab,
            own_slab,
        ),
        [pltpu.VMEM(x_shape.shape, F32), images(frames)],
        flops * frames,
        *resid_terms, b_rows, m_rows, w, fz, coil_of,
    )
    (grad,) = call(
        basis_kernel,
        (jax.ShapeDtypeStruct((2 * rank * slab * halves, LANES), F32),),
        [pltpu.VMEM(((2 * rank + 1) * (slab * halves + PITCH), LANES), F32)],
        2 * 2 * rank * 4 * frames * slab * width * 8,
        sent, got, v_own, g, swap(theirs, "cuts", 1),
    )
    return grad, pieces


def pairs(terms):
    while len(terms) > 1:
        odd = [terms[-1]] if len(terms) % 2 else []
        terms = [a + b for a, b in zip(terms[::2], terms[1::2])] + odd
    return terms[0]


def body(basis, coil_maps, factors, lines, kdata):
    n_cuts, n_frame = lax.axis_size("cuts"), lax.axis_size("frame")
    readout = basis.shape[3]
    rank = basis.shape[1]
    own = factors.shape[2]
    scale = 1.0 / math.sqrt(coil_maps.shape[1] * lines.shape[1] * n_cuts * readout * n_frame)
    grads, fg = [], 0.0
    for x in range(readout):
        grad, term = one_position(
            basis[:, :, :, x], coil_maps[:, :, :, x], factors, lines, kdata[..., x], scale
        )
        grads.append(grad)
        fg = fg + term
    pieces = fg.reshape((n_cuts * n_frame,) + fg.shape[2:])
    arriving = lax.all_to_all(pieces, ("cuts", "frame"), 0, 0, tiled=True)
    arriving, grads = lax.optimization_barrier((arriving, grads))
    grads = [grad.reshape(2, rank, basis.shape[2], -1) for grad in grads]
    basis_grad = grads[0][:, :, :, None] if readout == 1 else jnp.stack(grads, axis=3)
    parts = arriving.astype(F32).reshape((n_cuts // 2, 2, n_frame) + fg.shape[2:])
    summed = jnp.sum(parts, axis=(0, 2))
    folded = summed.reshape(2, summed.shape[1], -1, 2, rank)
    return basis_grad, folded.transpose(3, 4, 0, 2, 1).reshape(2, rank, own)


def solution(mesh):
    placed = (
        P(None, None, "cuts", "frame", None),
        P(None, None, "cuts", "frame", None),
        P(None, None, "frame"),
        P(None, "cuts"),
        P(None, None, "cuts", None, "frame"),
    )
    return jax.shard_map(
        body,
        mesh=mesh,
        in_specs=placed,
        out_specs=(P(None, None, "cuts", "frame", None), P(None, None, "frame")),
        check_vma=False,
    )
```

```python
import functools
import math

import jax
import jax.numpy as jnp
import numpy as np
from jax import lax
from jax.experimental import pallas as pl
from jax.experimental.pallas import tpu as pltpu
from jax.sharding import PartitionSpec as P

F32 = jnp.float32
BF16 = jnp.bfloat16
LANES = 128
TILE = 16
PITCH = 8


def trig(product, size):
    angle = (product % size).astype(F32) * (2.0 * math.pi / size)
    return jnp.cos(angle), jnp.sin(angle)


def write_dft(out_ref, size, index):
    lanes = index.shape[1]
    fine = lax.broadcasted_iota(jnp.int32, (TILE, lanes), 0)
    b_cos, b_sin = trig(fine * index[:TILE], size)
    coarse = lax.broadcasted_iota(jnp.int32, (size // TILE, lanes), 0) * TILE
    a_cos, a_sin = trig(coarse * index[: size // TILE], size)
    factor = 1.0 / math.sqrt(size)
    a_cos, a_sin = a_cos * factor, a_sin * factor
    for a in range(size // TILE):
        rows = slice(a * TILE, (a + 1) * TILE)
        p_cos, p_sin = a_cos[a : a + 1], a_sin[a : a + 1]
        out_ref[rows, :lanes] = (p_cos * b_cos - p_sin * b_sin).astype(BF16)
        out_ref[rows, lanes:] = (p_sin * b_cos + p_cos * b_sin).astype(BF16)


def nn(a, b):
    return lax.dot_general(a, b, (((1,), (0,)), ((), ())), preferred_element_type=F32)


def nt(a, b):
    return lax.dot_general(a, b, (((1,), (1,)), ((), ())), preferred_element_type=F32)


def tn(a, b):
    return lax.dot_general(a, b, (((0,), (0,)), ((), ())), preferred_element_type=F32)


def total(refs):
    terms = [ref[...].astype(F32) for ref in refs]
    while len(terms) > 1:
        odd = [terms[-1]] if len(terms) % 2 else []
        terms = [a + b for a, b in zip(terms[::2], terms[1::2])] + odd
    return terms[0]


def arrived(sent_ref, got_ref):
    sent, got = sent_ref[...].astype(F32), got_ref[...].astype(F32)
    even = in_pair()[1] == 0
    return jnp.where(even, sent, got), jnp.where(even, got, sent)


def factor_matrix(v_re, v_im):
    top = jnp.concatenate([v_re, -v_im], axis=1)
    bottom = jnp.concatenate([v_im, v_re], axis=1)
    return jnp.concatenate([top, bottom], axis=0).astype(BF16)


def half_factors(v_ref, others, place):
    _, own, rank = v_ref.shape
    half = own // 2
    v = v_ref[...].astype(F32)
    blocks = [(v[0], v[1])]
    for a in range(0, rank * (lax.axis_size("frame") - 1), rank):
        blocks.append((others[:own, a : a + rank], others[own : 2 * own, a : a + rank]))
    return [
        jnp.concatenate(
            [jnp.where(place == 0, b[p][:half], b[p][half:]) for b in blocks], axis=0
        )
        for p in range(2)
    ]


def adjoint_pair(w):
    half = w.shape[1] // 2
    return jnp.concatenate([w, jnp.concatenate([-w[:, half:], w[:, :half]], axis=1)], axis=0)


def tree(value):
    terms = [value[i] for i in range(value.shape[0])]
    while len(terms) > 1:
        odd = [terms[-1]] if len(terms) % 2 else []
        terms = [a + b for a, b in zip(terms[::2], terms[1::2])] + odd
    return terms[0].astype(F32)


def in_pair():
    return lax.axis_index("cuts") // 2, lax.axis_index("cuts") % 2


def frame_of(step, own):
    return ((step // own) ^ lax.axis_index("frame")) * own + step % own


def tables_kernel(real, coils, after_ref, taby_ref, tabz_ref, coil_ref):
    del after_ref
    width, depth, pad = taby_ref.shape[0], tabz_ref.shape[0], coil_ref.shape[2]
    write_dft(taby_ref, width, lax.broadcasted_iota(jnp.int32, (max(TILE, width // TILE), width), 1))
    slice_of = lax.broadcasted_iota(jnp.int32, (max(TILE, depth // TILE), pad), 1) % real
    write_dft(tabz_ref, depth, slice_of + in_pair()[0] * real)
    column = lax.broadcasted_iota(jnp.int32, coil_ref.shape[1:], 1) // real
    row = lax.broadcasted_iota(jnp.int32, coil_ref.shape[1:], 0)
    for part in range(2):
        place = (row == column + part * coils) & (column < coils)
        coil_ref[part] = place.astype(F32).astype(BF16)


def turn_kernel(after_ref, b_ref, b_got_ref, m_ref, m_got_ref, b_out, m_out, turn_ref):
    del after_ref
    images, slab, width = b_ref.shape
    pitch = -(-slab // 8) * 8 + PITCH
    first = in_pair()[1] == 0
    for n, ref in enumerate((b_ref, b_got_ref)):
        start = jnp.where(first, n, 1 - n) * slab
        for h in range(width // LANES):
            lanes = slice(h * LANES, (h + 1) * LANES)
            for k in range(images):
                turn_ref[h, k * pitch : k * pitch + slab, :] = ref[k, :, lanes].astype(F32)
            for z in range(slab):
                rows = turn_ref[h, pl.ds(z, images, stride=pitch), :].astype(BF16)
                for k in range(0, b_out.shape[0], 2 * slab):
                    b_out[pl.ds(start + z + k, 1), :, lanes] = rows[None]
    mine, got = m_ref[...].astype(F32), m_got_ref[...].astype(F32)
    both = [jnp.where(first, mine, got), jnp.where(first, got, mine)]
    m_out[...] = jnp.concatenate(both, axis=2).astype(BF16)


def write_tables(pos, taby_ref, tabz_ref, w_ref, fz_ref):
    per, own = pos.shape[0] // 2, pos.shape[1] // lax.axis_size("frame")
    half = own // 2
    first_half = in_pair()[1] == 0
    frames = pos.shape[1] // 2

    def column(row, u):
        t = u // half * own + u % half
        rows = slice(row, row + per)
        return jnp.where(first_half, pos[rows, t : t + 1], pos[rows, t + half : t + half + 1])

    at_y = lax.broadcasted_iota(jnp.int32, (per, taby_ref.shape[0]), 1).astype(F32)
    at_z = lax.broadcasted_iota(jnp.int32, (per, tabz_ref.shape[0]), 1).astype(F32)
    group = max(1, 128 // per)
    for g in range(0, frames, group):
        hot_y, hot_z = (
            jnp.concatenate(
                [
                    jnp.where(iota == column(first, t), 1.0, 0.0)
                    for t in range(g, g + group)
                ],
                axis=0,
            ).astype(BF16)
            for iota, first in ((at_y, 0), (at_z, per))
        )
        rows = slice(g * per, (g + group) * per)
        w_ref[rows, :] = nn(hot_y, taby_ref[...]).astype(BF16)
        fz_ref[rows, :] = nn(hot_z, tabz_ref[...]).astype(BF16)


def predict_kernel(own, frames, slab, *refs):
    sent_ref, got_ref, v_ref, taby_ref, tabz_ref, coil_ref, b_ref, m_ref, kd_ref = refs[:9]
    pred_ref, w_ref, fz_ref, x_ref, i_ref = refs[9:]
    steps = frames
    width = b_ref.shape[2]
    rows = m_ref.shape[1]
    pad = fz_ref.shape[1] // 2
    per = w_ref.shape[0] // frames
    coils = rows // slab
    halves = width // LANES
    pitch = 2 * steps + PITCH
    stride = frames + PITCH

    pos, others = arrived(sent_ref, got_ref)
    write_tables(pos[: 2 * per, : 2 * frames], taby_ref, tabz_ref, w_ref, fz_ref)
    v = factor_matrix(*half_factors(v_ref, others, in_pair()[1]))
    for z in range(slab):
        image = nn(v, b_ref[z])
        for h in range(halves):
            i_ref[h, z * pitch : z * pitch + 2 * steps, :] = image[:, h * LANES : (h + 1) * LANES]

    m_re = m_ref[0].reshape(coils, slab, width)
    m_im = m_ref[1].reshape(coils, slab, width)

    def frame(step, carry):
        t = frame_of(step, own)
        i_re, i_im = (
            jnp.concatenate(
                [i_ref[h, pl.ds(at, slab, stride=pitch), :] for h in range(halves)], axis=1
            ).astype(BF16)[None]
            for at in (step, steps + step)
        )
        p_re = (m_re * i_re - m_im * i_im).reshape(rows, width)
        p_im = (m_re * i_im + m_im * i_re).reshape(rows, width)
        at = pl.ds(pl.multiple_of(t * per, TILE), per)
        lhs = adjoint_pair(w_ref[at, :])
        y = jnp.concatenate([(nt(p_re[k:k+128], lhs[:, :width]) + nt(p_im[k:k+128], lhs[:, width:])).T for k in range(0,rows,128)],axis=1)
        y_re, y_im = y[:per], y[per:]
        f = fz_ref[at, :].astype(F32)
        f_cos, f_sin = f[:, :rows], f[:, pad : pad + rows]
        x = jnp.concatenate([y_re * f_cos + y_im * f_sin, y_im * f_cos - y_re * f_sin], axis=0)
        for h in range(x_ref.shape[0]):
            lanes = min(LANES, rows - h * LANES)
            x_ref[h, pl.ds(t, 2 * per, stride=stride), :lanes] = x[:, h * LANES : h * LANES + lanes]
        return carry

    lax.fori_loop(0, steps, frame, 0, unroll=math.gcd(steps, 16))
    blocks = max(1, min(per, 512 // frames))

    def summed(part, first):
        at = [(part * per + first + k) * stride for k in range(blocks)]
        halves_of = [
            jnp.concatenate([x_ref[h, a : a + frames, :] for a in at], axis=0)
            for h in range(x_ref.shape[0])
        ]
        x = jnp.concatenate(halves_of, axis=1)[:, :rows].astype(BF16)
        return nt(coil_ref[part, :, :rows], x)

    for first in range(0, per, blocks):
        pred_ref[:, first * frames : (first + blocks) * frames] = (
            summed(0, first) + summed(1, first)
        ).astype(BF16)
    size = kd_ref.shape[1]
    at = pl.ds(pl.multiple_of(in_pair()[0] * size, LANES), size)
    pred_ref[:, at] = (pred_ref[:, at].astype(F32) - kd_ref[...].astype(F32)).astype(BF16)


def gradient_kernel(own, frames, slab, real, scale, n_r, *refs):
    r_refs, refs = refs[:n_r], refs[n_r:]
    b_ref, m_ref, w_ref, fz_ref, coil_ref, fg_ref, mine_ref, theirs_ref, r_ref, g_ref = refs
    steps = frames
    width = b_ref.shape[2]
    rank = b_ref.shape[1] // 2
    rows = m_ref.shape[1]
    pad = fz_ref.shape[1] // 2
    per = w_ref.shape[0] // frames
    coils = rows // slab
    halves = width // LANES
    pitch = 2 * steps + PITCH
    stride = frames + PITCH

    resid = total(r_refs).astype(BF16)
    blocks = max(1, min(per, 512 // frames))
    for part in range(2):
        for first in range(0, per, blocks):
            r = tn(resid[:, first * frames : (first + blocks) * frames], coil_ref[part])
            for k in range(blocks):
                at = (part * per + first + k) * stride
                for h in range(r_ref.shape[0]):
                    r_ref[h, at : at + frames, :] = r[
                        k * frames : (k + 1) * frames, h * LANES : (h + 1) * LANES
                    ]

    m_re = m_ref[0].reshape(coils, slab, width)
    m_im = m_ref[1].reshape(coils, slab, width)

    def frame(step, carry):
        t = frame_of(step, own)
        at = pl.ds(pl.multiple_of(t * per, TILE), per)
        rhs = adjoint_pair(w_ref[at, :])
        f = fz_ref[at, :].astype(F32)
        f_cos, f_sin = f[:, :pad], f[:, pad:]
        r = jnp.concatenate(
            [r_ref[h, pl.ds(t, 2 * per, stride=stride), :] for h in range(r_ref.shape[0])], axis=1
        )
        r_re, r_im = r[:per], r[per:]
        q = jnp.concatenate([r_re * f_cos - r_im * f_sin, r_im * f_cos + r_re * f_sin], axis=0)
        u = tn(q[:, :rows].astype(BF16), rhs).astype(BF16)
        u_re = u[:, :width].reshape(coils, slab, width)
        u_im = u[:, width:].reshape(coils, slab, width)
        g_re = tree(m_re * u_re + m_im * u_im)
        g_im = tree(m_re * u_im - m_im * u_re)
        for h in range(halves):
            lanes = slice(h * LANES, (h + 1) * LANES)
            g_ref[h, pl.ds(step, slab, stride=pitch), :] = g_re[:, lanes]
            g_ref[h, pl.ds(steps + step, slab, stride=pitch), :] = g_im[:, lanes]
        return carry

    lax.fori_loop(0, steps, frame, 0, unroll=math.gcd(steps, 16))
    acc = jnp.zeros((2 * steps, 2 * rank), F32)
    for ref, place in ((mine_ref, in_pair()[1]), (theirs_ref, 1 - in_pair()[1])):
        for n in range(ref.shape[0]):
            z = n // real * 2 * real + place * real + n % real
            at = pl.ds(pl.multiple_of(z * pitch, 8), 2 * steps)
            g = jnp.concatenate([g_ref[h, at, :] for h in range(halves)], axis=1).astype(BF16)
            ref[n] = g
            acc = acc + nt(g, b_ref[pl.ds(z, 1)][0])
    top, bottom = acc[:steps], acc[steps:]
    fg = jnp.concatenate(
        [top[:, :rank] + bottom[:, rank:], bottom[:, :rank] - top[:, rank:]], axis=1
    )
    fg = (fg * scale).astype(fg_ref.dtype)
    n_cuts, n_frame, n_rows, n_lanes = fg_ref.shape
    for d in range(n_frame):
        piece = jnp.concatenate(
            [
                fg[d * own + k : d * own + k + n_rows].astype(F32)
                for k in range(0, own, n_rows)
            ],
            axis=1,
        ).astype(fg_ref.dtype)
        target = lax.axis_index("frame") ^ d
        for c in range(n_cuts):
            fg_ref[c, pl.ds(target, 1)] = piece[None]


def basis_kernel(sent_ref, got_ref, v_ref, g_ref, g_got_ref, grad_ref, rows_ref):
    _, others = arrived(sent_ref, got_ref)
    place = in_pair()[1]
    pairs_of = [
        (factor_matrix(*half_factors(v_ref, others, place)), g_ref),
        (factor_matrix(*half_factors(v_ref, others, 1 - place)), g_got_ref),
    ]
    halves = g_ref.shape[2] // LANES
    images = 2 * v_ref.shape[2]
    slab = grad_ref.shape[0] // (images * halves)
    pitch = slab * halves + PITCH
    for z in range(slab):
        grad = functools.reduce(
            jnp.add,
            [tn(v, ref[k]) for v, ref in pairs_of for k in range(z, g_ref.shape[0], slab)],
        )
        for h in range(halves):
            rows_ref[pl.ds(z * halves + h, images, stride=pitch), :] = grad[
                :, h * LANES : (h + 1) * LANES
            ]
    for n in range(images):
        grad_ref[n * slab * halves : (n + 1) * slab * halves, :] = rows_ref[
            n * pitch : n * pitch + slab * halves, :
        ]


def stages(size):
    steps, stride = [(1, 2)], 2
    if (size // stride).bit_length() % 2 == 0:
        steps.append((stride, 2))
        stride *= 2
    while stride < size:
        steps.append((stride, 4))
        stride *= 4
    return steps


def swap(value, axis, distance):
    size = lax.axis_size(axis)
    return lax.ppermute(value, axis, [(i, i ^ distance) for i in range(size)])


def shares(value, axis, last=1, skip=0):
    steps = stages(lax.axis_size(axis))[skip:]
    for number, (stride, radix) in enumerate(steps):
        if number + last == len(steps) + 1:
            return value
        terms = [value] + [swap(value, axis, stride * d) for d in range(1, radix)]
        if number + 1 < len(steps):
            value = pairs([term.astype(F32) for term in terms]).astype(value.dtype)
    return terms


def grown(value, rows, lanes):
    return jnp.pad(value, ((0, rows - value.shape[0]), (0, lanes - value.shape[1])))


def collect(positions, v_own, meanwhile):
    n_cuts, n_frame = lax.axis_size("cuts"), lax.axis_size("frame")
    even = lax.axis_index("cuts") % 2 == 0
    stride, radix = stages(n_cuts)[-1]
    near = shares(positions, "cuts", last=2)
    rank = v_own.shape[2]
    rows = max(near.shape[0], math.prod(v_own.shape[:2]))
    lanes = max(near.shape[1], rank)
    v_packet = grown(v_own.reshape(-1, rank).astype(near.dtype), rows, lanes)
    near, v_packet = lax.optimization_barrier((near, v_packet))
    packet = jnp.where(even, grown(near, rows, lanes), v_packet)
    got = []
    for d in range(1, max(radix, n_frame)):
        route = []
        for c in range(n_cuts):
            for f in range(n_frame):
                if c % 2 == 0 and d < radix:
                    route.append((c * n_frame + f, (c ^ stride * d) * n_frame + f))
                if c % 2 == 1 and d < n_frame:
                    route.append((c * n_frame + f, c * n_frame + (f ^ d)))
        got.append(lax.ppermute(packet, ("cuts", "frame"), route))
    staged = meanwhile(packet)
    got, staged = lax.optimization_barrier((got, staged))
    joined = pairs([x.astype(F32) for x in (packet, *got[: radix - 1])]).astype(near.dtype)
    others = jnp.concatenate([x[:, :rank] for x in got[: n_frame - 1]], axis=1)
    lanes = max(lanes, others.shape[1])
    sent = jnp.where(even, grown(joined, rows, lanes), grown(others, rows, lanes))
    return sent, swap(sent, "cuts", 1), staged


def call(kernel, outs, scratch, flops, *operands, limit=0):
    def size(x):
        rows = [-(-x.shape[-2] // TILE) * TILE, -(-x.shape[-1] // LANES) * LANES]
        return math.prod(x.shape[:-2]) * math.prod(rows) * jnp.dtype(x.dtype).itemsize

    nbytes = sum(size(x) for x in operands)
    held = nbytes + sum(size(x) for x in (*outs, *scratch))
    limit = limit or min(56, 10 + held * 5 // (4 * 1024 * 1024))
    return pl.pallas_call(
        kernel,
        out_shape=outs,
        scratch_shapes=scratch,
        compiler_params=pltpu.CompilerParams(vmem_limit_bytes=limit * 1024 * 1024),
        cost_estimate=pl.CostEstimate(flops=flops, bytes_accessed=nbytes, transcendentals=0),
    )(*operands)


def one_position(basis, coil_maps, factors, lines, kdata, scale):
    n_cuts, n_frame = lax.axis_size("cuts"), lax.axis_size("frame")
    cut = lax.axis_index("cuts")
    rank, slab, width = basis.shape[1:]
    coils = coil_maps.shape[1]
    columns = lines.shape[1]
    half = factors.shape[2] // 2
    frames = lines.shape[0] // 2
    per = columns * n_cuts
    samples = frames * per
    depth = slab * n_cuts
    ky_rows = width // n_cuts

    spread = max(1, TILE // (2 * slab))
    tall = spread * 2 * slab
    coil_groups = -(-coils // spread)
    rows = coil_groups * tall
    pad = -(-rows // LANES) * LANES
    coil_rows = -(-2 * coils // 8) * 8

    kind = BF16 if max(width, depth) <= 256 else F32
    turned = lines.T
    mine = jnp.stack([cut * ky_rows + turned // depth, turned % depth])
    owner = lax.broadcasted_iota(jnp.int32, (2 * per, 2 * frames), 0) // columns % n_cuts == cut
    every = jnp.broadcast_to(mine[:, None], (2, n_cuts, columns, 2 * frames))
    placed = jnp.where(owner, every.reshape(2 * per, 2 * frames), 0).astype(kind)
    v_own = factors.transpose(0, 2, 1)
    maps = jnp.pad(coil_maps, ((0, 0), (0, coil_groups * spread - coils), (0, 0), (0, 0)))
    images_in = basis.reshape(2 * rank, slab, width)

    flops = 2 * 2 * per * rows * 2 * width * 8
    halves = width // LANES
    x_shape = jax.ShapeDtypeStruct((pad // LANES, (2 * per + 1) * (frames + PITCH), LANES), F32)

    def images(steps):
        return pltpu.VMEM((halves, (tall + 1) * (2 * steps + PITCH), LANES), F32)

    _, b, m, k = lax.optimization_barrier((placed, images_in, maps, kdata))
    b_got, m_got, k_got = (swap(x, "cuts", 1) for x in (b, m, k))

    def stage(packet):
        tables = call(
            functools.partial(tables_kernel, 2 * slab, coils),
            (
                jax.ShapeDtypeStruct((width, 2 * width), BF16),
                jax.ShapeDtypeStruct((depth, 2 * pad), BF16),
                jax.ShapeDtypeStruct((2, coil_rows, pad), BF16),
            ),
            [],
            1024 * 1024 * 1024,
            b_got,
        )
        turned = call(
            turn_kernel,
            (
                jax.ShapeDtypeStruct((tall, 2 * rank, width), BF16),
                jax.ShapeDtypeStruct((2, maps.shape[1], 2 * slab, width), BF16),
            ),
            [pltpu.VMEM((halves, (2 * rank + 1) * (-(-slab // 8) * 8 + PITCH), LANES), F32)],
            1024 * 1024 * 1024,
            packet, images_in, b_got, maps, m_got,
        )
        return tables, turned

    sent, got, ((taby, tabz, coil_of), (b_rows, m_rows)) = collect(placed, v_own, stage)
    m_rows = m_rows.reshape(2, rows, width)
    even = lax.axis_index("cuts") % 2 == 0
    _, mine, k_got = lax.optimization_barrier((sent, kdata, k_got))
    both = jnp.stack([jnp.where(even, mine, k_got), jnp.where(even, k_got, mine)])
    both = both.transpose(1, 4, 0, 3, 2).reshape(2 * coils, 2 * columns, n_frame, 2, half)
    kd = jnp.where(even, both[..., 0, :], both[..., 1, :]).reshape(2 * coils, -1)
    kd = jnp.pad(kd, ((0, coil_rows - 2 * coils), (0, 0)))
    predicted, w, fz = call(
        functools.partial(predict_kernel, half, frames, tall),
        (
            jax.ShapeDtypeStruct((coil_rows, samples), BF16),
            jax.ShapeDtypeStruct((samples, 2 * width), BF16),
            jax.ShapeDtypeStruct((samples, 2 * pad), BF16),
        ),
        [pltpu.VMEM(x_shape.shape, F32), images(frames)],
        flops * frames,
        sent, got, v_own, taby, tabz, coil_of, b_rows, m_rows, kd,
    )
    resid_terms = shares(predicted, "cuts", skip=1)

    fold = max(1, LANES // (2 * rank))
    own_slab = jax.ShapeDtypeStruct((tall // 2, 2 * frames, width), BF16)
    pieces, g, theirs = call(
        functools.partial(gradient_kernel, half, frames, tall, slab, scale, len(resid_terms)),
        (
            jax.ShapeDtypeStruct((n_cuts, n_frame, half // fold, 2 * rank * fold), BF16),
            own_slab,
            own_slab,
        ),
        [pltpu.VMEM(x_shape.shape, F32), images(frames)],
        flops * frames,
        *resid_terms, b_rows, m_rows, w, fz, coil_of,
    )
    (grad,) = call(
        basis_kernel,
        (jax.ShapeDtypeStruct((2 * rank * slab * halves, LANES), F32),),
        [pltpu.VMEM(((2 * rank + 1) * (slab * halves + PITCH), LANES), F32)],
        2 * 2 * rank * 4 * frames * slab * width * 8,
        sent, got, v_own, g, swap(theirs, "cuts", 1),
    )
    return grad, pieces


def pairs(terms):
    while len(terms) > 1:
        odd = [terms[-1]] if len(terms) % 2 else []
        terms = [a + b for a, b in zip(terms[::2], terms[1::2])] + odd
    return terms[0]


def body(basis, coil_maps, factors, lines, kdata):
    n_cuts, n_frame = lax.axis_size("cuts"), lax.axis_size("frame")
    readout = basis.shape[3]
    rank = basis.shape[1]
    own = factors.shape[2]
    scale = 1.0 / math.sqrt(coil_maps.shape[1] * lines.shape[1] * n_cuts * readout * n_frame)
    grads, fg = [], 0.0
    for x in range(readout):
        grad, term = one_position(
            basis[:, :, :, x], coil_maps[:, :, :, x], factors, lines, kdata[..., x], scale
        )
        grads.append(grad)
        fg = fg + term
    pieces = fg.reshape((n_cuts * n_frame,) + fg.shape[2:])
    arriving = lax.all_to_all(pieces, ("cuts", "frame"), 0, 0, tiled=True)
    arriving, grads = lax.optimization_barrier((arriving, grads))
    grads = [grad.reshape(2, rank, basis.shape[2], -1) for grad in grads]
    basis_grad = grads[0][:, :, :, None] if readout == 1 else jnp.stack(grads, axis=3)
    parts = arriving.astype(F32).reshape((n_cuts // 2, 2, n_frame) + fg.shape[2:])
    summed = jnp.sum(parts, axis=(0, 2))
    folded = summed.reshape(2, summed.shape[1], -1, 2, rank)
    return basis_grad, folded.transpose(3, 4, 0, 2, 1).reshape(2, rank, own)


def solution(mesh):
    placed = (
        P(None, None, "cuts", "frame", None),
        P(None, None, "cuts", "frame", None),
        P(None, None, "frame"),
        P(None, "cuts"),
        P(None, None, "cuts", None, "frame"),
    )
    return jax.shard_map(
        body,
        mesh=mesh,
        in_specs=placed,
        out_specs=(P(None, None, "cuts", "frame", None), P(None, None, "frame")),
        check_vma=False,
    )
```

```python
import functools
import math

import jax
import jax.numpy as jnp
import numpy as np
from jax import lax
from jax.experimental import pallas as pl
from jax.experimental.pallas import tpu as pltpu
from jax.sharding import PartitionSpec as P

F32 = jnp.float32
BF16 = jnp.bfloat16
LANES = 128
TILE = 16
PITCH = 8


def trig(product, size):
    angle = (product % size).astype(F32) * (2.0 * math.pi / size)
    return jnp.cos(angle), jnp.sin(angle)


def write_dft(out_ref, size, index):
    lanes = index.shape[1]
    fine = lax.broadcasted_iota(jnp.int32, (TILE, lanes), 0)
    b_cos, b_sin = trig(fine * index[:TILE], size)
    coarse = lax.broadcasted_iota(jnp.int32, (size // TILE, lanes), 0) * TILE
    a_cos, a_sin = trig(coarse * index[: size // TILE], size)
    factor = 1.0 / math.sqrt(size)
    a_cos, a_sin = a_cos * factor, a_sin * factor
    for a in range(size // TILE):
        rows = slice(a * TILE, (a + 1) * TILE)
        p_cos, p_sin = a_cos[a : a + 1], a_sin[a : a + 1]
        out_ref[rows, :lanes] = (p_cos * b_cos - p_sin * b_sin).astype(BF16)
        out_ref[rows, lanes:] = (p_sin * b_cos + p_cos * b_sin).astype(BF16)


def nn(a, b):
    return lax.dot_general(a, b, (((1,), (0,)), ((), ())), preferred_element_type=F32)


def nt(a, b):
    return lax.dot_general(a, b, (((1,), (1,)), ((), ())), preferred_element_type=F32)


def tn(a, b):
    return lax.dot_general(a, b, (((0,), (0,)), ((), ())), preferred_element_type=F32)


def total(refs):
    terms = [ref[...].astype(F32) for ref in refs]
    while len(terms) > 1:
        odd = [terms[-1]] if len(terms) % 2 else []
        terms = [a + b for a, b in zip(terms[::2], terms[1::2])] + odd
    return terms[0]


def arrived(sent_ref, got_ref):
    sent, got = sent_ref[...].astype(F32), got_ref[...].astype(F32)
    even = in_pair()[1] == 0
    return jnp.where(even, sent, got), jnp.where(even, got, sent)


def factor_matrix(v_re, v_im):
    top = jnp.concatenate([v_re, -v_im], axis=1)
    bottom = jnp.concatenate([v_im, v_re], axis=1)
    return jnp.concatenate([top, bottom], axis=0).astype(BF16)


def half_factors(v_ref, others, place):
    _, own, rank = v_ref.shape
    half = own // 2
    v = v_ref[...].astype(F32)
    blocks = [(v[0], v[1])]
    for a in range(0, rank * (lax.axis_size("frame") - 1), rank):
        blocks.append((others[:own, a : a + rank], others[own : 2 * own, a : a + rank]))
    return [
        jnp.concatenate(
            [jnp.where(place == 0, b[p][:half], b[p][half:]) for b in blocks], axis=0
        )
        for p in range(2)
    ]


def adjoint_pair(w):
    half = w.shape[1] // 2
    return jnp.concatenate([w, jnp.concatenate([-w[:, half:], w[:, :half]], axis=1)], axis=0)


def tree(value):
    terms = [value[i] for i in range(value.shape[0])]
    while len(terms) > 1:
        odd = [terms[-1]] if len(terms) % 2 else []
        terms = [a + b for a, b in zip(terms[::2], terms[1::2])] + odd
    return terms[0].astype(F32)


def in_pair():
    return lax.axis_index("cuts") // 2, lax.axis_index("cuts") % 2


def frame_of(step, own):
    return ((step // own) ^ lax.axis_index("frame")) * own + step % own


def tables_kernel(real, coils, after_ref, taby_ref, tabz_ref, coil_ref):
    del after_ref
    width, depth, pad = taby_ref.shape[0], tabz_ref.shape[0], coil_ref.shape[2]
    write_dft(taby_ref, width, lax.broadcasted_iota(jnp.int32, (max(TILE, width // TILE), width), 1))
    slice_of = lax.broadcasted_iota(jnp.int32, (max(TILE, depth // TILE), pad), 1) % real
    write_dft(tabz_ref, depth, slice_of + in_pair()[0] * real)
    column = lax.broadcasted_iota(jnp.int32, coil_ref.shape[1:], 1) // real
    row = lax.broadcasted_iota(jnp.int32, coil_ref.shape[1:], 0)
    for part in range(2):
        place = (row == column + part * coils) & (column < coils)
        coil_ref[part] = place.astype(F32).astype(BF16)


def turn_kernel(after_ref, b_ref, b_got_ref, m_ref, m_got_ref, b_out, m_out, turn_ref):
    del after_ref
    images, slab, width = b_ref.shape
    pitch = -(-slab // 8) * 8 + PITCH
    first = in_pair()[1] == 0
    for n, ref in enumerate((b_ref, b_got_ref)):
        start = jnp.where(first, n, 1 - n) * slab
        for h in range(width // LANES):
            lanes = slice(h * LANES, (h + 1) * LANES)
            for k in range(images):
                turn_ref[h, k * pitch : k * pitch + slab, :] = ref[k, :, lanes].astype(F32)
            for z in range(slab):
                rows = turn_ref[h, pl.ds(z, images, stride=pitch), :].astype(BF16)
                for k in range(0, b_out.shape[0], 2 * slab):
                    b_out[pl.ds(start + z + k, 1), :, lanes] = rows[None]
    mine, got = m_ref[...].astype(F32), m_got_ref[...].astype(F32)
    both = [jnp.where(first, mine, got), jnp.where(first, got, mine)]
    m_out[...] = jnp.concatenate(both, axis=2).astype(BF16)


def write_tables(pos, taby_ref, tabz_ref, w_ref, fz_ref):
    per, own = pos.shape[0] // 2, pos.shape[1] // lax.axis_size("frame")
    half = own // 2
    first_half = in_pair()[1] == 0
    frames = pos.shape[1] // 2

    def column(row, u):
        t = u // half * own + u % half
        rows = slice(row, row + per)
        return jnp.where(first_half, pos[rows, t : t + 1], pos[rows, t + half : t + half + 1])

    at_y = lax.broadcasted_iota(jnp.int32, (per, taby_ref.shape[0]), 1).astype(F32)
    at_z = lax.broadcasted_iota(jnp.int32, (per, tabz_ref.shape[0]), 1).astype(F32)
    group = max(1, 128 // per)
    for g in range(0, frames, group):
        hot_y, hot_z = (
            jnp.concatenate(
                [
                    jnp.where(iota == column(first, t), 1.0, 0.0)
                    for t in range(g, g + group)
                ],
                axis=0,
            ).astype(BF16)
            for iota, first in ((at_y, 0), (at_z, per))
        )
        rows = slice(g * per, (g + group) * per)
        w_ref[rows, :] = nn(hot_y, taby_ref[...]).astype(BF16)
        fz_ref[rows, :] = nn(hot_z, tabz_ref[...]).astype(BF16)


def predict_kernel(own, frames, slab, *refs):
    sent_ref, got_ref, v_ref, taby_ref, tabz_ref, coil_ref, b_ref, m_ref, kd_ref = refs[:9]
    pred_ref, w_ref, fz_ref, x_ref, i_ref = refs[9:]
    steps = frames
    width = b_ref.shape[2]
    rows = m_ref.shape[1]
    pad = fz_ref.shape[1] // 2
    per = w_ref.shape[0] // frames
    coils = rows // slab
    halves = width // LANES
    pitch = 2 * steps + PITCH
    stride = frames + PITCH

    pos, others = arrived(sent_ref, got_ref)
    write_tables(pos[: 2 * per, : 2 * frames], taby_ref, tabz_ref, w_ref, fz_ref)
    v = factor_matrix(*half_factors(v_ref, others, in_pair()[1]))
    for z in range(slab):
        image = nn(v, b_ref[z])
        for h in range(halves):
            i_ref[h, z * pitch : z * pitch + 2 * steps, :] = image[:, h * LANES : (h + 1) * LANES]

    m_re = m_ref[0].reshape(coils, slab, width)
    m_im = m_ref[1].reshape(coils, slab, width)

    def frame(step, carry):
        t = frame_of(step, own)
        i_re, i_im = (
            jnp.concatenate(
                [i_ref[h, pl.ds(at, slab, stride=pitch), :] for h in range(halves)], axis=1
            ).astype(BF16)[None]
            for at in (step, steps + step)
        )
        p_re = (m_re * i_re - m_im * i_im).reshape(rows, width)
        p_im = (m_re * i_im + m_im * i_re).reshape(rows, width)
        at = pl.ds(pl.multiple_of(t * per, TILE), per)
        lhs = adjoint_pair(w_ref[at, :])
        y = jnp.concatenate([(nt(p_re[k:k+128], lhs[:, :width]) + nt(p_im[k:k+128], lhs[:, width:])).T for k in range(0,rows,128)],axis=1)
        y_re, y_im = y[:per], y[per:]
        f = fz_ref[at, :].astype(F32)
        f_cos, f_sin = f[:, :rows], f[:, pad : pad + rows]
        x = jnp.concatenate([y_re * f_cos + y_im * f_sin, y_im * f_cos - y_re * f_sin], axis=0)
        for h in range(x_ref.shape[0]):
            lanes = min(LANES, rows - h * LANES)
            x_ref[h, pl.ds(t, 2 * per, stride=stride), :lanes] = x[:, h * LANES : h * LANES + lanes]
        return carry

    lax.fori_loop(0, steps, frame, 0, unroll=math.gcd(steps, 16))
    blocks = max(1, min(per, 512 // frames))

    def summed(part, first):
        at = [(part * per + first + k) * stride for k in range(blocks)]
        halves_of = [
            jnp.concatenate([x_ref[h, a : a + frames, :] for a in at], axis=0)
            for h in range(x_ref.shape[0])
        ]
        x = jnp.concatenate(halves_of, axis=1)[:, :rows].astype(BF16)
        return nt(coil_ref[part, :, :rows], x)

    for first in range(0, per, blocks):
        pred_ref[:, first * frames : (first + blocks) * frames] = (
            summed(0, first) + summed(1, first)
        ).astype(BF16)
    size = kd_ref.shape[1]
    at = pl.ds(pl.multiple_of(in_pair()[0] * size, LANES), size)
    pred_ref[:, at] = (pred_ref[:, at].astype(F32) - kd_ref[...].astype(F32)).astype(BF16)


def gradient_kernel(own, frames, slab, real, scale, n_r, *refs):
    r_refs, refs = refs[:n_r], refs[n_r:]
    b_ref, m_ref, w_ref, fz_ref, coil_ref, fg_ref, mine_ref, theirs_ref, r_ref, g_ref = refs
    steps = frames
    width = b_ref.shape[2]
    rank = b_ref.shape[1] // 2
    rows = m_ref.shape[1]
    pad = fz_ref.shape[1] // 2
    per = w_ref.shape[0] // frames
    coils = rows // slab
    halves = width // LANES
    pitch = 2 * steps + PITCH
    stride = frames + PITCH

    resid = total(r_refs).astype(BF16)
    blocks = max(1, min(per, 512 // frames))
    for part in range(2):
        for first in range(0, per, blocks):
            r = tn(resid[:, first * frames : (first + blocks) * frames], coil_ref[part])
            for k in range(blocks):
                at = (part * per + first + k) * stride
                for h in range(r_ref.shape[0]):
                    r_ref[h, at : at + frames, :] = r[
                        k * frames : (k + 1) * frames, h * LANES : (h + 1) * LANES
                    ]

    m_re = m_ref[0].reshape(coils, slab, width)
    m_im = m_ref[1].reshape(coils, slab, width)

    def frame(step, carry):
        t = frame_of(step, own)
        at = pl.ds(pl.multiple_of(t * per, TILE), per)
        rhs = adjoint_pair(w_ref[at, :])
        f = fz_ref[at, :].astype(F32)
        f_cos, f_sin = f[:, :pad], f[:, pad:]
        r = jnp.concatenate(
            [r_ref[h, pl.ds(t, 2 * per, stride=stride), :] for h in range(r_ref.shape[0])], axis=1
        )
        r_re, r_im = r[:per], r[per:]
        q = jnp.concatenate([r_re * f_cos - r_im * f_sin, r_im * f_cos + r_re * f_sin], axis=0)
        u = tn(q[:, :rows].astype(BF16), rhs).astype(BF16)
        u_re = u[:, :width].reshape(coils, slab, width)
        u_im = u[:, width:].reshape(coils, slab, width)
        g_re = tree(m_re * u_re + m_im * u_im)
        g_im = tree(m_re * u_im - m_im * u_re)
        for h in range(halves):
            lanes = slice(h * LANES, (h + 1) * LANES)
            g_ref[h, pl.ds(step, slab, stride=pitch), :] = g_re[:, lanes]
            g_ref[h, pl.ds(steps + step, slab, stride=pitch), :] = g_im[:, lanes]
        return carry

    lax.fori_loop(0, steps, frame, 0, unroll=math.gcd(steps, 16))
    acc = jnp.zeros((2 * steps, 2 * rank), F32)
    for ref, place in ((mine_ref, in_pair()[1]), (theirs_ref, 1 - in_pair()[1])):
        for n in range(ref.shape[0]):
            z = n // real * 2 * real + place * real + n % real
            at = pl.ds(pl.multiple_of(z * pitch, 8), 2 * steps)
            g = jnp.concatenate([g_ref[h, at, :] for h in range(halves)], axis=1).astype(BF16)
            ref[n] = g
            acc = acc + nt(g, b_ref[pl.ds(z, 1)][0])
    top, bottom = acc[:steps], acc[steps:]
    fg = jnp.concatenate(
        [top[:, :rank] + bottom[:, rank:], bottom[:, :rank] - top[:, rank:]], axis=1
    )
    fg = (fg * scale).astype(fg_ref.dtype)
    n_cuts, n_frame, n_rows, n_lanes = fg_ref.shape
    for d in range(n_frame):
        piece = jnp.concatenate(
            [
                fg[d * own + k : d * own + k + n_rows].astype(F32)
                for k in range(0, own, n_rows)
            ],
            axis=1,
        ).astype(fg_ref.dtype)
        target = lax.axis_index("frame") ^ d
        for c in range(n_cuts):
            fg_ref[c, pl.ds(target, 1)] = piece[None]


def basis_kernel(sent_ref, got_ref, v_ref, g_ref, g_got_ref, grad_ref, rows_ref):
    _, others = arrived(sent_ref, got_ref)
    place = in_pair()[1]
    pairs_of = [
        (factor_matrix(*half_factors(v_ref, others, place)), g_ref),
        (factor_matrix(*half_factors(v_ref, others, 1 - place)), g_got_ref),
    ]
    halves = g_ref.shape[2] // LANES
    images = 2 * v_ref.shape[2]
    slab = grad_ref.shape[0] // (images * halves)
    pitch = slab * halves + PITCH
    for z in range(slab):
        grad = functools.reduce(
            jnp.add,
            [tn(v, ref[k]) for v, ref in pairs_of for k in range(z, g_ref.shape[0], slab)],
        )
        for h in range(halves):
            rows_ref[pl.ds(z * halves + h, images, stride=pitch), :] = grad[
                :, h * LANES : (h + 1) * LANES
            ]
    for n in range(images):
        grad_ref[n * slab * halves : (n + 1) * slab * halves, :] = rows_ref[
            n * pitch : n * pitch + slab * halves, :
        ]


def stages(size):
    steps, stride = [(1, 2)], 2
    if (size // stride).bit_length() % 2 == 0:
        steps.append((stride, 2))
        stride *= 2
    while stride < size:
        steps.append((stride, 4))
        stride *= 4
    return steps


def swap(value, axis, distance):
    size = lax.axis_size(axis)
    return lax.ppermute(value, axis, [(i, i ^ distance) for i in range(size)])


def shares(value, axis, last=1, skip=0):
    steps = stages(lax.axis_size(axis))[skip:]
    for number, (stride, radix) in enumerate(steps):
        if number + last == len(steps) + 1:
            return value
        terms = [value] + [swap(value, axis, stride * d) for d in range(radix - 1, 0, -1)][::-1]
        if number + 1 < len(steps):
            value = pairs([term.astype(F32) for term in terms]).astype(value.dtype)
    return terms


def grown(value, rows, lanes):
    return jnp.pad(value, ((0, rows - value.shape[0]), (0, lanes - value.shape[1])))


def collect(positions, v_own, meanwhile):
    n_cuts, n_frame = lax.axis_size("cuts"), lax.axis_size("frame")
    even = lax.axis_index("cuts") % 2 == 0
    stride, radix = stages(n_cuts)[-1]
    near = shares(positions, "cuts", last=2)
    rank = v_own.shape[2]
    rows = max(near.shape[0], math.prod(v_own.shape[:2]))
    lanes = max(near.shape[1], rank)
    v_packet = grown(v_own.reshape(-1, rank).astype(near.dtype), rows, lanes)
    near, v_packet = lax.optimization_barrier((near, v_packet))
    packet = jnp.where(even, grown(near, rows, lanes), v_packet)
    got = []
    for d in range(1, max(radix, n_frame)):
        route = []
        for c in range(n_cuts):
            for f in range(n_frame):
                if c % 2 == 0 and d < radix:
                    route.append((c * n_frame + f, (c ^ stride * d) * n_frame + f))
                if c % 2 == 1 and d < n_frame:
                    route.append((c * n_frame + f, c * n_frame + (f ^ d)))
        got.append(lax.ppermute(packet, ("cuts", "frame"), route))
    staged = meanwhile(packet)
    got, staged = lax.optimization_barrier((got, staged))
    joined = pairs([x.astype(F32) for x in (packet, *got[: radix - 1])]).astype(near.dtype)
    others = jnp.concatenate([x[:, :rank] for x in got[: n_frame - 1]], axis=1)
    lanes = max(lanes, others.shape[1])
    sent = jnp.where(even, grown(joined, rows, lanes), grown(others, rows, lanes))
    return sent, swap(sent, "cuts", 1), staged


def call(kernel, outs, scratch, flops, *operands, limit=0):
    def size(x):
        rows = [-(-x.shape[-2] // TILE) * TILE, -(-x.shape[-1] // LANES) * LANES]
        return math.prod(x.shape[:-2]) * math.prod(rows) * jnp.dtype(x.dtype).itemsize

    nbytes = sum(size(x) for x in operands)
    held = nbytes + sum(size(x) for x in (*outs, *scratch))
    limit = limit or min(56, 10 + held * 5 // (4 * 1024 * 1024))
    return pl.pallas_call(
        kernel,
        out_shape=outs,
        scratch_shapes=scratch,
        compiler_params=pltpu.CompilerParams(vmem_limit_bytes=limit * 1024 * 1024),
        cost_estimate=pl.CostEstimate(flops=flops, bytes_accessed=nbytes, transcendentals=0),
    )(*operands)


def one_position(basis, coil_maps, factors, lines, kdata, scale):
    n_cuts, n_frame = lax.axis_size("cuts"), lax.axis_size("frame")
    cut = lax.axis_index("cuts")
    rank, slab, width = basis.shape[1:]
    coils = coil_maps.shape[1]
    columns = lines.shape[1]
    half = factors.shape[2] // 2
    frames = lines.shape[0] // 2
    per = columns * n_cuts
    samples = frames * per
    depth = slab * n_cuts
    ky_rows = width // n_cuts

    spread = max(1, TILE // (2 * slab))
    tall = spread * 2 * slab
    coil_groups = -(-coils // spread)
    rows = coil_groups * tall
    pad = -(-rows // LANES) * LANES
    coil_rows = -(-2 * coils // 8) * 8

    kind = BF16 if max(width, depth) <= 256 else F32
    turned = lines.T
    mine = jnp.stack([cut * ky_rows + turned // depth, turned % depth])
    owner = lax.broadcasted_iota(jnp.int32, (2 * per, 2 * frames), 0) // columns % n_cuts == cut
    every = jnp.broadcast_to(mine[:, None], (2, n_cuts, columns, 2 * frames))
    placed = jnp.where(owner, every.reshape(2 * per, 2 * frames), 0).astype(kind)
    v_own = factors.transpose(0, 2, 1)
    maps = jnp.pad(coil_maps, ((0, 0), (0, coil_groups * spread - coils), (0, 0), (0, 0)))
    images_in = basis.reshape(2 * rank, slab, width)

    flops = 2 * 2 * per * rows * 2 * width * 8
    halves = width // LANES
    x_shape = jax.ShapeDtypeStruct((pad // LANES, (2 * per + 1) * (frames + PITCH), LANES), F32)

    def images(steps):
        return pltpu.VMEM((halves, (tall + 1) * (2 * steps + PITCH), LANES), F32)

    _, b, m, k = lax.optimization_barrier((placed, images_in, maps, kdata))
    b_got, m_got, k_got = (swap(x, "cuts", 1) for x in (b, m, k))

    def stage(packet):
        tables = call(
            functools.partial(tables_kernel, 2 * slab, coils),
            (
                jax.ShapeDtypeStruct((width, 2 * width), BF16),
                jax.ShapeDtypeStruct((depth, 2 * pad), BF16),
                jax.ShapeDtypeStruct((2, coil_rows, pad), BF16),
            ),
            [],
            1024 * 1024 * 1024,
            b_got,
        )
        turned = call(
            turn_kernel,
            (
                jax.ShapeDtypeStruct((tall, 2 * rank, width), BF16),
                jax.ShapeDtypeStruct((2, maps.shape[1], 2 * slab, width), BF16),
            ),
            [pltpu.VMEM((halves, (2 * rank + 1) * (-(-slab // 8) * 8 + PITCH), LANES), F32)],
            1024 * 1024 * 1024,
            packet, images_in, b_got, maps, m_got,
        )
        return tables, turned

    sent, got, ((taby, tabz, coil_of), (b_rows, m_rows)) = collect(placed, v_own, stage)
    m_rows = m_rows.reshape(2, rows, width)
    even = lax.axis_index("cuts") % 2 == 0
    _, mine, k_got = lax.optimization_barrier((sent, kdata, k_got))
    both = jnp.stack([jnp.where(even, mine, k_got), jnp.where(even, k_got, mine)])
    both = both.transpose(1, 4, 0, 3, 2).reshape(2 * coils, 2 * columns, n_frame, 2, half)
    kd = jnp.where(even, both[..., 0, :], both[..., 1, :]).reshape(2 * coils, -1)
    kd = jnp.pad(kd, ((0, coil_rows - 2 * coils), (0, 0)))
    predicted, w, fz = call(
        functools.partial(predict_kernel, half, frames, tall),
        (
            jax.ShapeDtypeStruct((coil_rows, samples), BF16),
            jax.ShapeDtypeStruct((samples, 2 * width), BF16),
            jax.ShapeDtypeStruct((samples, 2 * pad), BF16),
        ),
        [pltpu.VMEM(x_shape.shape, F32), images(frames)],
        flops * frames,
        sent, got, v_own, taby, tabz, coil_of, b_rows, m_rows, kd,
    )
    resid_terms = shares(predicted, "cuts", skip=1)

    fold = max(1, LANES // (2 * rank))
    own_slab = jax.ShapeDtypeStruct((tall // 2, 2 * frames, width), BF16)
    pieces, g, theirs = call(
        functools.partial(gradient_kernel, half, frames, tall, slab, scale, len(resid_terms)),
        (
            jax.ShapeDtypeStruct((n_cuts, n_frame, half // fold, 2 * rank * fold), BF16),
            own_slab,
            own_slab,
        ),
        [pltpu.VMEM(x_shape.shape, F32), images(frames)],
        flops * frames,
        *resid_terms, b_rows, m_rows, w, fz, coil_of,
    )
    (grad,) = call(
        basis_kernel,
        (jax.ShapeDtypeStruct((2 * rank * slab * halves, LANES), F32),),
        [pltpu.VMEM(((2 * rank + 1) * (slab * halves + PITCH), LANES), F32)],
        2 * 2 * rank * 4 * frames * slab * width * 8,
        sent, got, v_own, g, swap(theirs, "cuts", 1),
    )
    return grad, pieces


def pairs(terms):
    while len(terms) > 1:
        odd = [terms[-1]] if len(terms) % 2 else []
        terms = [a + b for a, b in zip(terms[::2], terms[1::2])] + odd
    return terms[0]


def body(basis, coil_maps, factors, lines, kdata):
    n_cuts, n_frame = lax.axis_size("cuts"), lax.axis_size("frame")
    readout = basis.shape[3]
    rank = basis.shape[1]
    own = factors.shape[2]
    scale = 1.0 / math.sqrt(coil_maps.shape[1] * lines.shape[1] * n_cuts * readout * n_frame)
    grads, fg = [], 0.0
    for x in range(readout):
        grad, term = one_position(
            basis[:, :, :, x], coil_maps[:, :, :, x], factors, lines, kdata[..., x], scale
        )
        grads.append(grad)
        fg = fg + term
    pieces = fg.reshape((n_cuts * n_frame,) + fg.shape[2:])
    arriving = lax.all_to_all(pieces, ("cuts", "frame"), 0, 0, tiled=True)
    arriving, grads = lax.optimization_barrier((arriving, grads))
    grads = [grad.reshape(2, rank, basis.shape[2], -1) for grad in grads]
    basis_grad = grads[0][:, :, :, None] if readout == 1 else jnp.stack(grads, axis=3)
    parts = arriving.astype(F32).reshape((n_cuts // 2, 2, n_frame) + fg.shape[2:])
    summed = jnp.sum(parts, axis=(0, 2))
    folded = summed.reshape(2, summed.shape[1], -1, 2, rank)
    return basis_grad, folded.transpose(3, 4, 0, 2, 1).reshape(2, rank, own)


def solution(mesh):
    placed = (
        P(None, None, "cuts", "frame", None),
        P(None, None, "cuts", "frame", None),
        P(None, None, "frame"),
        P(None, "cuts"),
        P(None, None, "cuts", None, "frame"),
    )
    return jax.shard_map(
        body,
        mesh=mesh,
        in_specs=placed,
        out_specs=(P(None, None, "cuts", "frame", None), P(None, None, "frame")),
        check_vma=False,
    )
```
